32 devices in a mesh: nodes: 8 (over z, x), cams: 4 (over y, core).
Axes of the slice: x: 2, y: 2, z: 4, core: 2. Of those that a mesh axis runs over, the one named last changes fastest.
Arguments:
- iterate: float32 [64, 12, 128], P(('nodes', 'cams')), may hold values from -6 to 6
- residual: float32 [64, 12, 128], P(('nodes', 'cams')), may hold values from -6 to 6
- direction: float32 [64, 12, 128], P(('nodes', 'cams')), may hold values from -5 to 5
- precond: float32 [64, 12, 128], P(('nodes', 'cams')), may hold values from 0.2 to 6, as said below
- send_list: int32 [8, 8, 3], P('nodes'), may hold values from -1 to 7, as said below
- grads: bfloat16 [12, 65536], P(None, ('nodes', 'cams')), may hold values from -2.390625 to 2.390625
- node_refs: int32 [4, 65536], P(None, ('nodes', 'cams')), may hold values from 0 to 3071, as said below
- skin: bfloat16 [4, 65536], P(None, ('nodes', 'cams')), may hold values from 0.099609375 to 1
- rigid_nbr: int32 [64, 6, 128], P(('nodes', 'cams')), may hold values from 0 to 127, as said below
Outputs:
- new_iterate: float32 [64, 12, 128], P(('nodes', 'cams'))
- new_residual: float32 [64, 12, 128], P(('nodes', 'cams'))
- new_direction: float32 [64, 12, 128], P(('nodes', 'cams'))
The draws below stay inside these ranges and needn't reach their ends.
Inputs may be any that keep to these rules, and one draw needn't show every extreme that they name: `precond`: Positive. `send_list`: for each owner and receiver the live entries come first and the rest are -1; at most 3 live entries, and every receiver n has all 3 slots live from owner (n - 1) mod 8. `node_refs`: every reference names a live slot of its device's receiver; the 4 references of a pixel lie in the same slot. `rigid_nbr`: never the node itself.
All inputs are finite; a program needn't handle non-finite values.
Results may differ from the reference program's by a relative error of at most 0.00085.
Values sent between devices are 32-bit elements; how exact they have to be, the bound alone decides.
No kernel may reach another device: no remote copies, remote signals or barrier semaphores. Data moves between devices by JAX's collectives and lax.ppermute only.
A program may use at most 64 MiB of HBM per device.

```python
import jax
import jax.numpy as jnp
from jax import lax

PARAMS = 12
NPATCH = 128
SKIN = 4
RIG = 6
FRAMES = 8
SLOTS = 3
PIX = 2048
PD = 8
PATCHES = 64
PIXELS = 65536
N_NODES = 8
N_CAMS = 4


def live_counts(key):
    base = jax.random.fold_in(key, 7)
    first, second = jax.random.split(base)
    hotness = jax.random.randint(first, (N_NODES,), 0, 4)
    sparse = jax.random.randint(second, (N_NODES, N_NODES), 0, SLOTS // 2 + 1)
    counts = jnp.where(hotness[None, :] == 0, SLOTS, sparse)
    indices = jnp.arange(N_NODES, dtype=jnp.int32)
    forced = indices[None, :] == (indices[:, None] + 1) % N_NODES
    return jnp.where(forced, SLOTS, counts).astype(jnp.int32)


def draw_send_list(key, part):
    counts = live_counts(key)
    chosen = jax.random.randint(jax.random.fold_in(key, 11), (N_NODES, N_NODES, SLOTS), 0, PD)
    positions = jnp.arange(SLOTS, dtype=jnp.int32)
    return jnp.where(positions[None, None, :] < counts[:, :, None], chosen, -1).astype(jnp.int32)


def search_row(running, wanted):
    return jnp.searchsorted(running, wanted, side='right')


def draw_node_refs(key, part):
    counts = live_counts(key)
    positions = jnp.arange(SLOTS, dtype=jnp.int32)
    live = (positions[None, None, :] < counts[:, :, None]).astype(jnp.int32)
    per_receiver = jnp.transpose(live, (1, 0, 2)).reshape(N_NODES, N_NODES * SLOTS)
    running = jnp.cumsum(per_receiver, axis=1)
    totals = running[:, -1]
    devices = N_NODES * N_CAMS
    receiver = jnp.arange(devices, dtype=jnp.int32) // N_CAMS
    streams = jax.random.split(jax.random.fold_in(key, 13), 3)
    wanted = jax.random.randint(streams[0], (devices, PIX), 0, totals[receiver][:, None])
    slot_ids = jax.vmap(search_row)(running[receiver], wanted).astype(jnp.int32)
    base_node = jax.random.randint(streams[1], (1, devices, PIX), 0, NPATCH)
    offsets = jax.random.randint(streams[2], (SKIN, devices, PIX), 0, NPATCH)
    offsets = offsets.at[0].set(0)
    within = (base_node + offsets) % NPATCH
    node_ids = slot_ids[None] * NPATCH + within
    return node_ids.reshape(SKIN, devices * PIX).astype(jnp.int32)


def draw_rigid_nbr(key, part):
    stride = jax.random.randint(jax.random.fold_in(key, 17), (PATCHES, RIG, NPATCH), 1, NPATCH)
    return ((jnp.arange(NPATCH, dtype=jnp.int32)[None, None, :] + stride) % NPATCH).astype(jnp.int32)


def draw_direction(key, part):
    position = jnp.arange(PATCHES, dtype=jnp.float32)[:, None, None] / PATCHES
    ramp = 0.7 * (1.0 + 0.8 * position)
    values = jax.random.normal(jax.random.fold_in(key, 19), (PATCHES, PARAMS, NPATCH), jnp.float32)
    return jnp.clip(values * ramp, -5.0, 5.0)


def draw_precond(key, part):
    position = jnp.arange(PATCHES, dtype=jnp.float32)[:, None, None] / PATCHES
    ramp = 1.0 + 2.0 * position
    spread = jax.random.uniform(jax.random.fold_in(key, 29), (PATCHES, PARAMS, NPATCH), jnp.float32, jnp.log(0.2), jnp.log(2.0))
    values = jnp.exp(spread)
    return jnp.clip(values * ramp, 0.2, 6.0)


def block_levels(stream_key, shape, cuts, low, largest):
    loudness = 1.0
    for dim, shards_of in cuts:
        draws = jax.random.uniform(jax.random.fold_in(jax.random.fold_in(stream_key, 6), dim), (shards_of,), jnp.float32, low / len(cuts), largest / len(cuts))
        loudness = loudness * jnp.repeat(jnp.exp(draws), shape[dim] // shards_of).reshape((-1,) + (1,) * (len(shape) - 1 - dim))
    return loudness


def bell_draw(stream_key, dims, scale, limit, shards=(), held_as=jnp.bfloat16):
    entries = jax.random.normal(stream_key, dims, jnp.float32) * scale
    if len(shards) > 0:
        entries = block_levels(stream_key, dims, shards, -0.22, 0.18) * entries
    return jnp.clip(entries, min=-limit, max=limit).astype(held_as)


def setup_inputs(seed: int = 0) -> dict:
    key_list = jax.random.split(jax.random.key(seed), 10)
    return {
        "iterate": bell_draw(key_list[0], (PATCHES, PARAMS, NPATCH), 1.0, 6.0, ((0, 32),), jnp.float32),
        "residual": bell_draw(key_list[1], (PATCHES, PARAMS, NPATCH), 1.0, 6.0, ((0, 32),), jnp.float32),
        "direction": draw_direction(jax.random.fold_in(key_list[9], 71), 0),
        "precond": draw_precond(jax.random.fold_in(key_list[9], 71), 0),
        "send_list": draw_send_list(jax.random.fold_in(key_list[9], 71), 0),
        "grads": bell_draw(key_list[5], (PARAMS, PIXELS), 0.4, 2.390625, ((1, 32),)),
        "node_refs": draw_node_refs(jax.random.fold_in(key_list[9], 71), 0),
        "skin": jnp.clip(0.099609375 + 0.9003906 * jax.random.uniform(key_list[7], (SKIN, PIXELS), jnp.float32) ** block_levels(key_list[7], (SKIN, PIXELS), ((1, 32),), -0.2, 0.2), 0.099609375, 1.0).astype(jnp.bfloat16),
        "rigid_nbr": draw_rigid_nbr(jax.random.fold_in(key_list[9], 71), 0),
    }


temporal_weight = 0.5
rigid_weight = 0.1


def rigidity_one(patch, neighbours):
    difference = patch[:, None, :] - patch[:, neighbours]
    summed = jnp.sum(difference, axis=1)
    summed = summed.at[:, neighbours].add(-difference)
    return rigid_weight * summed


def temporal(direction):
    frame_step = PATCHES // FRAMES
    padding = jnp.zeros((frame_step,) + direction.shape[1:], jnp.float32)
    earlier = jnp.concatenate([padding, direction[:-frame_step]], 0)
    following = jnp.concatenate([direction[frame_step:], padding], 0)
    return temporal_weight * (2.0 * direction - earlier - following)


def data_term(direction, send_list, grads, node_refs, skin):
    nodewise = jnp.transpose(direction, (0, 2, 1)).reshape(PATCHES * NPATCH, PARAMS)

    def advance(totals, device):
        receiver = device // N_CAMS
        offset = device * PIX
        grad_block = lax.dynamic_slice_in_dim(grads, offset, PIX, 1).astype(jnp.float32).T
        node_ids = lax.dynamic_slice_in_dim(node_refs, offset, PIX, 1)
        weights = lax.dynamic_slice_in_dim(skin, offset, PIX, 1).astype(jnp.float32)
        source = node_ids // (SLOTS * NPATCH)
        slot_ids = (node_ids // NPATCH) % SLOTS
        within = node_ids % NPATCH
        listed = send_list[source, receiver, slot_ids]
        usable = (listed >= 0).astype(jnp.float32)
        row_ids = (source * PD + jnp.maximum(listed, 0)) * NPATCH + within
        values = nodewise[row_ids] * usable[..., None]
        projected = jnp.sum(values * grad_block[None], axis=2)
        response = jnp.sum(weights * projected, axis=0)
        pieces = (weights * usable * response[None])[..., None] * grad_block[None]
        return totals.at[row_ids].add(pieces), None

    totals, _ = lax.scan(advance, jnp.zeros_like(nodewise), jnp.arange(N_NODES * N_CAMS, dtype=jnp.int32))
    return jnp.transpose(totals.reshape(PATCHES, NPATCH, PARAMS), (0, 2, 1))


def reference(iterate, residual, direction, precond, send_list, grads, node_refs, skin, rigid_nbr):
    image_all = data_term(direction, send_list, grads, node_refs, skin)
    image_all = image_all + jax.vmap(rigidity_one)(direction, rigid_nbr) + temporal(direction)
    start_norm = jnp.sum(residual * precond * residual)
    curvature = jnp.sum(direction * image_all)
    step_length = start_norm / curvature
    new_iterate = iterate + step_length * direction
    new_residual = residual - step_length * image_all
    scaled_new = precond * new_residual
    new_norm = jnp.sum(new_residual * scaled_new)
    new_direction = scaled_new + (new_norm / start_norm) * direction
    return new_iterate, new_residual, new_direction
```

```python
import functools

import jax
import jax.numpy as jnp
from jax import lax
from jax.experimental import pallas as pl
from jax.experimental.pallas import tpu as pltpu
from jax.sharding import PartitionSpec as P

FRAMES = 8
AXES = ("nodes", "cams")
temporal_weight = 0.5
rigid_weight = 0.1
NN = (((1,), (0,)), ((), ()))
NT = (((1,), (1,)), ((), ()))
LANES = 128
ROWS = 16

VMEM = pl.BlockSpec(memory_space=pltpu.VMEM)


def halves(value):
    high = value.astype(jnp.bfloat16)
    low = (value - high.astype(jnp.float32)).astype(jnp.bfloat16)
    return high, low


def data_kernel(
    sizes, gathered, grads, node_refs, skin, out, lists, slots_t, masked, grads_pad, products, sem
):
    owners, cams, slot_count, held, params, block_rows, chunk = sizes
    slots = owners * slot_count
    pixels = grads.shape[1]
    receiver = lax.axis_index("nodes")
    list_rows = pl.ds(held * params, lists.shape[1])
    copy = pltpu.make_async_copy(gathered.at[:, list_rows, :], lists, sem)
    copy.start()
    grads_pad[...] = jnp.zeros_like(grads_pad)
    grads_pad[0:params, :] = grads[...].astype(jnp.float32)
    out[...] = jnp.zeros_like(out)
    copy.wait()

    def patch_of(slot):
        entry = receiver * slot_count + slot % slot_count
        return lists[slot // slot_count, entry // LANES, entry % LANES].astype(jnp.int32)

    def fetch(slot, carry):
        listed = jnp.maximum(patch_of(slot), 0)
        start = (listed // held) * block_rows + listed % held
        rows = gathered[slot // slot_count, pl.ds(start, ROWS, stride=held), :]
        slots_t[pl.ds(pl.multiple_of(slot * ROWS, ROWS), ROWS), :] = rows
        return carry

    lax.fori_loop(0, slots, fetch, 0, unroll=slots <= 32)
    table = slots_t[...].T
    high, low = halves(table)
    table = jnp.concatenate([high, low], axis=0)
    node_rows = lax.broadcasted_iota(jnp.int32, (LANES, chunk), 0)

    for at in range(0, pixels, chunk):
        cols = slice(at, at + chunk)
        refs = node_refs[:, cols]
        node = lax.bitwise_and(refs, LANES - 1)
        slot_of = lax.shift_right_logical(refs[0:1], 7)
        weights = skin[:, cols].astype(jnp.float32)
        grad16 = grads_pad[:, cols]
        spread = jnp.where(node_rows == node[0:1], weights[0:1], 0.0)
        for k in range(1, refs.shape[0]):
            spread = spread + jnp.where(node_rows == node[k : k + 1], weights[k : k + 1], 0.0)

        def mask(slot, carry):
            piece = jnp.where(slot_of == slot, grad16, 0.0).astype(jnp.bfloat16)
            masked[pl.ds(pl.multiple_of(slot * ROWS, ROWS), ROWS), :] = piece
            return carry

        lax.fori_loop(0, slots, mask, 0, unroll=slots <= 32)
        live = masked[...]
        pulled = lax.dot_general(table, live, NN, preferred_element_type=jnp.float32)
        pulled = pulled[:LANES] + pulled[LANES:]
        projected = jnp.sum(spread * pulled, axis=0, keepdims=True)
        high, low = halves(spread * projected)
        part = lax.dot_general(
            live, jnp.concatenate([high, low], axis=0), NT, preferred_element_type=jnp.float32
        )
        part = part[:, :LANES] + part[:, LANES:]
        if at == 0:
            products[...] = part
        else:
            products[...] += part

    def give(slot, carry):
        listed = patch_of(slot)

        @pl.when(listed >= 0)
        def _():
            device = (slot // slot_count) * cams + listed // held
            where = pl.ds(device * held * params + listed % held, params, stride=held)
            piece = products[pl.ds(pl.multiple_of(slot * ROWS, ROWS), params), :]
            out[where, :] = out[where, :] + piece

        return carry

    lax.fori_loop(0, slots, give, 0, unroll=slots <= 32)


def local_kernel(held, step, direction, gathered, nbr, out):
    rows = direction.shape[0]
    devices = gathered.shape[0]
    me = lax.axis_index("nodes") * lax.axis_size("cams") + lax.axis_index("cams")
    value = direction[...]
    before = gathered[jnp.maximum(me - step, 0), 0:rows, :]
    after = gathered[jnp.minimum(me + step, devices - 1), 0:rows, :]
    earlier = jnp.where(me >= step, before, 0.0)
    following = jnp.where(me + step < devices, after, 0.0)
    temporal = temporal_weight * (2.0 * value - earlier - following)
    high, low = halves(value)
    ones = jnp.ones((16, LANES), jnp.bfloat16)
    stack = jnp.concatenate([high.astype(jnp.float32), low.astype(jnp.float32), ones.astype(jnp.float32)], axis=0)
    stack = stack.astype(jnp.bfloat16)
    node_rows = lax.broadcasted_iota(jnp.int32, (LANES, LANES), 0)
    patch_row = lax.broadcasted_iota(jnp.int32, (rows, LANES), 0) % held
    edges = nbr.shape[0] // held
    rigid = jnp.zeros_like(value)
    for q in range(held):
        hits = jnp.zeros((LANES, LANES), jnp.float32)
        for r in range(edges):
            row = nbr[r * held + q : r * held + q + 1, :]
            hits = hits + jnp.where(node_rows == row, 1.0, 0.0)
        hits = hits.astype(jnp.bfloat16)
        pulled = lax.dot_general(stack, hits, NN, preferred_element_type=jnp.float32)
        pushed = lax.dot_general(stack, hits, NT, preferred_element_type=jnp.float32)
        degree = pushed[2 * rows : 2 * rows + 1]
        both = pulled + pushed
        part = value * (degree + float(edges)) - (both[:rows] + both[rows : 2 * rows])
        rigid = jnp.where(patch_row == q, part, rigid)
    out[...] = rigid_weight * rigid + temporal


def image_kernel(received, local, direction, residual, precond, image, sums):
    total = jnp.sum(received[...], axis=0) + local[...]
    image[...] = total
    value = residual[...]
    scale = precond[...]
    scaled = scale * value
    rows = [
        jnp.sum(value * scaled, axis=0, keepdims=True),
        jnp.sum(direction[...] * total, axis=0, keepdims=True),
        jnp.sum(total * scaled, axis=0, keepdims=True),
        jnp.sum(total * (scale * total), axis=0, keepdims=True),
    ]
    sums[...] = jnp.concatenate(rows + [jnp.zeros((4, LANES), jnp.float32)], axis=0)


def update_kernel(
    sums, image, iterate, residual, direction, precond, new_iterate, new_residual, new_direction
):
    total = jnp.sum(jnp.sum(sums[...], axis=0), axis=1, keepdims=True)
    start, curvature, cross, square = (total[i : i + 1] for i in range(4))
    step = start / curvature
    norm = start - 2.0 * step * cross + step * step * square
    ratio = norm / start
    value = direction[...]
    left = residual[...] - step * image[...]
    new_iterate[...] = iterate[...] + step * value
    new_residual[...] = left
    new_direction[...] = precond[...] * left + ratio * value


def flat(value):
    return jnp.transpose(value, (1, 0, 2)).reshape(-1, value.shape[2])


def on_device(iterate, residual, direction, precond, send_list, grads, node_refs, skin, rigid_nbr):
    held, params, lanes = direction.shape
    pixels = grads.shape[1]
    owners = lax.axis_size("nodes")
    cams = lax.axis_size("cams")
    devices = owners * cams
    slot_count = send_list.shape[2]
    slots = owners * slot_count
    rows = held * params
    f32 = jnp.float32
    iterate, residual, direction, precond = (flat(v) for v in (iterate, residual, direction, precond))
    nbr = flat(rigid_nbr)

    listed = send_list.reshape(-1).astype(f32)
    list_rows = -(-listed.shape[0] // lanes)
    block_rows = -(-(rows + list_rows) // 8) * 8
    listed = jnp.pad(listed, (0, (block_rows - rows) * lanes - listed.shape[0]))
    block = jnp.concatenate([direction, listed.reshape(-1, lanes)], axis=0)
    gathered = lax.all_gather(block, AXES, axis=0, tiled=False)

    chunk = 512
    sizes = (owners, cams, slot_count, held, params, block_rows, chunk)
    products = pl.pallas_call(
        functools.partial(data_kernel, sizes),
        out_shape=jax.ShapeDtypeStruct((devices * rows, lanes), f32),
        in_specs=[VMEM] * 4,
        out_specs=VMEM,
        scratch_shapes=[
            pltpu.SMEM((owners, list_rows, lanes), f32),
            pltpu.VMEM((slots * ROWS, lanes), f32),
            pltpu.VMEM((slots * ROWS, chunk), jnp.bfloat16),
            pltpu.VMEM((ROWS, pixels), f32),
            pltpu.VMEM((slots * ROWS, lanes), f32),
            pltpu.SemaphoreType.DMA,
        ],
        compiler_params=pltpu.CompilerParams(vmem_limit_bytes=48 * 1024 * 1024),
        name="data_products",
    )(gathered.reshape(owners, cams * block_rows, lanes), grads, node_refs, skin)

    received = lax.all_to_all(
        products.reshape(devices, rows, lanes), AXES, split_axis=0, concat_axis=0, tiled=True
    )
    step = devices // FRAMES
    local = pl.pallas_call(
        functools.partial(local_kernel, held, step),
        out_shape=jax.ShapeDtypeStruct((rows, lanes), f32),
        in_specs=[VMEM] * 3,
        out_specs=VMEM,
        compiler_params=pltpu.CompilerParams(vmem_limit_bytes=48 * 1024 * 1024),
        name="local_terms",
    )(direction, gathered, nbr)
    image, sums = pl.pallas_call(
        image_kernel,
        out_shape=(
            jax.ShapeDtypeStruct((rows, lanes), f32),
            jax.ShapeDtypeStruct((8, lanes), f32),
        ),
        in_specs=[VMEM] * 5,
        out_specs=(VMEM, VMEM),
        compiler_params=pltpu.CompilerParams(vmem_limit_bytes=48 * 1024 * 1024),
        name="image_sums",
    )(received, local, direction, residual, precond)
    sums = lax.all_gather(sums, AXES, axis=0, tiled=False)
    outs = pl.pallas_call(
        update_kernel,
        out_shape=(jax.ShapeDtypeStruct((rows, lanes), f32),) * 3,
        in_specs=[VMEM] * 6,
        out_specs=(VMEM,) * 3,
        name="update",
    )(sums, image, iterate, residual, direction, precond)
    return tuple(jnp.transpose(v.reshape(params, held, lanes), (1, 0, 2)) for v in outs)


def solution(mesh):
    split = P(AXES, None, None)
    pixel_split = P(None, AXES)
    in_specs = (split,) * 4 + (P("nodes", None, None),) + (pixel_split,) * 3 + (split,)
    return jax.shard_map(
        on_device, mesh=mesh, in_specs=in_specs, out_specs=(split,) * 3, check_vma=False
    )
```

```python
import functools

import jax
import jax.numpy as jnp
from jax import lax
from jax.experimental import pallas as pl
from jax.experimental.pallas import tpu as pltpu
from jax.sharding import PartitionSpec as P

FRAMES = 8
AXES = ("nodes", "cams")
temporal_weight = 0.5
rigid_weight = 0.1
NN = (((1,), (0,)), ((), ()))
NT = (((1,), (1,)), ((), ()))
LANES = 128
ROWS = 16
f32 = jnp.float32
bf16 = jnp.bfloat16

VMEM = pl.BlockSpec(memory_space=pltpu.VMEM)


def limit(slots, pixels):
    need = 8 * 2**20 + slots * ROWS * pixels * 3
    return pltpu.CompilerParams(vmem_limit_bytes=min(need, 56 * 2**20))


def halves(value):
    high = value.astype(bf16)
    low = (value - high.astype(f32)).astype(bf16)
    return high, low


def rows_sum(value):
    return jnp.sum(value, axis=0, keepdims=True)


def loop(count, body):
    lax.fori_loop(0, count, lambda i, carry: (body(i), carry)[1], 0, unroll=count <= 32)


def pack_kernel(block_rows, direction, send_list, out, block):
    rows = direction.shape[0]
    slot_count, owners = send_list.shape
    block[...] = jnp.zeros_like(block)
    block[0:rows, :] = direction[...]
    for s in range(slot_count):
        row, lane = divmod(s * owners, LANES)
        listed = send_list[s : s + 1, :].astype(f32)
        block[rows + row : rows + row + 1, lane : lane + owners] = listed
    value = block[0:block_rows, :]
    for device in range(out.shape[0] // block_rows):
        out[device * block_rows : (device + 1) * block_rows, :] = value


def prepare_kernel(
    held, direction, residual, precond, nbr, grads, node_refs, skin,
    rigid_out, start_out, spread_out, masked, grads_pad,
):
    params, pixels = grads.shape
    slots = masked.shape[0] // ROWS
    chunk = 512
    grads_pad[...] = jnp.zeros_like(grads_pad)
    grads_pad[0:params, :] = grads[...].astype(f32)
    node_rows = lax.broadcasted_iota(jnp.int32, (LANES, chunk), 0)
    for at in range(0, pixels, chunk):
        cols = slice(at, at + chunk)
        refs = node_refs[:, cols]
        node = lax.bitwise_and(refs, LANES - 1)
        slot_of = lax.shift_right_logical(refs[0:1], 7)
        weights = skin[:, cols].astype(f32)
        grad16 = grads_pad[:, cols]
        spread = jnp.where(node_rows == node[0:1], weights[0:1], 0.0)
        for k in range(1, refs.shape[0]):
            spread = spread + jnp.where(node_rows == node[k : k + 1], weights[k : k + 1], 0.0)
        spread_out[:, cols] = spread

        def mask(slot):
            piece = jnp.where(slot_of == slot, grad16, 0.0).astype(bf16)
            masked[pl.ds(pl.multiple_of(slot * ROWS, ROWS), ROWS), cols] = piece

        loop(slots, mask)

    value = direction[...]
    rows = value.shape[0]
    high, low = halves(value)
    stack = jnp.concatenate([high.astype(f32), low.astype(f32), jnp.ones((16, LANES), f32)], axis=0)
    stack = stack.astype(bf16)
    node_rows = lax.broadcasted_iota(jnp.int32, (LANES, LANES), 0)
    patch_row = lax.broadcasted_iota(jnp.int32, (rows, LANES), 0) % held
    edges = nbr.shape[0] // held
    rigid = jnp.zeros_like(value)
    for q in range(held):
        hits = jnp.zeros((LANES, LANES), f32)
        for r in range(edges):
            row = nbr[r * held + q : r * held + q + 1, :]
            hits = hits + jnp.where(node_rows == row, 1.0, 0.0)
        hits = hits.astype(bf16)
        pulled = lax.dot_general(stack, hits, NN, preferred_element_type=f32)
        pushed = lax.dot_general(stack, hits, NT, preferred_element_type=f32)
        degree = pushed[2 * rows : 2 * rows + 1]
        both = pulled + pushed
        part = value * (degree + float(edges)) - (both[:rows] + both[rows : 2 * rows])
        rigid = jnp.where(patch_row == q, part, rigid)
    rigid_out[...] = rigid_weight * rigid
    left = residual[...]
    start_out[...] = jnp.broadcast_to(rows_sum(left * (precond[...] * left)), start_out.shape)


def data_kernel(
    sizes, gathered, direction, rigid, start, spread, masked,
    out, local_out, lists, list_rows, table_rows, products, sem,
):
    owners, cams, slot_count, held, params, block_rows, step = sizes
    devices = owners * cams
    rows = held * params
    slots = owners * slot_count
    pixels = spread.shape[1]
    receiver = lax.axis_index("nodes")
    me = receiver * cams + lax.axis_index("cams")
    extra = block_rows - rows
    for owner in range(owners):
        at = owner * cams * block_rows + rows
        list_rows[owner * extra : (owner + 1) * extra, :] = gathered[at : at + extra, :]
    copy = pltpu.make_async_copy(list_rows, lists, sem)
    copy.start()
    out[...] = jnp.zeros_like(out)
    table_rows[...] = jnp.zeros_like(table_rows)
    value = direction[...]
    before = gathered[pl.ds(jnp.maximum(me - step, 0) * block_rows, rows), :]
    after = gathered[pl.ds(jnp.minimum(me + step, devices - 1) * block_rows, rows), :]
    earlier = jnp.where(me >= step, before, 0.0)
    following = jnp.where(me + step < devices, after, 0.0)
    local = rigid[...] + temporal_weight * (2.0 * value - earlier - following)
    local_out[...] = local
    curvature = rows_sum(value * local)
    copy.wait()

    def patch_of(slot):
        entry = (slot % slot_count) * owners + receiver
        row = (slot // slot_count) * extra + entry // LANES
        return lists[row, entry % LANES].astype(jnp.int32)

    def fetch(slot):
        listed = jnp.maximum(patch_of(slot), 0)
        device = (slot // slot_count) * cams + listed // held
        where = pl.ds(device * block_rows + listed % held, params, stride=held)
        table_rows[pl.ds(pl.multiple_of(slot * ROWS, ROWS), params), :] = gathered[where, :]

    loop(slots, fetch)
    high, low = halves(table_rows[...].T)
    table = jnp.concatenate([high, low], axis=0)

    chunk = 512
    for at in range(0, pixels, chunk):
        cols = slice(at, at + chunk)
        live = masked[:, cols]
        weights = spread[:, cols]
        pulled = lax.dot_general(table, live, NN, preferred_element_type=f32)
        pulled = pulled[:LANES] + pulled[LANES:]
        projected = rows_sum(weights * pulled)
        squared = projected * projected
        for lane in range(0, chunk, LANES):
            curvature = curvature + squared[:, lane : lane + LANES]
        high, low = halves(weights * projected)
        both = jnp.concatenate([high, low], axis=0)
        part = lax.dot_general(live, both, NT, preferred_element_type=f32)
        part = part[:, :LANES] + part[:, LANES:]
        if at == 0:
            products[...] = part
        else:
            products[...] += part

    def give(slot):
        listed = patch_of(slot)

        @pl.when(listed >= 0)
        def _():
            device = (slot // slot_count) * cams + listed // held
            where = pl.ds(device * block_rows + listed % held, params, stride=held)
            piece = products[pl.ds(pl.multiple_of(slot * ROWS, ROWS), params), :]
            out[where, :] = out[where, :] + piece

    loop(slots, give)
    half = LANES // 2
    lane_of = lax.broadcasted_iota(jnp.int32, (1, LANES), 1)
    start_row = start[0:1, :]
    start_row = start_row + pltpu.roll(start_row, half, 1)
    curvature = curvature + pltpu.roll(curvature, half, 1)
    scalars = jnp.where(lane_of < half, start_row, curvature)

    def tell(device):
        out[pl.ds(device * block_rows + rows, 1), :] = scalars

    loop(devices, tell)


def image_kernel(block_rows, received, local, direction, residual, precond, image_out, scalars, norms):
    rows = local.shape[0]
    total = received[0:block_rows, :]
    for device in range(1, received.shape[0] // block_rows):
        total = total + received[device * block_rows : (device + 1) * block_rows, :]
    half = LANES // 2
    lane_of = lax.broadcasted_iota(jnp.int32, (1, LANES), 1)
    last = total[rows : rows + 1]
    start = jnp.sum(jnp.where(lane_of < half, last, 0.0), axis=1, keepdims=True)
    curvature = jnp.sum(jnp.where(lane_of < half, 0.0, last), axis=1, keepdims=True)
    step = start / curvature
    image = total[0:rows] + local[...]
    left = residual[...] - step * image
    image_out[...] = image
    norms[...] = jnp.broadcast_to(rows_sum(left * (precond[...] * left)), norms.shape)
    scalars[...] = jnp.where(
        lax.broadcasted_iota(jnp.int32, scalars.shape, 0) == 0,
        jnp.broadcast_to(start, scalars.shape),
        jnp.broadcast_to(step, scalars.shape),
    )


def iterate_kernel(scalars, image, iterate, residual, direction, new_iterate, new_residual):
    step = scalars[1:2, :]
    new_iterate[...] = iterate[...] + step * direction[...]
    new_residual[...] = residual[...] - step * image[...]


def direction_kernel(norms, scalars, image, residual, direction, precond, new_direction):
    norm = jnp.sum(rows_sum(norms[...]), axis=1, keepdims=True)
    start = scalars[0:1, :]
    left = residual[...] - scalars[1:2, :] * image[...]
    new_direction[...] = precond[...] * left + (norm / start) * direction[...]


def flat(value):
    return jnp.transpose(value, (1, 0, 2)).reshape(-1, value.shape[2])


def exchange(blocks, devices):
    rows, lanes = blocks.shape
    blocks = blocks.reshape(devices, rows // devices, 1, lanes)
    blocks = lax.all_to_all(blocks, AXES, split_axis=0, concat_axis=0, tiled=True)
    return blocks.reshape(rows, lanes)


def on_device(iterate, residual, direction, precond, send_list, grads, node_refs, skin, rigid_nbr):
    held, params, lanes = direction.shape
    pixels = grads.shape[1]
    owners = lax.axis_size("nodes")
    cams = lax.axis_size("cams")
    devices = owners * cams
    slot_count = send_list.shape[2]
    slots = owners * slot_count
    asked = limit(slots, pixels)
    rows = held * params
    extra = -(-slots // lanes)
    block_rows = rows + extra
    vector = jax.ShapeDtypeStruct((rows, lanes), f32)
    few = jax.ShapeDtypeStruct((8, lanes), f32)
    blocks = jax.ShapeDtypeStruct((devices * block_rows, lanes), f32)
    iterate, residual, direction, precond = (flat(v) for v in (iterate, residual, direction, precond))
    nbr = flat(rigid_nbr)
    listed = jnp.transpose(send_list, (2, 0, 1)).reshape(slot_count, owners)

    packed = pl.pallas_call(
        functools.partial(pack_kernel, block_rows),
        out_shape=blocks,
        in_specs=[VMEM] * 2,
        out_specs=VMEM,
        scratch_shapes=[pltpu.VMEM((-(-block_rows // 8) * 8, lanes), f32)],
        compiler_params=asked,
        name="pack",
    )(direction, listed)
    gathered = exchange(packed, devices)

    rigid, start, spread, masked = pl.pallas_call(
        functools.partial(prepare_kernel, held),
        out_shape=(
            vector,
            few,
            jax.ShapeDtypeStruct((lanes, pixels), f32),
            jax.ShapeDtypeStruct((slots * ROWS, pixels), bf16),
        ),
        in_specs=[VMEM] * 7,
        out_specs=(VMEM,) * 4,
        scratch_shapes=[pltpu.VMEM((ROWS, pixels), f32)],
        compiler_params=asked,
        name="prepare",
    )(direction, residual, precond, nbr, grads, node_refs, skin)

    sizes = (owners, cams, slot_count, held, params, block_rows, devices // FRAMES)
    products, local = pl.pallas_call(
        functools.partial(data_kernel, sizes),
        out_shape=(blocks, vector),
        in_specs=[VMEM] * 6,
        out_specs=(VMEM, VMEM),
        scratch_shapes=[
            pltpu.SMEM((owners * extra, lanes), f32),
            pltpu.VMEM((owners * extra, lanes), f32),
            pltpu.VMEM((slots * ROWS, lanes), f32),
            pltpu.VMEM((slots * ROWS, lanes), f32),
            pltpu.SemaphoreType.DMA,
        ],
        compiler_params=asked,
        name="data_products",
    )(gathered, direction, rigid, start, spread, masked)
    received = exchange(products, devices)

    image, scalars, norms = pl.pallas_call(
        functools.partial(image_kernel, block_rows),
        out_shape=(vector, few, jax.ShapeDtypeStruct((devices, lanes), f32)),
        in_specs=[VMEM] * 5,
        out_specs=(VMEM,) * 3,
        compiler_params=asked,
        name="image",
    )(received, local, direction, residual, precond)
    norms = exchange(norms, devices)
    new_iterate, new_residual = pl.pallas_call(
        iterate_kernel,
        out_shape=(vector,) * 2,
        in_specs=[VMEM] * 5,
        out_specs=(VMEM,) * 2,
        compiler_params=asked,
        name="iterate",
    )(scalars, image, iterate, residual, direction)
    new_direction = pl.pallas_call(
        direction_kernel,
        out_shape=vector,
        in_specs=[VMEM] * 6,
        out_specs=VMEM,
        compiler_params=asked,
        name="direction",
    )(norms, scalars, image, residual, direction, precond)
    outs = (new_iterate, new_residual, new_direction)
    return tuple(jnp.transpose(v.reshape(params, held, lanes), (1, 0, 2)) for v in outs)


def solution(mesh):
    split = P(AXES, None, None)
    pixel_split = P(None, AXES)
    in_specs = (split,) * 4 + (P("nodes", None, None),) + (pixel_split,) * 3 + (split,)
    return jax.shard_map(
        on_device, mesh=mesh, in_specs=in_specs, out_specs=(split,) * 3, check_vma=False
    )
```

```python
import functools

import jax
import jax.numpy as jnp
from jax import lax
from jax.experimental import pallas as pl
from jax.experimental.pallas import tpu as pltpu
from jax.sharding import PartitionSpec as P

FRAMES = 8
AXES = ("nodes", "cams")
temporal_weight = 0.5
rigid_weight = 0.1
NN = (((1,), (0,)), ((), ()))
NT = (((1,), (1,)), ((), ()))
LANES = 128
ROWS = 16
f32 = jnp.float32
bf16 = jnp.bfloat16

VMEM = pl.BlockSpec(memory_space=pltpu.VMEM)
HBM = pl.BlockSpec(memory_space=pltpu.HBM)


def limit(slots, pixels):
    need = 8 * 2**20 + slots * ROWS * pixels * 3
    return pltpu.CompilerParams(vmem_limit_bytes=min(need, 56 * 2**20))


def halves(value):
    high = value.astype(bf16)
    low = (value - high.astype(f32)).astype(bf16)
    return high, low


def rows_sum(value):
    return jnp.sum(value, axis=0, keepdims=True)


def loop(count, body):
    lax.fori_loop(0, count, lambda i, carry: (body(i), carry)[1], 0, unroll=count <= 32)


def pack_kernel(block_rows, direction_hbm, send_list_hbm, out, block, send_list, sems):
    rows = direction_hbm.shape[0]
    slot_count, _, owners = send_list.shape
    list_copy = pltpu.make_async_copy(send_list_hbm, send_list, sems.at[0])
    list_copy.start()
    copy = pltpu.make_async_copy(direction_hbm, block.at[0:rows, :], sems.at[1])
    copy.start()
    block[rows:, :] = jnp.zeros((block.shape[0] - rows, LANES), f32)
    list_copy.wait()
    for s in range(slot_count):
        row, lane = divmod(s * owners, LANES)
        block[rows + row : rows + row + 1, lane : lane + owners] = send_list[s].astype(f32)
    copy.wait()
    value = block[0:block_rows, :]
    for device in range(out.shape[0] // block_rows):
        out[device * block_rows : (device + 1) * block_rows, :] = value


def prepare_kernel(
    held, direction, residual, precond, nbr, grads, node_refs, skin,
    rigid_out, start_out, spread_out, masked, grads_pad,
):
    params, pixels = grads.shape
    slots = masked.shape[0] // ROWS
    chunk = 512
    grads_pad[...] = jnp.zeros_like(grads_pad)
    grads_pad[0:params, :] = grads[...].astype(f32)
    node_rows = lax.broadcasted_iota(jnp.int32, (LANES, chunk), 0)
    for at in range(0, pixels, chunk):
        cols = slice(at, at + chunk)
        refs = node_refs[:, cols]
        node = lax.bitwise_and(refs, LANES - 1)
        slot_of = lax.shift_right_logical(refs[0:1], 7)
        weights = skin[:, cols].astype(f32)
        grad16 = grads_pad[:, cols]
        spread = jnp.where(node_rows == node[0:1], weights[0:1], 0.0)
        for k in range(1, refs.shape[0]):
            spread = spread + jnp.where(node_rows == node[k : k + 1], weights[k : k + 1], 0.0)
        spread_out[:, cols] = spread

        def mask(slot):
            piece = jnp.where(slot_of == slot, grad16, 0.0).astype(bf16)
            masked[pl.ds(pl.multiple_of(slot * ROWS, ROWS), ROWS), cols] = piece

        loop(slots, mask)

    value = direction[...]
    rows = value.shape[0]
    high, low = halves(value)
    stack = jnp.concatenate([high.astype(f32), low.astype(f32), jnp.ones((16, LANES), f32)], axis=0)
    stack = stack.astype(bf16)
    node_rows = lax.broadcasted_iota(jnp.int32, (LANES, LANES), 0)
    patch_row = lax.broadcasted_iota(jnp.int32, (rows, LANES), 0) % held
    edges = nbr.shape[0] // held
    rigid = jnp.zeros_like(value)
    for q in range(held):
        hits = jnp.zeros((LANES, LANES), f32)
        for r in range(edges):
            row = nbr[r * held + q : r * held + q + 1, :]
            hits = hits + jnp.where(node_rows == row, 1.0, 0.0)
        hits = hits.astype(bf16)
        pulled = lax.dot_general(stack, hits, NN, preferred_element_type=f32)
        pushed = lax.dot_general(stack, hits, NT, preferred_element_type=f32)
        degree = pushed[2 * rows : 2 * rows + 1]
        both = pulled + pushed
        part = value * (degree + float(edges)) - (both[:rows] + both[rows : 2 * rows])
        rigid = jnp.where(patch_row == q, part, rigid)
    rigid_out[...] = rigid_weight * rigid
    left = residual[...]
    start_out[...] = jnp.broadcast_to(rows_sum(left * (precond[...] * left)), start_out.shape)


def data_kernel(
    sizes, gathered, rigid, start, spread, masked,
    out, local_out, lists, list_rows, table_rows, products, sem,
):
    owners, cams, slot_count, held, params, block_rows, step = sizes
    devices = owners * cams
    rows = held * params
    slots = owners * slot_count
    pixels = spread.shape[1]
    receiver = lax.axis_index("nodes")
    me = receiver * cams + lax.axis_index("cams")
    extra = block_rows - rows
    for owner in range(owners):
        at = owner * cams * block_rows + rows
        list_rows[owner * extra : (owner + 1) * extra, :] = gathered[at : at + extra, :]
    copy = pltpu.make_async_copy(list_rows, lists, sem)
    copy.start()
    out[...] = jnp.zeros_like(out)
    table_rows[...] = jnp.zeros_like(table_rows)
    value = gathered[pl.ds(me * block_rows, rows), :]
    before = gathered[pl.ds(jnp.maximum(me - step, 0) * block_rows, rows), :]
    after = gathered[pl.ds(jnp.minimum(me + step, devices - 1) * block_rows, rows), :]
    earlier = jnp.where(me >= step, before, 0.0)
    following = jnp.where(me + step < devices, after, 0.0)
    local = rigid[...] + temporal_weight * (2.0 * value - earlier - following)
    local_out[...] = local
    curvature = rows_sum(value * local)
    copy.wait()

    def patch_of(slot):
        entry = (slot % slot_count) * owners + receiver
        row = (slot // slot_count) * extra + entry // LANES
        return lists[row, entry % LANES].astype(jnp.int32)

    def fetch(slot):
        listed = jnp.maximum(patch_of(slot), 0)
        device = (slot // slot_count) * cams + listed // held
        where = pl.ds(device * block_rows + listed % held, params, stride=held)
        table_rows[pl.ds(pl.multiple_of(slot * ROWS, ROWS), params), :] = gathered[where, :]

    loop(slots, fetch)
    high, low = halves(table_rows[...].T)
    table = jnp.concatenate([high, low], axis=0)

    chunk = 512
    for at in range(0, pixels, chunk):
        cols = slice(at, at + chunk)
        live = masked[:, cols]
        weights = spread[:, cols]
        pulled = lax.dot_general(table, live, NN, preferred_element_type=f32)
        pulled = pulled[:LANES] + pulled[LANES:]
        projected = rows_sum(weights * pulled)
        squared = projected * projected
        for lane in range(0, chunk, LANES):
            curvature = curvature + squared[:, lane : lane + LANES]
        high, low = halves(weights * projected)
        both = jnp.concatenate([high, low], axis=0)
        part = lax.dot_general(live, both, NT, preferred_element_type=f32)
        part = part[:, :LANES] + part[:, LANES:]
        if at == 0:
            products[...] = part
        else:
            products[...] += part

    def give(slot):
        listed = jnp.maximum(patch_of(slot), 0)
        device = (slot // slot_count) * cams + listed // held
        where = pl.ds(device * block_rows + listed % held, params, stride=held)
        piece = products[pl.ds(pl.multiple_of(slot * ROWS, ROWS), params), :]
        out[where, :] = out[where, :] + piece

    loop(slots, give)
    half = LANES // 2
    lane_of = lax.broadcasted_iota(jnp.int32, (1, LANES), 1)
    start_row = start[0:1, :]
    start_row = start_row + pltpu.roll(start_row, half, 1)
    curvature = curvature + pltpu.roll(curvature, half, 1)
    scalars = jnp.where(lane_of < half, start_row, curvature)

    def tell(device):
        out[pl.ds(device * block_rows + rows, 1), :] = scalars

    loop(devices, tell)


def image_kernel(block_rows, received, local, direction, residual, precond, image_out, scalars, norms):
    rows = local.shape[0]
    total = received[0:block_rows, :]
    for device in range(1, received.shape[0] // block_rows):
        total = total + received[device * block_rows : (device + 1) * block_rows, :]
    half = LANES // 2
    lane_of = lax.broadcasted_iota(jnp.int32, (1, LANES), 1)
    last = total[rows : rows + 1]
    start = jnp.sum(jnp.where(lane_of < half, last, 0.0), axis=1, keepdims=True)
    curvature = jnp.sum(jnp.where(lane_of < half, 0.0, last), axis=1, keepdims=True)
    step = start / curvature
    image = total[0:rows] + local[...]
    left = residual[...] - step * image
    image_out[...] = image
    norms[...] = jnp.broadcast_to(rows_sum(left * (precond[...] * left)), norms.shape)
    scalars[...] = jnp.where(
        lax.broadcasted_iota(jnp.int32, scalars.shape, 0) == 0,
        jnp.broadcast_to(start, scalars.shape),
        jnp.broadcast_to(step, scalars.shape),
    )


def iterate_kernel(scalars, image, iterate, residual, direction, new_iterate, new_residual):
    step = scalars[1:2, :]
    new_iterate[...] = iterate[...] + step * direction[...]
    new_residual[...] = residual[...] - step * image[...]


def direction_kernel(norms, scalars, image, residual, direction, precond, new_direction):
    norm = jnp.sum(rows_sum(norms[...]), axis=1, keepdims=True)
    start = scalars[0:1, :]
    left = residual[...] - scalars[1:2, :] * image[...]
    new_direction[...] = precond[...] * left + (norm / start) * direction[...]


def flat(value):
    return jnp.transpose(value, (1, 0, 2)).reshape(-1, value.shape[2])


def exchange(blocks, devices):
    rows, lanes = blocks.shape
    blocks = blocks.reshape(devices, rows // devices, 1, lanes)
    blocks = lax.all_to_all(blocks, AXES, split_axis=0, concat_axis=0, tiled=True)
    return blocks.reshape(rows, lanes)


def on_device(iterate, residual, direction, precond, send_list, grads, node_refs, skin, rigid_nbr):
    held, params, lanes = direction.shape
    pixels = grads.shape[1]
    owners = lax.axis_size("nodes")
    cams = lax.axis_size("cams")
    devices = owners * cams
    slot_count = send_list.shape[2]
    slots = owners * slot_count
    asked = limit(slots, pixels)
    rows = held * params
    extra = -(-slots // lanes)
    block_rows = rows + extra
    vector = jax.ShapeDtypeStruct((rows, lanes), f32)
    few = jax.ShapeDtypeStruct((8, lanes), f32)
    blocks = jax.ShapeDtypeStruct((devices * block_rows, lanes), f32)
    iterate, residual, direction, precond = (flat(v) for v in (iterate, residual, direction, precond))
    nbr = flat(rigid_nbr)
    listed = jnp.transpose(send_list, (2, 0, 1))

    packed = pl.pallas_call(
        functools.partial(pack_kernel, block_rows),
        out_shape=blocks,
        in_specs=[HBM] * 2,
        out_specs=VMEM,
        scratch_shapes=[
            pltpu.VMEM((-(-block_rows // 8) * 8, lanes), f32),
            pltpu.VMEM((slot_count, 1, owners), jnp.int32),
            pltpu.SemaphoreType.DMA((2,)),
        ],
        compiler_params=asked,
        name="pack",
    )(direction, listed)
    gathered = exchange(packed, devices)

    rigid, start, spread, masked = pl.pallas_call(
        functools.partial(prepare_kernel, held),
        out_shape=(
            vector,
            few,
            jax.ShapeDtypeStruct((lanes, pixels), f32),
            jax.ShapeDtypeStruct((slots * ROWS, pixels), bf16),
        ),
        in_specs=[VMEM] * 7,
        out_specs=(VMEM,) * 4,
        scratch_shapes=[pltpu.VMEM((ROWS, pixels), f32)],
        compiler_params=asked,
        name="prepare",
    )(direction, residual, precond, nbr, grads, node_refs, skin)

    sizes = (owners, cams, slot_count, held, params, block_rows, devices // FRAMES)
    products, local = pl.pallas_call(
        functools.partial(data_kernel, sizes),
        out_shape=(blocks, vector),
        in_specs=[VMEM] * 5,
        out_specs=(VMEM, VMEM),
        scratch_shapes=[
            pltpu.SMEM((owners * extra, lanes), f32),
            pltpu.VMEM((owners * extra, lanes), f32),
            pltpu.VMEM((slots * ROWS, lanes), f32),
            pltpu.VMEM((slots * ROWS, lanes), f32),
            pltpu.SemaphoreType.DMA,
        ],
        compiler_params=asked,
        name="data_products",
    )(gathered, rigid, start, spread, masked)
    received = exchange(products, devices)

    image, scalars, norms = pl.pallas_call(
        functools.partial(image_kernel, block_rows),
        out_shape=(vector, few, jax.ShapeDtypeStruct((devices, lanes), f32)),
        in_specs=[VMEM] * 5,
        out_specs=(VMEM,) * 3,
        compiler_params=asked,
        name="image",
    )(received, local, direction, residual, precond)
    norms = exchange(norms, devices)
    new_iterate, new_residual = pl.pallas_call(
        iterate_kernel,
        out_shape=(vector,) * 2,
        in_specs=[VMEM] * 5,
        out_specs=(VMEM,) * 2,
        compiler_params=asked,
        name="iterate",
    )(scalars, image, iterate, residual, direction)
    new_direction = pl.pallas_call(
        direction_kernel,
        out_shape=vector,
        in_specs=[VMEM] * 6,
        out_specs=VMEM,
        compiler_params=asked,
        name="direction",
    )(norms, scalars, image, residual, direction, precond)
    outs = (new_iterate, new_residual, new_direction)
    return tuple(jnp.transpose(v.reshape(params, held, lanes), (1, 0, 2)) for v in outs)


def solution(mesh):
    split = P(AXES, None, None)
    pixel_split = P(None, AXES)
    in_specs = (split,) * 4 + (P("nodes", None, None),) + (pixel_split,) * 3 + (split,)
    return jax.shard_map(
        on_device, mesh=mesh, in_specs=in_specs, out_specs=(split,) * 3, check_vma=False
    )
```

```python
import functools

import jax
import jax.numpy as jnp
from jax import lax
from jax.experimental import pallas as pl
from jax.experimental.pallas import tpu as pltpu
from jax.sharding import PartitionSpec as P

FRAMES = 8
AXES = ("nodes", "cams")
temporal_weight = 0.5
rigid_weight = 0.1
NN = (((1,), (0,)), ((), ()))
NT = (((1,), (1,)), ((), ()))
LANES = 128
ROWS = 16
f32 = jnp.float32
bf16 = jnp.bfloat16

VMEM = pl.BlockSpec(memory_space=pltpu.VMEM)
SMEM = pl.BlockSpec(memory_space=pltpu.SMEM)


def limit(slots, pixels):
    need = 8 * 2**20 + slots * ROWS * pixels * 3
    return pltpu.CompilerParams(vmem_limit_bytes=min(need, 56 * 2**20))


def halves(value):
    high = value.astype(bf16)
    low = (value - high.astype(f32)).astype(bf16)
    return high, low


def rows_sum(value):
    return jnp.sum(value, axis=0, keepdims=True)


def loop(count, body):
    lax.fori_loop(0, count, lambda i, carry: (body(i), carry)[1], 0, unroll=count <= 32)


def pack_kernel(block_rows, direction, list_rows, out, block):
    rows = direction.shape[0]
    block[0:rows, :] = direction[...]
    block[rows:block_rows, :] = list_rows[...]
    value = block[0:block_rows, :]

    def write(device):
        out[pl.ds(device * block_rows, block_rows), :] = value

    loop(out.shape[0] // block_rows, write)


def prepare_kernel(
    held, piece, direction, residual, precond, nbr, grads, node_refs, skin,
    stack_out, sums_out, spread_out, masked, grads_pad,
):
    params, pixels = grads.shape
    slots = masked.shape[0] // ROWS
    chunk = 512
    grads_pad[...] = jnp.zeros_like(grads_pad)
    grads_pad[0:params, :] = grads[...].astype(f32)
    node_rows = lax.broadcasted_iota(jnp.int32, (LANES, chunk), 0)
    for at in range(0, pixels, chunk):
        cols = slice(at, at + chunk)
        refs = node_refs[:, cols]
        node = lax.bitwise_and(refs, LANES - 1)
        slot_of = lax.shift_right_logical(refs[0:1], 7)
        weights = skin[:, cols].astype(f32)
        grad16 = grads_pad[:, cols]
        spread = jnp.where(node_rows == node[0:1], weights[0:1], 0.0)
        for k in range(1, refs.shape[0]):
            spread = spread + jnp.where(node_rows == node[k : k + 1], weights[k : k + 1], 0.0)
        spread_out[:, cols] = spread

        def mask(slot):
            piece = jnp.where(slot_of == slot, grad16, 0.0).astype(bf16)
            masked[pl.ds(pl.multiple_of(slot * ROWS, ROWS), ROWS), cols] = piece

        loop(slots, mask)

    value = direction[...]
    rows = value.shape[0]
    high, low = halves(value)
    stack = jnp.concatenate([high.astype(f32), low.astype(f32), jnp.ones((16, LANES), f32)], axis=0)
    stack = stack.astype(bf16)
    node_rows = lax.broadcasted_iota(jnp.int32, (LANES, LANES), 0)
    patch_row = lax.broadcasted_iota(jnp.int32, (rows, LANES), 0) % held
    edges = nbr.shape[0] // held
    rigid = jnp.zeros_like(value)
    for q in range(held):
        hits = jnp.zeros((LANES, LANES), f32)
        for r in range(edges):
            row = nbr[r * held + q : r * held + q + 1, :]
            hits = hits + jnp.where(node_rows == row, 1.0, 0.0)
        hits = hits.astype(bf16)
        pulled = lax.dot_general(stack, hits, NN, preferred_element_type=f32)
        pushed = lax.dot_general(stack, hits, NT, preferred_element_type=f32)
        degree = pushed[2 * rows : 2 * rows + 1]
        both = pulled + pushed
        part = value * (degree + float(edges)) - (both[:rows] + both[rows : 2 * rows])
        rigid = jnp.where(patch_row == q, part, rigid)
    left = residual[...]
    scale = precond[...]
    near = rigid_weight * rigid + (2.0 * temporal_weight) * value
    pieces = stack_out.shape[0] // (3 * piece)
    for c in range(pieces):
        for k, source in enumerate((left, scale, near)):
            part = source[c * piece : (c + 1) * piece] if c * piece < rows else jnp.zeros((piece, LANES), f32)
            stack_out[(3 * c + k) * piece : (3 * c + k + 1) * piece, :] = part
    sums_out[0:1, :] = rows_sum(left * (scale * left))
    sums_out[1:2, :] = rows_sum(value * near)


def data_kernel(
    sizes, gathered, sums, spread, masked,
    out, frames_out, lists, list_rows, table_rows, products, sem,
):
    owners, cams, slot_count, held, params, part, block_rows, back_rows, step = sizes
    devices = owners * cams
    rows = held * params
    piece = held * part
    slots = owners * slot_count
    pixels = spread.shape[1]
    receiver = lax.axis_index("nodes")
    cam = lax.axis_index("cams")
    extra = block_rows - rows
    for owner in range(owners):
        at = owner * cams * block_rows + rows
        list_rows[owner * extra : (owner + 1) * extra, :] = gathered[at : at + extra, :]
    copy = pltpu.make_async_copy(list_rows, lists, sem)
    copy.start()
    table_rows[...] = jnp.zeros_like(table_rows)
    curvature = sums[1:2, :]
    inside = cam * piece < rows
    offset = jnp.minimum(cam * piece, rows - piece)
    for c in range(cams):
        device = receiver * cams + c
        value = gathered[pl.ds(device * block_rows + offset, piece), :]
        before = gathered[pl.ds(jnp.maximum(device - step, 0) * block_rows + offset, piece), :]
        after = gathered[
            pl.ds(jnp.minimum(device + step, devices - 1) * block_rows + offset, piece), :
        ]
        earlier = jnp.where(jnp.logical_and(inside, device >= step), before, 0.0)
        following = jnp.where(jnp.logical_and(inside, device + step < devices), after, 0.0)
        frames = -temporal_weight * (earlier + following)
        frames_out[c * piece : (c + 1) * piece, :] = frames
        curvature = curvature + rows_sum(value * frames)
    copy.wait()

    def patch_of(slot):
        entry = (slot % slot_count) * owners + receiver
        row = (slot // slot_count) * extra + entry // LANES
        return lists[row, entry % LANES].astype(jnp.int32)

    def fetch(slot):
        listed = jnp.maximum(patch_of(slot), 0)
        device = (slot // slot_count) * cams + listed // held
        where = pl.ds(device * block_rows + listed % held, params, stride=held)
        table_rows[pl.ds(pl.multiple_of(slot * ROWS, ROWS), params), :] = gathered[where, :]

    loop(slots, fetch)
    high, low = halves(table_rows[...].T)
    table = jnp.concatenate([high, low], axis=0)

    chunk = 512
    for at in range(0, pixels, chunk):
        cols = slice(at, at + chunk)
        live = masked[:, cols]
        weights = spread[:, cols]
        pulled = lax.dot_general(table, live, NN, preferred_element_type=f32)
        pulled = pulled[:LANES] + pulled[LANES:]
        projected = rows_sum(weights * pulled)
        squared = projected * projected
        for lane in range(0, chunk, LANES):
            curvature = curvature + squared[:, lane : lane + LANES]
        high, low = halves(weights * projected)
        both = jnp.concatenate([high, low], axis=0)
        back = lax.dot_general(live, both, NT, preferred_element_type=f32)
        back = back[:, :LANES] + back[:, LANES:]
        if at == 0:
            products[...] = back
        else:
            products[...] += back

    half = LANES // 2
    lane_of = lax.broadcasted_iota(jnp.int32, (1, LANES), 1)
    start = sums[0:1, :]
    start = start + pltpu.roll(start, half, 1)
    curvature = curvature + pltpu.roll(curvature, half, 1)
    scalars = jnp.where(lane_of < half, start, curvature)

    def give(owner):
        for c in range(cams):
            base = (owner * cams + c) * back_rows
            for s in range(slot_count):
                if c * part < params:
                    at = (owner * slot_count + s) * ROWS + c * part
                    value = products[pl.ds(at, part), :]
                else:
                    value = jnp.zeros((part, LANES), f32)
                out[pl.ds(base + s * part, part), :] = value
            out[pl.ds(base + slot_count * part, 1), :] = scalars

    loop(owners, give)


def image_kernel(sizes, received, frames, mine, send_list, scalars, blocks, image):
    owners, cams, slot_count, held, params, part, block_rows, back_rows, step = sizes
    piece = held * part
    image[...] = jnp.zeros_like(image)
    last = jnp.zeros((1, LANES), f32)

    def collect(owner, last):
        at = owner * cams * back_rows
        total = received[pl.ds(at, back_rows), :]
        for c in range(1, cams):
            total = total + received[pl.ds(at + c * back_rows, back_rows), :]
        for s in range(slot_count):
            listed = jnp.maximum(send_list[s, 0, owner], 0)
            where = pl.ds((listed // held) * piece + listed % held, part, stride=held)
            image[where, :] = image[where, :] + total[s * part : (s + 1) * part]
        return last + total[back_rows - 1 : back_rows]

    last = lax.fori_loop(0, owners, collect, last, unroll=owners <= 32)
    half = LANES // 2
    lane_of = lax.broadcasted_iota(jnp.int32, (1, LANES), 1)
    start = jnp.sum(jnp.where(lane_of < half, last, 0.0), axis=1, keepdims=True)
    curvature = jnp.sum(jnp.where(lane_of < half, 0.0, last), axis=1, keepdims=True)
    length = start / curvature
    norms = jnp.zeros((1, LANES), f32)
    for c in range(cams):
        rows = slice(c * piece, (c + 1) * piece)
        residual, precond, near = (
            mine[(3 * c + k) * piece : (3 * c + k + 1) * piece, :] for k in range(3)
        )
        value = image[rows, :] + near + frames[rows, :]
        image[rows, :] = value
        left = residual - length * value
        norms = norms + rows_sum(left * (precond * left))
    scalars[0:1, :] = jnp.broadcast_to(start, (1, LANES))
    scalars[1:2, :] = jnp.broadcast_to(length, (1, LANES))

    def tell(owner):
        for c in range(cams):
            base = (owner * cams + c) * (piece + 1)
            blocks[pl.ds(base, 1), :] = norms
            blocks[pl.ds(base + 1, piece), :] = image[c * piece : (c + 1) * piece, :]

    loop(owners, tell)


def update_kernel(
    sizes, arrived, scalars, iterate, residual, direction, precond,
    new_iterate, new_residual, new_direction,
):
    owners, cams, slot_count, held, params, part, block_rows, back_rows, step = sizes
    piece = held * part
    rows = iterate.shape[0]
    own = lax.axis_index("nodes")
    norms = arrived[0:1, :]
    for device in range(1, owners * cams):
        norms = norms + arrived[device * (piece + 1) : device * (piece + 1) + 1, :]
    start, length = scalars[0:1, :], scalars[1:2, :]
    ratio = jnp.sum(norms, axis=1, keepdims=True) / start
    for c in range(rows // piece):
        here = slice(c * piece, (c + 1) * piece)
        image = arrived[pl.ds((own * cams + c) * (piece + 1) + 1, piece), :]
        value = direction[here, :]
        left = residual[here, :] - length * image
        new_iterate[here, :] = iterate[here, :] + length * value
        new_residual[here, :] = left
        new_direction[here, :] = precond[here, :] * left + ratio * value


def flat(value):
    return jnp.transpose(value, (1, 0, 2)).reshape(-1, value.shape[2])


def exchange(blocks, axes):
    rows, lanes = blocks.shape
    peers = lax.axis_size(axes)
    blocks = blocks.reshape(peers, rows // peers, 1, lanes)
    blocks = lax.all_to_all(blocks, axes, split_axis=0, concat_axis=0, tiled=True)
    return blocks.reshape(rows, lanes)


def on_device(iterate, residual, direction, precond, send_list, grads, node_refs, skin, rigid_nbr):
    held, params, lanes = direction.shape
    pixels = grads.shape[1]
    owners = lax.axis_size("nodes")
    cams = lax.axis_size("cams")
    devices = owners * cams
    slot_count = send_list.shape[2]
    slots = owners * slot_count
    asked = limit(slots, pixels)
    rows = held * params
    extra = -(-slots // lanes)
    block_rows = rows + extra
    part = next(n for n in range(1, params + 1) if params % n == 0 and n * cams >= params)
    piece = held * part
    back_rows = slot_count * part + 1
    sizes = (
        owners, cams, slot_count, held, params, part, block_rows, back_rows, devices // FRAMES
    )

    def array(count):
        return jax.ShapeDtypeStruct((count, lanes), f32)

    iterate, residual, direction, precond = (flat(v) for v in (iterate, residual, direction, precond))
    nbr = flat(rigid_nbr)
    by_slot = jnp.transpose(send_list, (2, 0, 1))
    listed = by_slot.reshape(-1).astype(f32)
    list_rows = jnp.pad(listed, (0, extra * lanes - slots)).reshape(extra, lanes)

    packed = pl.pallas_call(
        functools.partial(pack_kernel, block_rows),
        out_shape=array(devices * block_rows),
        in_specs=[VMEM] * 2,
        out_specs=VMEM,
        scratch_shapes=[pltpu.VMEM((-(-block_rows // 8) * 8, lanes), f32)],
        compiler_params=asked,
        name="pack",
    )(direction, list_rows)
    gathered = exchange(packed, AXES)

    stack, sums, spread, masked = pl.pallas_call(
        functools.partial(prepare_kernel, held, piece),
        out_shape=(
            array(3 * cams * piece),
            array(8),
            jax.ShapeDtypeStruct((lanes, pixels), f32),
            jax.ShapeDtypeStruct((slots * ROWS, pixels), bf16),
        ),
        in_specs=[VMEM] * 7,
        out_specs=(VMEM,) * 4,
        scratch_shapes=[pltpu.VMEM((ROWS, pixels), f32)],
        compiler_params=asked,
        name="prepare",
    )(direction, residual, precond, nbr, grads, node_refs, skin)
    mine, sums = lax.optimization_barrier((exchange(stack, "cams"), sums))

    products, frames = pl.pallas_call(
        functools.partial(data_kernel, sizes),
        out_shape=(array(devices * back_rows), array(cams * piece)),
        in_specs=[VMEM] * 4,
        out_specs=(VMEM, VMEM),
        scratch_shapes=[
            pltpu.SMEM((owners * extra, lanes), f32),
            pltpu.VMEM((owners * extra, lanes), f32),
            pltpu.VMEM((slots * ROWS, lanes), f32),
            pltpu.VMEM((slots * ROWS, lanes), f32),
            pltpu.SemaphoreType.DMA,
        ],
        compiler_params=asked,
        name="data_products",
    )(gathered, sums, spread, masked)
    received = exchange(products, AXES)

    scalars, blocks = pl.pallas_call(
        functools.partial(image_kernel, sizes),
        out_shape=(array(8), array(devices * (piece + 1))),
        in_specs=[VMEM] * 3 + [SMEM],
        out_specs=(VMEM,) * 2,
        scratch_shapes=[pltpu.VMEM((cams * piece, lanes), f32)],
        compiler_params=asked,
        name="image",
    )(received, frames, mine, by_slot)
    arrived = exchange(blocks, AXES)
    outs = pl.pallas_call(
        functools.partial(update_kernel, sizes),
        out_shape=(array(rows),) * 3,
        in_specs=[VMEM] * 6,
        out_specs=(VMEM,) * 3,
        compiler_params=asked,
        name="update",
    )(arrived, scalars, iterate, residual, direction, precond)
    return tuple(jnp.transpose(v.reshape(params, held, lanes), (1, 0, 2)) for v in outs)


def solution(mesh):
    split = P(AXES, None, None)
    pixel_split = P(None, AXES)
    in_specs = (split,) * 4 + (P("nodes", None, None),) + (pixel_split,) * 3 + (split,)
    return jax.shard_map(
        on_device, mesh=mesh, in_specs=in_specs, out_specs=(split,) * 3, check_vma=False
    )
```

```python
import functools

import jax
import jax.numpy as jnp
from jax import lax
from jax.experimental import pallas as pl
from jax.experimental.pallas import tpu as pltpu
from jax.sharding import PartitionSpec as P

FRAMES = 8
AXES = ("nodes", "cams")
temporal_weight = 0.5
rigid_weight = 0.1
NN = (((1,), (0,)), ((), ()))
NT = (((1,), (1,)), ((), ()))
LANES = 128
ROWS = 16
f32 = jnp.float32
bf16 = jnp.bfloat16

VMEM = pl.BlockSpec(memory_space=pltpu.VMEM)
SMEM = pl.BlockSpec(memory_space=pltpu.SMEM)


def limit(slots, pixels):
    need = 8 * 2**20 + slots * ROWS * pixels * 3
    return pltpu.CompilerParams(vmem_limit_bytes=min(need, 56 * 2**20))


def halves(value):
    high = value.astype(bf16)
    low = (value - high.astype(f32)).astype(bf16)
    return high, low


def rows_sum(value):
    return jnp.sum(value, axis=0, keepdims=True)


def loop(count, body):
    lax.fori_loop(0, count, lambda i, carry: (body(i), carry)[1], 0, unroll=count <= 32)


def pack_kernel(block_rows, direction, list_rows, out, block):
    rows = direction.shape[0]
    block[0:rows, :] = direction[...]
    block[rows:block_rows, :] = list_rows[...]
    value = block[0:block_rows, :]

    def write(device):
        out[pl.ds(device * block_rows, block_rows), :] = value

    loop(out.shape[0] // block_rows, write)


def near_kernel(held, piece, rows, joined, stack_out, sums_out):
    value = joined[0:rows, :]
    left = joined[rows : 2 * rows, :]
    scale = joined[2 * rows : 3 * rows, :]
    high, low = halves(value)
    stack = jnp.concatenate([high.astype(f32), low.astype(f32), jnp.ones((16, LANES), f32)], axis=0)
    stack = stack.astype(bf16)
    node_rows = lax.broadcasted_iota(jnp.int32, (LANES, LANES), 0).astype(f32)
    patch_row = lax.broadcasted_iota(jnp.int32, (rows, LANES), 0) % held
    edges = (joined.shape[0] - 3 * rows) // held
    rigid = jnp.zeros_like(value)
    for q in range(held):
        hits = jnp.zeros((LANES, LANES), f32)
        for r in range(edges):
            at = 3 * rows + r * held + q
            hits = hits + jnp.where(node_rows == joined[at : at + 1, :], 1.0, 0.0)
        hits = hits.astype(bf16)
        pulled = lax.dot_general(stack, hits, NN, preferred_element_type=f32)
        pushed = lax.dot_general(stack, hits, NT, preferred_element_type=f32)
        degree = pushed[2 * rows : 2 * rows + 1]
        both = pulled + pushed
        part = value * (degree + float(edges)) - (both[:rows] + both[rows : 2 * rows])
        rigid = jnp.where(patch_row == q, part, rigid)
    near = rigid_weight * rigid + (2.0 * temporal_weight) * value
    for c in range(stack_out.shape[0] // (3 * piece)):
        for k, source in enumerate((left, scale, near)):
            if c * piece < rows:
                part = source[c * piece : (c + 1) * piece]
            else:
                part = jnp.zeros((piece, LANES), f32)
            stack_out[(3 * c + k) * piece : (3 * c + k + 1) * piece, :] = part
    sums_out[0:1, :] = rows_sum(left * (scale * left))
    sums_out[1:2, :] = rows_sum(value * near)


def masks_kernel(grads, node_refs, skin, spread_out, masked, grads_pad):
    params, pixels = grads.shape
    slots = masked.shape[0] // ROWS
    chunk = 512
    grads_pad[...] = jnp.zeros_like(grads_pad)
    grads_pad[0:params, :] = grads[...].astype(f32)
    node_rows = lax.broadcasted_iota(jnp.int32, (LANES, chunk), 0)
    for at in range(0, pixels, chunk):
        cols = slice(at, at + chunk)
        refs = node_refs[:, cols]
        node = lax.bitwise_and(refs, LANES - 1)
        slot_of = lax.shift_right_logical(refs[0:1], 7)
        weights = skin[:, cols].astype(f32)
        grad16 = grads_pad[:, cols]
        spread = jnp.where(node_rows == node[0:1], weights[0:1], 0.0)
        for k in range(1, refs.shape[0]):
            spread = spread + jnp.where(node_rows == node[k : k + 1], weights[k : k + 1], 0.0)
        spread_out[:, cols] = spread

        def mask(slot):
            piece = jnp.where(slot_of == slot, grad16, 0.0).astype(bf16)
            masked[pl.ds(pl.multiple_of(slot * ROWS, ROWS), ROWS), cols] = piece

        loop(slots, mask)


def data_kernel(
    sizes, gathered, sums, spread, masked,
    out, frames_out, lists, list_rows, table_rows, products, sem,
):
    owners, cams, slot_count, held, params, part, block_rows, back_rows, step = sizes
    devices = owners * cams
    rows = held * params
    piece = held * part
    slots = owners * slot_count
    pixels = spread.shape[1]
    receiver = lax.axis_index("nodes")
    cam = lax.axis_index("cams")
    extra = block_rows - rows
    for owner in range(owners):
        at = owner * cams * block_rows + rows
        list_rows[owner * extra : (owner + 1) * extra, :] = gathered[at : at + extra, :]
    copy = pltpu.make_async_copy(list_rows, lists, sem)
    copy.start()
    table_rows[...] = jnp.zeros_like(table_rows)
    curvature = sums[1:2, :]
    inside = cam * piece < rows
    offset = jnp.minimum(cam * piece, rows - piece)
    for c in range(cams):
        device = receiver * cams + c
        value = gathered[pl.ds(device * block_rows + offset, piece), :]
        before = gathered[pl.ds(jnp.maximum(device - step, 0) * block_rows + offset, piece), :]
        after = gathered[
            pl.ds(jnp.minimum(device + step, devices - 1) * block_rows + offset, piece), :
        ]
        earlier = jnp.where(jnp.logical_and(inside, device >= step), before, 0.0)
        following = jnp.where(jnp.logical_and(inside, device + step < devices), after, 0.0)
        frames = -temporal_weight * (earlier + following)
        frames_out[c * piece : (c + 1) * piece, :] = frames
        curvature = curvature + rows_sum(value * frames)
    copy.wait()

    def patch_of(slot):
        entry = (slot % slot_count) * owners + receiver
        row = (slot // slot_count) * extra + entry // LANES
        return lists[row, entry % LANES].astype(jnp.int32)

    def fetch(slot):
        listed = jnp.maximum(patch_of(slot), 0)
        device = (slot // slot_count) * cams + listed // held
        where = pl.ds(device * block_rows + listed % held, params, stride=held)
        table_rows[pl.ds(pl.multiple_of(slot * ROWS, ROWS), params), :] = gathered[where, :]

    loop(slots, fetch)
    high, low = halves(table_rows[...].T)
    table = jnp.concatenate([high, low], axis=0)

    chunk = 512
    for at in range(0, pixels, chunk):
        cols = slice(at, at + chunk)
        live = masked[:, cols]
        weights = spread[:, cols]
        pulled = lax.dot_general(table, live, NN, preferred_element_type=f32)
        pulled = pulled[:LANES] + pulled[LANES:]
        projected = rows_sum(weights * pulled)
        squared = projected * projected
        for lane in range(0, chunk, LANES):
            curvature = curvature + squared[:, lane : lane + LANES]
        high, low = halves(weights * projected)
        both = jnp.concatenate([high, low], axis=0)
        back = lax.dot_general(live, both, NT, preferred_element_type=f32)
        back = back[:, :LANES] + back[:, LANES:]
        if at == 0:
            products[...] = back
        else:
            products[...] += back

    half = LANES // 2
    lane_of = lax.broadcasted_iota(jnp.int32, (1, LANES), 1)
    start = sums[0:1, :]
    start = start + pltpu.roll(start, half, 1)
    curvature = curvature + pltpu.roll(curvature, half, 1)
    scalars = jnp.where(lane_of < half, start, curvature)

    def give(owner):
        for c in range(cams):
            base = (owner * cams + c) * back_rows
            for s in range(slot_count):
                if c * part < params:
                    at = (owner * slot_count + s) * ROWS + c * part
                    value = products[pl.ds(at, part), :]
                else:
                    value = jnp.zeros((part, LANES), f32)
                out[pl.ds(base + s * part, part), :] = value
            out[pl.ds(base + slot_count * part, 1), :] = scalars

    loop(owners, give)


def image_kernel(sizes, received, frames, mine, send_list, scalars, blocks, image):
    owners, cams, slot_count, held, params, part, block_rows, back_rows, step = sizes
    piece = held * part
    image[...] = jnp.zeros_like(image)
    last = jnp.zeros((1, LANES), f32)

    def collect(owner, last):
        at = owner * cams * back_rows
        total = received[pl.ds(at, back_rows), :]
        for c in range(1, cams):
            total = total + received[pl.ds(at + c * back_rows, back_rows), :]
        for s in range(slot_count):
            listed = jnp.maximum(send_list[s, 0, owner], 0)
            where = pl.ds((listed // held) * piece + listed % held, part, stride=held)
            image[where, :] = image[where, :] + total[s * part : (s + 1) * part]
        return last + total[back_rows - 1 : back_rows]

    last = lax.fori_loop(0, owners, collect, last, unroll=owners <= 32)
    half = LANES // 2
    lane_of = lax.broadcasted_iota(jnp.int32, (1, LANES), 1)
    start = jnp.sum(jnp.where(lane_of < half, last, 0.0), axis=1, keepdims=True)
    curvature = jnp.sum(jnp.where(lane_of < half, 0.0, last), axis=1, keepdims=True)
    length = start / curvature
    norms = jnp.zeros((1, LANES), f32)
    for c in range(cams):
        rows = slice(c * piece, (c + 1) * piece)
        residual, precond, near = (
            mine[(3 * c + k) * piece : (3 * c + k + 1) * piece, :] for k in range(3)
        )
        value = image[rows, :] + near + frames[rows, :]
        image[rows, :] = value
        left = residual - length * value
        norms = norms + rows_sum(left * (precond * left))
    scalars[0:1, :] = jnp.broadcast_to(start, (1, LANES))
    scalars[1:2, :] = jnp.broadcast_to(length, (1, LANES))

    def tell(owner):
        for c in range(cams):
            base = (owner * cams + c) * (piece + 1)
            blocks[pl.ds(base, 1), :] = norms
            blocks[pl.ds(base + 1, piece), :] = image[c * piece : (c + 1) * piece, :]

    loop(owners, tell)


def update_kernel(
    sizes, arrived, scalars, iterate, residual, direction, precond,
    new_iterate, new_residual, new_direction,
):
    owners, cams, slot_count, held, params, part, block_rows, back_rows, step = sizes
    piece = held * part
    rows = iterate.shape[0]
    own = lax.axis_index("nodes")
    norms = arrived[0:1, :]
    for device in range(1, owners * cams):
        norms = norms + arrived[device * (piece + 1) : device * (piece + 1) + 1, :]
    start, length = scalars[0:1, :], scalars[1:2, :]
    ratio = jnp.sum(norms, axis=1, keepdims=True) / start
    for c in range(rows // piece):
        here = slice(c * piece, (c + 1) * piece)
        image = arrived[pl.ds((own * cams + c) * (piece + 1) + 1, piece), :]
        value = direction[here, :]
        left = residual[here, :] - length * image
        new_iterate[here, :] = iterate[here, :] + length * value
        new_residual[here, :] = left
        new_direction[here, :] = precond[here, :] * left + ratio * value


def flat(value):
    return jnp.transpose(value, (1, 0, 2)).reshape(-1, value.shape[2])


def exchange(blocks, axes):
    rows, lanes = blocks.shape
    peers = lax.axis_size(axes)
    blocks = blocks.reshape(peers, rows // peers, 1, lanes)
    blocks = lax.all_to_all(blocks, axes, split_axis=0, concat_axis=0, tiled=True)
    return blocks.reshape(rows, lanes)


def on_device(iterate, residual, direction, precond, send_list, grads, node_refs, skin, rigid_nbr):
    held, params, lanes = direction.shape
    pixels = grads.shape[1]
    owners = lax.axis_size("nodes")
    cams = lax.axis_size("cams")
    devices = owners * cams
    slot_count = send_list.shape[2]
    slots = owners * slot_count
    asked = limit(slots, pixels)
    rows = held * params
    extra = -(-slots // lanes)
    block_rows = rows + extra
    part = next(n for n in range(1, params + 1) if params % n == 0 and n * cams >= params)
    piece = held * part
    back_rows = slot_count * part + 1
    sizes = (
        owners, cams, slot_count, held, params, part, block_rows, back_rows, devices // FRAMES
    )

    def array(count):
        return jax.ShapeDtypeStruct((count, lanes), f32)

    iterate, residual, direction, precond = (flat(v) for v in (iterate, residual, direction, precond))
    nbr = flat(rigid_nbr)
    by_slot = jnp.transpose(send_list, (2, 0, 1))
    listed = by_slot.reshape(-1).astype(f32)
    list_rows = jnp.pad(listed, (0, extra * lanes - slots)).reshape(extra, lanes)

    packed = pl.pallas_call(
        functools.partial(pack_kernel, block_rows),
        out_shape=array(devices * block_rows),
        in_specs=[VMEM] * 2,
        out_specs=VMEM,
        scratch_shapes=[pltpu.VMEM((-(-block_rows // 8) * 8, lanes), f32)],
        compiler_params=asked,
        name="pack",
    )(direction, list_rows)
    packed, nbr, node_refs = lax.optimization_barrier((packed, nbr, node_refs))
    gathered = exchange(packed, AXES)

    joined = jnp.concatenate([direction, residual, precond, nbr.astype(f32)], axis=0)
    stack, sums = pl.pallas_call(
        functools.partial(near_kernel, held, piece, rows),
        out_shape=(array(3 * cams * piece), array(8)),
        in_specs=[VMEM],
        out_specs=(VMEM,) * 2,
        compiler_params=asked,
        name="near",
    )(joined)
    spread, masked = pl.pallas_call(
        masks_kernel,
        out_shape=(
            jax.ShapeDtypeStruct((lanes, pixels), f32),
            jax.ShapeDtypeStruct((slots * ROWS, pixels), bf16),
        ),
        in_specs=[VMEM] * 3,
        out_specs=(VMEM,) * 2,
        scratch_shapes=[pltpu.VMEM((ROWS, pixels), f32)],
        compiler_params=asked,
        name="masks",
    )(grads, node_refs, skin)
    mine, sums = lax.optimization_barrier((exchange(stack, "cams"), sums))

    products, frames = pl.pallas_call(
        functools.partial(data_kernel, sizes),
        out_shape=(array(devices * back_rows), array(cams * piece)),
        in_specs=[VMEM] * 4,
        out_specs=(VMEM, VMEM),
        scratch_shapes=[
            pltpu.SMEM((owners * extra, lanes), f32),
            pltpu.VMEM((owners * extra, lanes), f32),
            pltpu.VMEM((slots * ROWS, lanes), f32),
            pltpu.VMEM((slots * ROWS, lanes), f32),
            pltpu.SemaphoreType.DMA,
        ],
        compiler_params=asked,
        name="data_products",
    )(gathered, sums, spread, masked)
    received = exchange(products, AXES)

    scalars, blocks = pl.pallas_call(
        functools.partial(image_kernel, sizes),
        out_shape=(array(8), array(devices * (piece + 1))),
        in_specs=[VMEM] * 3 + [SMEM],
        out_specs=(VMEM,) * 2,
        scratch_shapes=[pltpu.VMEM((cams * piece, lanes), f32)],
        compiler_params=asked,
        name="image",
    )(received, frames, mine, by_slot)
    arrived = exchange(blocks, AXES)
    outs = pl.pallas_call(
        functools.partial(update_kernel, sizes),
        out_shape=(array(rows),) * 3,
        in_specs=[VMEM] * 6,
        out_specs=(VMEM,) * 3,
        compiler_params=asked,
        name="update",
    )(arrived, scalars, iterate, residual, direction, precond)
    return tuple(jnp.transpose(v.reshape(params, held, lanes), (1, 0, 2)) for v in outs)


def solution(mesh):
    split = P(AXES, None, None)
    pixel_split = P(None, AXES)
    in_specs = (split,) * 4 + (P("nodes", None, None),) + (pixel_split,) * 3 + (split,)
    return jax.shard_map(
        on_device, mesh=mesh, in_specs=in_specs, out_specs=(split,) * 3, check_vma=False
    )
```

```python
import functools

import jax
import jax.numpy as jnp
from jax import lax
from jax.experimental import pallas as pl
from jax.experimental.pallas import tpu as pltpu
from jax.sharding import PartitionSpec as P

FRAMES = 8
AXES = ("nodes", "cams")
temporal_weight = 0.5
rigid_weight = 0.1
NN = (((1,), (0,)), ((), ()))
NT = (((1,), (1,)), ((), ()))
LANES = 128
ROWS = 16
f32 = jnp.float32
bf16 = jnp.bfloat16

VMEM = pl.BlockSpec(memory_space=pltpu.VMEM)
SMEM = pl.BlockSpec(memory_space=pltpu.SMEM)


def limit(slots, pixels):
    need = 8 * 2**20 + slots * ROWS * pixels * 3
    return pltpu.CompilerParams(vmem_limit_bytes=min(need, 56 * 2**20))


def halves(value):
    high = value.astype(bf16)
    low = (value - high.astype(f32)).astype(bf16)
    return high, low


def rows_sum(value):
    return jnp.sum(value, axis=0, keepdims=True)


def loop(count, body):
    lax.fori_loop(0, count, lambda i, carry: (body(i), carry)[1], 0, unroll=count <= 32)


def pack_kernel(block_rows, block, out):
    value = block[0:block_rows, :]

    def write(device):
        out[pl.ds(device * block_rows, block_rows), :] = value

    loop(out.shape[0] // block_rows, write)


def near_kernel(held, piece, rows, joined, sums_out, *pieces):
    *pieces, near_rows = pieces
    value = joined[0:rows, :]
    left = joined[rows : 2 * rows, :]
    scale = joined[2 * rows : 3 * rows, :]
    high, low = halves(value)
    stack = jnp.concatenate([high.astype(f32), low.astype(f32), jnp.ones((16, LANES), f32)], axis=0)
    stack = stack.astype(bf16)
    node_rows = lax.broadcasted_iota(jnp.int32, (LANES, LANES), 0).astype(f32)
    patch_row = lax.broadcasted_iota(jnp.int32, (rows, LANES), 0) % held
    edges = (joined.shape[0] - 3 * rows) // held
    rigid = jnp.zeros_like(value)
    for q in range(held):
        hits = jnp.zeros((LANES, LANES), f32)
        for r in range(edges):
            at = 3 * rows + r * held + q
            hits = hits + jnp.where(node_rows == joined[at : at + 1, :], 1.0, 0.0)
        hits = hits.astype(bf16)
        pulled = lax.dot_general(stack, hits, NN, preferred_element_type=f32)
        pushed = lax.dot_general(stack, hits, NT, preferred_element_type=f32)
        degree = pushed[2 * rows : 2 * rows + 1]
        both = pulled + pushed
        part = value * (degree + float(edges)) - (both[:rows] + both[rows : 2 * rows])
        rigid = jnp.where(patch_row == q, part, rigid)
    near = rigid_weight * rigid + (2.0 * temporal_weight) * value
    near_rows[...] = near
    cams = len(pieces)
    cam = lax.axis_index("cams")
    for distance, out in enumerate(pieces):
        target = lax.rem(cam + distance, cams) * piece
        offset = jnp.minimum(target, rows - piece)
        out[0:piece, :] = joined[pl.ds(rows + offset, piece), :]
        out[piece : 2 * piece, :] = joined[pl.ds(2 * rows + offset, piece), :]
        part = near_rows[pl.ds(offset, piece), :]
        out[2 * piece : 3 * piece, :] = part
        if cams * piece > rows:

            @pl.when(target >= rows)
            def _():
                out[...] = jnp.zeros_like(out)

    sums_out[0:1, :] = rows_sum(left * (scale * left))
    sums_out[1:2, :] = rows_sum(value * near)


def masks_kernel(grads, node_refs, skin, spread_out, masked, grads_pad):
    params, pixels = grads.shape
    slots = masked.shape[0] // ROWS
    chunk = 512
    grads_pad[...] = jnp.zeros_like(grads_pad)
    grads_pad[0:params, :] = grads[...].astype(f32)
    node_rows = lax.broadcasted_iota(jnp.int32, (LANES, chunk), 0)
    for at in range(0, pixels, chunk):
        cols = slice(at, at + chunk)
        refs = node_refs[:, cols]
        node = lax.bitwise_and(refs, LANES - 1)
        slot_of = lax.shift_right_logical(refs[0:1], 7)
        weights = skin[:, cols].astype(f32)
        grad16 = grads_pad[:, cols]
        spread = jnp.where(node_rows == node[0:1], weights[0:1], 0.0)
        for k in range(1, refs.shape[0]):
            spread = spread + jnp.where(node_rows == node[k : k + 1], weights[k : k + 1], 0.0)
        spread_out[:, cols] = spread

        def mask(slot):
            piece = jnp.where(slot_of == slot, grad16, 0.0).astype(bf16)
            masked[pl.ds(pl.multiple_of(slot * ROWS, ROWS), ROWS), cols] = piece

        loop(slots, mask)


def data_kernel(
    sizes, gathered, sums, spread, masked,
    out, frames_out, lists, list_rows, table_rows, products, sem,
):
    owners, cams, slot_count, held, params, part, block_rows, back_rows, step = sizes
    devices = owners * cams
    rows = held * params
    piece = held * part
    slots = owners * slot_count
    pixels = spread.shape[1]
    receiver = lax.axis_index("nodes")
    cam = lax.axis_index("cams")
    extra = block_rows - rows
    for owner in range(owners):
        at = owner * cams * block_rows + rows
        list_rows[owner * extra : (owner + 1) * extra, :] = gathered[at : at + extra, :]
    copy = pltpu.make_async_copy(list_rows, lists, sem)
    copy.start()
    table_rows[...] = jnp.zeros_like(table_rows)
    curvature = sums[1:2, :]
    inside = cam * piece < rows
    offset = jnp.minimum(cam * piece, rows - piece)
    for c in range(cams):
        device = receiver * cams + c
        value = gathered[pl.ds(device * block_rows + offset, piece), :]
        before = gathered[pl.ds(jnp.maximum(device - step, 0) * block_rows + offset, piece), :]
        after = gathered[
            pl.ds(jnp.minimum(device + step, devices - 1) * block_rows + offset, piece), :
        ]
        earlier = jnp.where(jnp.logical_and(inside, device >= step), before, 0.0)
        following = jnp.where(jnp.logical_and(inside, device + step < devices), after, 0.0)
        frames = -temporal_weight * (earlier + following)
        frames_out[c * piece : (c + 1) * piece, :] = frames
        curvature = curvature + rows_sum(value * frames)
    copy.wait()

    def patch_of(slot):
        entry = receiver * slot_count + slot % slot_count
        row = (slot // slot_count) * extra + entry // LANES
        return lists[row, entry % LANES].astype(jnp.int32)

    def fetch(slot):
        listed = jnp.maximum(patch_of(slot), 0)
        device = (slot // slot_count) * cams + listed // held
        where = pl.ds(device * block_rows + listed % held, params, stride=held)
        table_rows[pl.ds(pl.multiple_of(slot * ROWS, ROWS), params), :] = gathered[where, :]

    loop(slots, fetch)
    high, low = halves(table_rows[...].T)
    table = jnp.concatenate([high, low], axis=0)

    chunk = 512
    for at in range(0, pixels, chunk):
        cols = slice(at, at + chunk)
        live = masked[:, cols]
        weights = spread[:, cols]
        pulled = lax.dot_general(table, live, NN, preferred_element_type=f32)
        pulled = pulled[:LANES] + pulled[LANES:]
        projected = rows_sum(weights * pulled)
        squared = projected * projected
        for lane in range(0, chunk, LANES):
            curvature = curvature + squared[:, lane : lane + LANES]
        high, low = halves(weights * projected)
        both = jnp.concatenate([high, low], axis=0)
        back = lax.dot_general(live, both, NT, preferred_element_type=f32)
        back = back[:, :LANES] + back[:, LANES:]
        if at == 0:
            products[...] = back
        else:
            products[...] += back

    half = LANES // 2
    lane_of = lax.broadcasted_iota(jnp.int32, (1, LANES), 1)
    start = sums[0:1, :]
    start = start + pltpu.roll(start, half, 1)
    curvature = curvature + pltpu.roll(curvature, half, 1)
    scalars = jnp.where(lane_of < half, start, curvature)

    def give(owner):
        for c in range(cams):
            base = (owner * cams + c) * back_rows
            for s in range(slot_count):
                if c * part < params:
                    at = (owner * slot_count + s) * ROWS + c * part
                    value = products[pl.ds(at, part), :]
                else:
                    value = jnp.zeros((part, LANES), f32)
                out[pl.ds(base + s * part, part), :] = value
            out[pl.ds(base + slot_count * part, 1), :] = scalars

    loop(owners, give)


def image_kernel(sizes, send_list, received, frames, *refs):
    owners, cams, slot_count, held, params, part, block_rows, back_rows, step = sizes
    mine, (scalars, blocks, image) = refs[:cams], refs[cams:]
    cam = lax.axis_index("cams")
    piece = held * part
    image[...] = jnp.zeros_like(image)
    last = jnp.zeros((1, LANES), f32)

    def collect(owner, last):
        at = owner * cams * back_rows
        total = received[pl.ds(at, back_rows), :]
        for c in range(1, cams):
            total = total + received[pl.ds(at + c * back_rows, back_rows), :]
        for s in range(slot_count):
            listed = jnp.maximum(send_list[s, 0, owner], 0)
            where = pl.ds((listed // held) * piece + listed % held, part, stride=held)
            image[where, :] = image[where, :] + total[s * part : (s + 1) * part]
        return last + total[back_rows - 1 : back_rows]

    last = lax.fori_loop(0, owners, collect, last, unroll=owners <= 32)
    half = LANES // 2
    lane_of = lax.broadcasted_iota(jnp.int32, (1, LANES), 1)
    start = jnp.sum(jnp.where(lane_of < half, last, 0.0), axis=1, keepdims=True)
    curvature = jnp.sum(jnp.where(lane_of < half, 0.0, last), axis=1, keepdims=True)
    length = start / curvature
    norms = jnp.zeros((1, LANES), f32)
    for distance, block in enumerate(mine):
        rows = pl.ds(lax.rem(cam + cams - distance, cams) * piece, piece)
        residual, precond, near = (block[k * piece : (k + 1) * piece, :] for k in range(3))
        value = image[rows, :] + near + frames[rows, :]
        image[rows, :] = value
        left = residual - length * value
        norms = norms + rows_sum(left * (precond * left))
    scalars[0:1, :] = jnp.broadcast_to(start, (1, LANES))
    scalars[1:2, :] = jnp.broadcast_to(length, (1, LANES))

    def tell(owner):
        for c in range(cams):
            base = (owner * cams + c) * (piece + 1)
            blocks[pl.ds(base, 1), :] = norms
            blocks[pl.ds(base + 1, piece), :] = image[c * piece : (c + 1) * piece, :]

    loop(owners, tell)


def update_kernel(
    sizes, arrived, scalars, iterate, residual, direction, precond,
    new_iterate, new_residual, new_direction,
):
    owners, cams, slot_count, held, params, part, block_rows, back_rows, step = sizes
    piece = held * part
    rows = iterate.shape[0]
    own = lax.axis_index("nodes")
    norms = arrived[0:1, :]
    for device in range(1, owners * cams):
        norms = norms + arrived[device * (piece + 1) : device * (piece + 1) + 1, :]
    start, length = scalars[0:1, :], scalars[1:2, :]
    ratio = jnp.sum(norms, axis=1, keepdims=True) / start
    for c in range(rows // piece):
        here = slice(c * piece, (c + 1) * piece)
        image = arrived[pl.ds((own * cams + c) * (piece + 1) + 1, piece), :]
        value = direction[here, :]
        left = residual[here, :] - length * image
        new_iterate[here, :] = iterate[here, :] + length * value
        new_residual[here, :] = left
        new_direction[here, :] = precond[here, :] * left + ratio * value


def flat(value):
    return jnp.transpose(value, (1, 0, 2)).reshape(-1, value.shape[2])


def exchange(blocks, axes):
    rows, lanes = blocks.shape
    peers = lax.axis_size(axes)
    blocks = blocks.reshape(peers, rows // peers, 1, lanes)
    blocks = lax.all_to_all(blocks, axes, split_axis=0, concat_axis=0, tiled=True)
    return blocks.reshape(rows, lanes)


def on_device(iterate, residual, direction, precond, send_list, grads, node_refs, skin, rigid_nbr):
    held, params, lanes = direction.shape
    pixels = grads.shape[1]
    owners = lax.axis_size("nodes")
    cams = lax.axis_size("cams")
    devices = owners * cams
    slot_count = send_list.shape[2]
    slots = owners * slot_count
    asked = limit(slots, pixels)
    rows = held * params
    extra = -(-slots // lanes)
    block_rows = rows + extra
    part = next(n for n in range(1, params + 1) if params % n == 0 and n * cams >= params)
    piece = held * part
    back_rows = slot_count * part + 1
    sizes = (
        owners, cams, slot_count, held, params, part, block_rows, back_rows, devices // FRAMES
    )

    def array(count):
        return jax.ShapeDtypeStruct((count, lanes), f32)

    iterate, residual, direction, precond = (flat(v) for v in (iterate, residual, direction, precond))
    listed = send_list.reshape(-1).astype(f32)
    padded_rows = -(-block_rows // 8) * 8
    listed = jnp.pad(listed, (0, (padded_rows - rows) * lanes - slots)).reshape(-1, lanes)
    packed = pl.pallas_call(
        functools.partial(pack_kernel, block_rows),
        out_shape=array(devices * block_rows),
        in_specs=[VMEM],
        out_specs=VMEM,
        compiler_params=asked,
        name="pack",
    )(jnp.concatenate([direction, listed], axis=0))
    packed, rigid_nbr, node_refs = lax.optimization_barrier((packed, rigid_nbr, node_refs))
    gathered = exchange(packed, AXES)

    nbr = flat(rigid_nbr)
    by_slot = jnp.transpose(send_list, (2, 0, 1))
    joined = jnp.concatenate([direction, residual, precond, nbr.astype(f32)], axis=0)
    sums, *pieces = pl.pallas_call(
        functools.partial(near_kernel, held, piece, rows),
        out_shape=(array(8),) + (array(3 * piece),) * cams,
        in_specs=[VMEM],
        out_specs=(VMEM,) * (1 + cams),
        scratch_shapes=[pltpu.VMEM((rows, lanes), f32)],
        compiler_params=asked,
        name="near",
    )(joined)
    spread, masked = pl.pallas_call(
        masks_kernel,
        out_shape=(
            jax.ShapeDtypeStruct((lanes, pixels), f32),
            jax.ShapeDtypeStruct((slots * ROWS, pixels), bf16),
        ),
        in_specs=[VMEM] * 3,
        out_specs=(VMEM,) * 2,
        scratch_shapes=[pltpu.VMEM((ROWS, pixels), f32)],
        compiler_params=asked,
        name="masks",
    )(grads, node_refs, skin)
    products, frames = pl.pallas_call(
        functools.partial(data_kernel, sizes),
        out_shape=(array(devices * back_rows), array(cams * piece)),
        in_specs=[VMEM] * 4,
        out_specs=(VMEM, VMEM),
        scratch_shapes=[
            pltpu.SMEM((owners * extra, lanes), f32),
            pltpu.VMEM((owners * extra, lanes), f32),
            pltpu.VMEM((slots * ROWS, lanes), f32),
            pltpu.VMEM((slots * ROWS, lanes), f32),
            pltpu.SemaphoreType.DMA,
        ],
        compiler_params=asked,
        name="data_products",
    )(gathered, sums, spread, masked)
    received = exchange(products, AXES)
    frames, *pieces = lax.optimization_barrier((frames, *pieces))
    mine = [pieces[0]]
    for distance in range(1, cams):
        pairs = [(c, (c + distance) % cams) for c in range(cams)]
        mine.append(lax.ppermute(pieces[distance], "cams", pairs))

    scalars, blocks = pl.pallas_call(
        functools.partial(image_kernel, sizes),
        out_shape=(array(8), array(devices * (piece + 1))),
        in_specs=[SMEM] + [VMEM] * (2 + cams),
        out_specs=(VMEM,) * 2,
        scratch_shapes=[pltpu.VMEM((cams * piece, lanes), f32)],
        compiler_params=asked,
        name="image",
    )(by_slot, received, frames, *mine)
    arrived = exchange(blocks, AXES)
    outs = pl.pallas_call(
        functools.partial(update_kernel, sizes),
        out_shape=(array(rows),) * 3,
        in_specs=[VMEM] * 6,
        out_specs=(VMEM,) * 3,
        compiler_params=asked,
        name="update",
    )(arrived, scalars, iterate, residual, direction, precond)
    return tuple(jnp.transpose(v.reshape(params, held, lanes), (1, 0, 2)) for v in outs)


def solution(mesh):
    split = P(AXES, None, None)
    pixel_split = P(None, AXES)
    in_specs = (split,) * 4 + (P("nodes", None, None),) + (pixel_split,) * 3 + (split,)
    return jax.shard_map(
        on_device, mesh=mesh, in_specs=in_specs, out_specs=(split,) * 3, check_vma=False
    )
```

```python
import functools

import jax
import jax.numpy as jnp
from jax import lax
from jax.experimental import pallas as pl
from jax.experimental.pallas import tpu as pltpu
from jax.sharding import PartitionSpec as P

FRAMES = 8
AXES = ("nodes", "cams")
temporal_weight = 0.5
rigid_weight = 0.1
NN = (((1,), (0,)), ((), ()))
NT = (((1,), (1,)), ((), ()))
LANES = 128
ROWS = 16
f32 = jnp.float32
bf16 = jnp.bfloat16

VMEM = pl.BlockSpec(memory_space=pltpu.VMEM)
SMEM = pl.BlockSpec(memory_space=pltpu.SMEM)


def limit(slots, pixels):
    need = 8 * 2**20 + slots * ROWS * pixels * 3
    return pltpu.CompilerParams(vmem_limit_bytes=min(need, 56 * 2**20))


def halves(value):
    high = value.astype(bf16)
    low = (value - high.astype(f32)).astype(bf16)
    return high, low


def rows_sum(value):
    return jnp.sum(value, axis=0, keepdims=True)


def loop(count, body):
    lax.fori_loop(0, count, lambda i, carry: (body(i), carry)[1], 0, unroll=count <= 32)


def select_kernel(sizes, send_list, *refs):
    owners, cams, slot_count, held, params, part, back_rows = sizes
    rows = held * params
    blocks, (out, patches) = refs[:cams], refs[cams:]
    cam = lax.axis_index("cams")
    for distance, block in enumerate(blocks):
        at = lax.rem(cam + cams - distance, cams) * rows
        patches[pl.ds(pl.multiple_of(at, 8), rows), :] = block[...]

    def pick(owner):
        for s in range(slot_count):
            listed = send_list[s, 0, owner]
            where = pl.ds((listed // held) * rows + listed % held, params, stride=held)
            out[pl.ds((owner * slot_count + s) * params, params), :] = patches[where, :]

    loop(owners, pick)


def near_kernel(held, piece, rows, joined, earlier, following, sums_out, *pieces):
    *pieces, near_rows = pieces
    value = joined[0:rows, :]
    left = joined[rows : 2 * rows, :]
    scale = joined[2 * rows : 3 * rows, :]
    high, low = halves(value)
    stack = jnp.concatenate([high.astype(f32), low.astype(f32), jnp.ones((16, LANES), f32)], axis=0)
    stack = stack.astype(bf16)
    node_rows = lax.broadcasted_iota(jnp.int32, (LANES, LANES), 0).astype(f32)
    patch_row = lax.broadcasted_iota(jnp.int32, (rows, LANES), 0) % held
    edges = (joined.shape[0] - 3 * rows) // held
    rigid = jnp.zeros_like(value)
    for q in range(held):
        hits = jnp.zeros((LANES, LANES), f32)
        for r in range(edges):
            at = 3 * rows + r * held + q
            hits = hits + jnp.where(node_rows == joined[at : at + 1, :], 1.0, 0.0)
        hits = hits.astype(bf16)
        pulled = lax.dot_general(stack, hits, NN, preferred_element_type=f32)
        pushed = lax.dot_general(stack, hits, NT, preferred_element_type=f32)
        degree = pushed[2 * rows : 2 * rows + 1]
        both = pulled + pushed
        part = value * (degree + float(edges)) - (both[:rows] + both[rows : 2 * rows])
        rigid = jnp.where(patch_row == q, part, rigid)
    near = rigid_weight * rigid
    near = near + temporal_weight * (2.0 * value - earlier[...] - following[...])
    near_rows[...] = near
    cams = len(pieces)
    cam = lax.axis_index("cams")
    for distance, out in enumerate(pieces):
        target = lax.rem(cam + distance, cams) * piece
        offset = jnp.minimum(target, rows - piece)
        out[0:piece, :] = joined[pl.ds(rows + offset, piece), :]
        out[piece : 2 * piece, :] = joined[pl.ds(2 * rows + offset, piece), :]
        part = near_rows[pl.ds(offset, piece), :]
        out[2 * piece : 3 * piece, :] = part
        if cams * piece > rows:

            @pl.when(target >= rows)
            def _():
                out[...] = jnp.zeros_like(out)

    sums_out[0:1, :] = rows_sum(left * (scale * left))
    sums_out[1:2, :] = rows_sum(value * near)


def masks_kernel(grads, node_refs, skin, spread_out, masked, grads_pad):
    params, pixels = grads.shape
    slots = masked.shape[0] // ROWS
    chunk = 512
    grads_pad[...] = jnp.zeros_like(grads_pad)
    grads_pad[0:params, :] = grads[...].astype(f32)
    node_rows = lax.broadcasted_iota(jnp.int32, (LANES, chunk), 0)
    for at in range(0, pixels, chunk):
        cols = slice(at, at + chunk)
        refs = node_refs[:, cols]
        node = lax.bitwise_and(refs, LANES - 1)
        slot_of = lax.shift_right_logical(refs[0:1], 7)
        weights = skin[:, cols].astype(f32)
        grad16 = grads_pad[:, cols]
        spread = jnp.where(node_rows == node[0:1], weights[0:1], 0.0)
        for k in range(1, refs.shape[0]):
            spread = spread + jnp.where(node_rows == node[k : k + 1], weights[k : k + 1], 0.0)
        spread_out[:, cols] = spread

        def mask(slot):
            piece = jnp.where(slot_of == slot, grad16, 0.0).astype(bf16)
            masked[pl.ds(pl.multiple_of(slot * ROWS, ROWS), ROWS), cols] = piece

        loop(slots, mask)


def data_kernel(sizes, arrived, sums, spread, masked, out, table_rows, products):
    owners, cams, slot_count, held, params, part, back_rows = sizes
    slots = owners * slot_count
    pixels = spread.shape[1]
    curvature = sums[1:2, :]
    filler = jnp.zeros((ROWS - params, LANES), f32)

    def fetch(slot):
        at = pl.multiple_of(slot * ROWS, ROWS)
        table_rows[pl.ds(at, params), :] = arrived[pl.ds(slot * params, params), :]
        table_rows[pl.ds(at + params, ROWS - params), :] = filler

    loop(slots, fetch)
    high, low = halves(table_rows[...].T)
    table = jnp.concatenate([high, low], axis=0)

    chunk = 512
    for at in range(0, pixels, chunk):
        cols = slice(at, at + chunk)
        live = masked[:, cols]
        weights = spread[:, cols]
        pulled = lax.dot_general(table, live, NN, preferred_element_type=f32)
        pulled = pulled[:LANES] + pulled[LANES:]
        projected = rows_sum(weights * pulled)
        squared = projected * projected
        for lane in range(0, chunk, LANES):
            curvature = curvature + squared[:, lane : lane + LANES]
        high, low = halves(weights * projected)
        both = jnp.concatenate([high, low], axis=0)
        back = lax.dot_general(live, both, NT, preferred_element_type=f32)
        back = back[:, :LANES] + back[:, LANES:]
        if at == 0:
            products[...] = back
        else:
            products[...] += back

    half = LANES // 2
    lane_of = lax.broadcasted_iota(jnp.int32, (1, LANES), 1)
    start = sums[0:1, :]
    start = start + pltpu.roll(start, half, 1)
    curvature = curvature + pltpu.roll(curvature, half, 1)
    scalars = jnp.where(lane_of < half, start, curvature)

    def give(owner):
        for c in range(cams):
            base = (owner * cams + c) * back_rows
            for s in range(slot_count):
                if c * part < params:
                    at = (owner * slot_count + s) * ROWS + c * part
                    value = products[pl.ds(at, part), :]
                else:
                    value = jnp.zeros((part, LANES), f32)
                out[pl.ds(base + s * part, part), :] = value
            out[pl.ds(base + slot_count * part, 1), :] = scalars

    loop(owners, give)


def image_kernel(sizes, send_list, received, *refs):
    owners, cams, slot_count, held, params, part, back_rows = sizes
    mine, (scalars, blocks, image) = refs[:cams], refs[cams:]
    cam = lax.axis_index("cams")
    piece = held * part
    image[...] = jnp.zeros_like(image)
    last = jnp.zeros((1, LANES), f32)

    def collect(owner, last):
        at = owner * cams * back_rows
        total = received[pl.ds(at, back_rows), :]
        for c in range(1, cams):
            total = total + received[pl.ds(at + c * back_rows, back_rows), :]
        for s in range(slot_count):
            listed = send_list[s, 0, owner]
            where = pl.ds((listed // held) * piece + listed % held, part, stride=held)
            image[where, :] = image[where, :] + total[s * part : (s + 1) * part]
        return last + total[back_rows - 1 : back_rows]

    last = lax.fori_loop(0, owners, collect, last, unroll=owners <= 32)
    half = LANES // 2
    lane_of = lax.broadcasted_iota(jnp.int32, (1, LANES), 1)
    start = jnp.sum(jnp.where(lane_of < half, last, 0.0), axis=1, keepdims=True)
    curvature = jnp.sum(jnp.where(lane_of < half, 0.0, last), axis=1, keepdims=True)
    length = start / curvature
    norms = jnp.zeros((1, LANES), f32)
    for distance, block in enumerate(mine):
        rows = pl.ds(lax.rem(cam + cams - distance, cams) * piece, piece)
        residual, precond, near = (block[k * piece : (k + 1) * piece, :] for k in range(3))
        value = image[rows, :] + near
        image[rows, :] = value
        left = residual - length * value
        norms = norms + rows_sum(left * (precond * left))
    scalars[0:1, :] = jnp.broadcast_to(start, (1, LANES))
    scalars[1:2, :] = jnp.broadcast_to(length, (1, LANES))

    def tell(owner):
        for c in range(cams):
            base = (owner * cams + c) * (piece + 1)
            blocks[pl.ds(base, 1), :] = norms
            blocks[pl.ds(base + 1, piece), :] = image[c * piece : (c + 1) * piece, :]

    loop(owners, tell)


def update_kernel(
    sizes, arrived, scalars, iterate, residual, direction, precond,
    new_iterate, new_residual, new_direction,
):
    owners, cams, slot_count, held, params, part, back_rows = sizes
    piece = held * part
    rows = iterate.shape[0]
    own = lax.axis_index("nodes")
    norms = arrived[0:1, :]
    for device in range(1, owners * cams):
        norms = norms + arrived[device * (piece + 1) : device * (piece + 1) + 1, :]
    start, length = scalars[0:1, :], scalars[1:2, :]
    ratio = jnp.sum(norms, axis=1, keepdims=True) / start
    for c in range(rows // piece):
        here = slice(c * piece, (c + 1) * piece)
        image = arrived[pl.ds((own * cams + c) * (piece + 1) + 1, piece), :]
        value = direction[here, :]
        left = residual[here, :] - length * image
        new_iterate[here, :] = iterate[here, :] + length * value
        new_residual[here, :] = left
        new_direction[here, :] = precond[here, :] * left + ratio * value


def flat(value):
    return jnp.transpose(value, (1, 0, 2)).reshape(-1, value.shape[2])


def turned(value, cams, distance):
    return lax.ppermute(value, "cams", [(c, (c + distance) % cams) for c in range(cams)])


def shifted(value, by, devices):
    pairs = [(i, i + by) for i in range(devices) if 0 <= i + by < devices]
    return lax.ppermute(value, AXES, pairs)


def exchange(blocks, axes):
    rows, lanes = blocks.shape
    peers = lax.axis_size(axes)
    blocks = blocks.reshape(peers, rows // peers, 1, lanes)
    blocks = lax.all_to_all(blocks, axes, split_axis=0, concat_axis=0, tiled=True)
    return blocks.reshape(rows, lanes)


def on_device(iterate, residual, direction, precond, send_list, grads, node_refs, skin, rigid_nbr):
    held, params, lanes = direction.shape
    pixels = grads.shape[1]
    owners = lax.axis_size("nodes")
    cams = lax.axis_size("cams")
    devices = owners * cams
    slot_count = send_list.shape[2]
    slots = owners * slot_count
    asked = limit(slots, pixels)
    rows = held * params
    part = next(n for n in range(1, params + 1) if params % n == 0 and n * cams >= params)
    piece = held * part
    back_rows = slot_count * part + 1
    sizes = (owners, cams, slot_count, held, params, part, back_rows)

    def array(count):
        return jax.ShapeDtypeStruct((count, lanes), f32)

    iterate, residual, direction, precond = (flat(v) for v in (iterate, residual, direction, precond))
    by_slot = jnp.maximum(jnp.transpose(send_list, (2, 0, 1)), 0)
    owned = [direction] + [turned(direction, cams, distance) for distance in range(1, cams)]
    selected = pl.pallas_call(
        functools.partial(select_kernel, sizes),
        out_shape=array(slots * params),
        in_specs=[SMEM] + [VMEM] * cams,
        out_specs=VMEM,
        scratch_shapes=[pltpu.VMEM((cams * rows, lanes), f32)],
        compiler_params=asked,
        name="select",
    )(by_slot, *owned)
    selected, rigid_nbr, direction = lax.optimization_barrier((selected, rigid_nbr, direction))
    arrived = exchange(selected, "nodes")

    earlier = shifted(direction, devices // FRAMES, devices)
    following = shifted(direction, -(devices // FRAMES), devices)
    nbr = flat(rigid_nbr)
    joined = jnp.concatenate([direction, residual, precond, nbr.astype(f32)], axis=0)
    sums, *pieces = pl.pallas_call(
        functools.partial(near_kernel, held, piece, rows),
        out_shape=(array(8),) + (array(3 * piece),) * cams,
        in_specs=[VMEM] * 3,
        out_specs=(VMEM,) * (1 + cams),
        scratch_shapes=[pltpu.VMEM((rows, lanes), f32)],
        compiler_params=asked,
        name="near",
    )(joined, earlier, following)
    spread, masked = pl.pallas_call(
        masks_kernel,
        out_shape=(
            jax.ShapeDtypeStruct((lanes, pixels), f32),
            jax.ShapeDtypeStruct((slots * ROWS, pixels), bf16),
        ),
        in_specs=[VMEM] * 3,
        out_specs=(VMEM,) * 2,
        scratch_shapes=[pltpu.VMEM((ROWS, pixels), f32)],
        compiler_params=asked,
        name="masks",
    )(grads, node_refs, skin)
    products = pl.pallas_call(
        functools.partial(data_kernel, sizes),
        out_shape=array(devices * back_rows),
        in_specs=[VMEM] * 4,
        out_specs=VMEM,
        scratch_shapes=[
            pltpu.VMEM((slots * ROWS, lanes), f32),
            pltpu.VMEM((slots * ROWS, lanes), f32),
        ],
        compiler_params=asked,
        name="data_products",
    )(arrived, sums, spread, masked)
    products, *pieces = lax.optimization_barrier((products, *pieces))
    received = exchange(products, AXES)
    mine = pieces[:1] + [turned(pieces[distance], cams, distance) for distance in range(1, cams)]

    scalars, blocks = pl.pallas_call(
        functools.partial(image_kernel, sizes),
        out_shape=(array(8), array(devices * (piece + 1))),
        in_specs=[SMEM] + [VMEM] * (1 + cams),
        out_specs=(VMEM,) * 2,
        scratch_shapes=[pltpu.VMEM((cams * piece, lanes), f32)],
        compiler_params=asked,
        name="image",
    )(by_slot, received, *mine)
    arrived = exchange(blocks, AXES)
    outs = pl.pallas_call(
        functools.partial(update_kernel, sizes),
        out_shape=(array(rows),) * 3,
        in_specs=[VMEM] * 6,
        out_specs=(VMEM,) * 3,
        compiler_params=asked,
        name="update",
    )(arrived, scalars, iterate, residual, direction, precond)
    return tuple(jnp.transpose(v.reshape(params, held, lanes), (1, 0, 2)) for v in outs)


def solution(mesh):
    split = P(AXES, None, None)
    pixel_split = P(None, AXES)
    in_specs = (split,) * 4 + (P("nodes", None, None),) + (pixel_split,) * 3 + (split,)
    return jax.shard_map(
        on_device, mesh=mesh, in_specs=in_specs, out_specs=(split,) * 3, check_vma=False
    )
```

```python
import functools

import jax
import jax.numpy as jnp
from jax import lax
from jax.experimental import pallas as pl
from jax.experimental.pallas import tpu as pltpu
from jax.sharding import PartitionSpec as P

FRAMES = 8
AXES = ("nodes", "cams")
temporal_weight = 0.5
rigid_weight = 0.1
NN = (((1,), (0,)), ((), ()))
NT = (((1,), (1,)), ((), ()))
LANES = 128
ROWS = 16
f32 = jnp.float32
bf16 = jnp.bfloat16

VMEM = pl.BlockSpec(memory_space=pltpu.VMEM)
SMEM = pl.BlockSpec(memory_space=pltpu.SMEM)


def limit(slots, pixels):
    need = 8 * 2**20 + slots * ROWS * pixels * 3
    return pltpu.CompilerParams(vmem_limit_bytes=min(need, 56 * 2**20))


def halves(value):
    high = value.astype(bf16)
    low = (value - high.astype(f32)).astype(bf16)
    return high, low


def rows_sum(value):
    return jnp.sum(value, axis=0, keepdims=True)


def loop(count, body):
    lax.fori_loop(0, count, lambda i, carry: (body(i), carry)[1], 0, unroll=count <= 32)


def select_kernel(sizes, send_list, *refs):
    owners, cams, slot_count, held, params, part, back_rows = sizes
    rows = held * params
    blocks, (out, patches) = refs[:cams], refs[cams:]
    cam = lax.axis_index("cams")
    for distance, block in enumerate(blocks):
        at = lax.rem(cam + cams - distance, cams) * rows
        patches[pl.ds(pl.multiple_of(at, 8), rows), :] = block[0:rows, :]

    def pick(owner):
        for s in range(slot_count):
            listed = send_list[s, 0, owner]
            where = pl.ds((listed // held) * rows + listed % held, params, stride=held)
            out[pl.ds((owner * slot_count + s) * params, params), :] = patches[where, :]

    loop(owners, pick)


def near_kernel(held, piece, rows, joined, earlier, following, sums_out, *pieces):
    *pieces, near_rows = pieces
    value = joined[0:rows, :]
    left = joined[rows : 2 * rows, :]
    scale = joined[2 * rows : 3 * rows, :]
    high, low = halves(value)
    stack = jnp.concatenate([high.astype(f32), low.astype(f32), jnp.ones((16, LANES), f32)], axis=0)
    stack = stack.astype(bf16)
    node_rows = lax.broadcasted_iota(jnp.int32, (LANES, LANES), 0).astype(f32)
    patch_row = lax.broadcasted_iota(jnp.int32, (rows, LANES), 0) % held
    edges = (joined.shape[0] - 3 * rows) // held
    rigid = jnp.zeros_like(value)
    for q in range(held):
        hits = jnp.zeros((LANES, LANES), f32)
        for r in range(edges):
            at = 3 * rows + r * held + q
            hits = hits + jnp.where(node_rows == joined[at : at + 1, :], 1.0, 0.0)
        hits = hits.astype(bf16)
        pulled = lax.dot_general(stack, hits, NN, preferred_element_type=f32)
        pushed = lax.dot_general(stack, hits, NT, preferred_element_type=f32)
        degree = pushed[2 * rows : 2 * rows + 1]
        both = pulled + pushed
        part = value * (degree + float(edges)) - (both[:rows] + both[rows : 2 * rows])
        rigid = jnp.where(patch_row == q, part, rigid)
    near = rigid_weight * rigid
    near = near + temporal_weight * (2.0 * value - earlier[...] - following[...])
    near_rows[...] = near
    cams = len(pieces)
    cam = lax.axis_index("cams")
    for distance, out in enumerate(pieces):
        target = lax.rem(cam + distance, cams) * piece
        offset = jnp.minimum(target, rows - piece)
        out[0:piece, :] = joined[pl.ds(rows + offset, piece), :]
        out[piece : 2 * piece, :] = joined[pl.ds(2 * rows + offset, piece), :]
        part = near_rows[pl.ds(offset, piece), :]
        out[2 * piece : 3 * piece, :] = part
        if cams * piece > rows:

            @pl.when(target >= rows)
            def _():
                out[...] = jnp.zeros_like(out)

    sums_out[0:1, :] = rows_sum(left * (scale * left))
    sums_out[1:2, :] = rows_sum(value * near)


def masks_kernel(grads, node_refs, skin, spread_out, masked, grads_pad):
    params, pixels = grads.shape
    slots = masked.shape[0] // ROWS
    chunk = 512
    grads_pad[...] = jnp.zeros_like(grads_pad)
    grads_pad[0:params, :] = grads[...].astype(f32)
    node_rows = lax.broadcasted_iota(jnp.int32, (LANES, chunk), 0)
    for at in range(0, pixels, chunk):
        cols = slice(at, at + chunk)
        refs = node_refs[:, cols]
        node = lax.bitwise_and(refs, LANES - 1)
        slot_of = lax.shift_right_logical(refs[0:1], 7)
        weights = skin[:, cols].astype(f32)
        grad16 = grads_pad[:, cols]
        spread = jnp.where(node_rows == node[0:1], weights[0:1], 0.0)
        for k in range(1, refs.shape[0]):
            spread = spread + jnp.where(node_rows == node[k : k + 1], weights[k : k + 1], 0.0)
        spread_out[:, cols] = spread

        def mask(slot):
            piece = jnp.where(slot_of == slot, grad16, 0.0).astype(bf16)
            masked[pl.ds(pl.multiple_of(slot * ROWS, ROWS), ROWS), cols] = piece

        loop(slots, mask)


def data_kernel(sizes, arrived, spread, masked, out, squares_out, table_rows, products):
    owners, cams, slot_count, held, params, part, back_rows = sizes
    slots = owners * slot_count
    pixels = spread.shape[1]
    squares = jnp.zeros((1, LANES), f32)
    filler = jnp.zeros((ROWS - params, LANES), f32)

    def fetch(slot):
        at = pl.multiple_of(slot * ROWS, ROWS)
        table_rows[pl.ds(at, params), :] = arrived[pl.ds(slot * params, params), :]
        table_rows[pl.ds(at + params, ROWS - params), :] = filler

    loop(slots, fetch)
    high, low = halves(table_rows[...].T)
    table = jnp.concatenate([high, low], axis=0)

    chunk = 512
    for at in range(0, pixels, chunk):
        cols = slice(at, at + chunk)
        live = masked[:, cols]
        weights = spread[:, cols]
        pulled = lax.dot_general(table, live, NN, preferred_element_type=f32)
        pulled = pulled[:LANES] + pulled[LANES:]
        projected = rows_sum(weights * pulled)
        squared = projected * projected
        for lane in range(0, chunk, LANES):
            squares = squares + squared[:, lane : lane + LANES]
        high, low = halves(weights * projected)
        both = jnp.concatenate([high, low], axis=0)
        back = lax.dot_general(live, both, NT, preferred_element_type=f32)
        back = back[:, :LANES] + back[:, LANES:]
        if at == 0:
            products[...] = back
        else:
            products[...] += back

    squares_out[0:1, :] = squares

    def give(owner):
        for c in range(cams):
            base = (owner * cams + c) * back_rows
            for s in range(slot_count):
                if c * part < params:
                    at = (owner * slot_count + s) * ROWS + c * part
                    value = products[pl.ds(at, part), :]
                else:
                    value = jnp.zeros((part, LANES), f32)
                out[pl.ds(base + s * part, part), :] = value

    loop(owners, give)


def image_kernel(sizes, send_list, received, sums, squares, *refs):
    owners, cams, slot_count, held, params, part, back_rows = sizes
    mine, (blocks, image) = refs[:cams], refs[cams:]
    cam = lax.axis_index("cams")
    piece = held * part
    image[...] = jnp.zeros_like(image)

    def collect(owner):
        at = owner * cams * back_rows
        total = received[pl.ds(at, back_rows), :]
        for c in range(1, cams):
            total = total + received[pl.ds(at + c * back_rows, back_rows), :]
        for s in range(slot_count):
            listed = send_list[s, 0, owner]
            where = pl.ds((listed // held) * piece + listed % held, part, stride=held)
            image[where, :] = image[where, :] + total[s * part : (s + 1) * part]

    loop(owners, collect)
    cross = jnp.zeros((1, LANES), f32)
    square = jnp.zeros((1, LANES), f32)
    for distance, block in enumerate(mine):
        rows = pl.ds(lax.rem(cam + cams - distance, cams) * piece, piece)
        residual, precond, near = (block[k * piece : (k + 1) * piece, :] for k in range(3))
        value = image[rows, :] + near
        image[rows, :] = value
        cross = cross + rows_sum(value * (precond * residual))
        square = square + rows_sum(value * (precond * value))
    partial = (sums[0:1, :], sums[1:2, :] + squares[0:1, :], cross, square)
    lane_of = lax.broadcasted_iota(jnp.int32, (1, LANES), 1)
    scalars = jnp.zeros((1, LANES), f32)
    for k, row in enumerate(partial):
        scalars = jnp.where(lane_of == k, jnp.sum(row, axis=1, keepdims=True), scalars)

    def tell(owner):
        for c in range(cams):
            base = (owner * cams + c) * (piece + 1)
            blocks[pl.ds(base, 1), :] = scalars
            blocks[pl.ds(base + 1, piece), :] = image[c * piece : (c + 1) * piece, :]

    loop(owners, tell)


def update_kernel(sizes, returned, iterate, joined, new_iterate, new_residual, new_direction):
    owners, cams, slot_count, held, params, part, back_rows = sizes
    piece = held * part
    rows = iterate.shape[0]
    own = lax.axis_index("nodes")
    scalars = returned[0:1, :]
    for device in range(1, owners * cams):
        scalars = scalars + returned[device * (piece + 1) : device * (piece + 1) + 1, :]
    lane_of = lax.broadcasted_iota(jnp.int32, (1, LANES), 1)
    start, curvature, cross, square = (
        jnp.sum(jnp.where(lane_of == k, scalars, 0.0), axis=1, keepdims=True) for k in range(4)
    )
    length = start / curvature
    norm = start - 2.0 * length * cross + length * length * square
    ratio = norm / start
    for c in range(rows // piece):
        at = c * piece
        here = slice(at, at + piece)
        image = returned[pl.ds((own * cams + c) * (piece + 1) + 1, piece), :]
        value = joined[at : at + piece, :]
        left = joined[rows + at : rows + at + piece, :] - length * image
        new_iterate[here, :] = iterate[here, :] + length * value
        new_residual[here, :] = left
        new_direction[here, :] = joined[2 * rows + at : 2 * rows + at + piece, :] * left + ratio * value


def flat(value):
    return jnp.transpose(value, (1, 0, 2)).reshape(-1, value.shape[2])


def turned(value, cams, distance):
    return lax.ppermute(value, "cams", [(c, (c + distance) % cams) for c in range(cams)])


def shifted(value, by, devices):
    pairs = [(i, i + by) for i in range(devices) if 0 <= i + by < devices]
    return lax.ppermute(value, AXES, pairs)


def exchange(blocks, axes):
    rows, lanes = blocks.shape
    peers = lax.axis_size(axes)
    blocks = blocks.reshape(peers, rows // peers, 1, lanes)
    blocks = lax.all_to_all(blocks, axes, split_axis=0, concat_axis=0, tiled=True)
    return blocks.reshape(rows, lanes)


def on_device(iterate, residual, direction, precond, send_list, grads, node_refs, skin, rigid_nbr):
    held, params, lanes = direction.shape
    pixels = grads.shape[1]
    owners = lax.axis_size("nodes")
    cams = lax.axis_size("cams")
    devices = owners * cams
    slot_count = send_list.shape[2]
    slots = owners * slot_count
    asked = limit(slots, pixels)
    rows = held * params
    part = next(n for n in range(1, params + 1) if params % n == 0 and n * cams >= params)
    piece = held * part
    back_rows = slot_count * part
    sizes = (owners, cams, slot_count, held, params, part, back_rows)

    def array(count):
        return jax.ShapeDtypeStruct((count, lanes), f32)

    iterate, residual, direction, precond = (flat(v) for v in (iterate, residual, direction, precond))
    by_slot = jnp.maximum(jnp.transpose(send_list, (2, 0, 1)), 0)
    nbr = flat(rigid_nbr).astype(f32)
    joined = jnp.concatenate([direction, residual, precond, nbr], axis=0)
    owned = [joined] + [turned(direction, cams, distance) for distance in range(1, cams)]
    selected = pl.pallas_call(
        functools.partial(select_kernel, sizes),
        out_shape=array(slots * params),
        in_specs=[SMEM] + [VMEM] * cams,
        out_specs=VMEM,
        scratch_shapes=[pltpu.VMEM((cams * rows, lanes), f32)],
        compiler_params=asked,
        name="select",
    )(by_slot, *owned)
    selected, node_refs = lax.optimization_barrier((selected, node_refs))
    arrived = exchange(selected, "nodes")
    spread, masked = pl.pallas_call(
        masks_kernel,
        out_shape=(
            jax.ShapeDtypeStruct((lanes, pixels), f32),
            jax.ShapeDtypeStruct((slots * ROWS, pixels), bf16),
        ),
        in_specs=[VMEM] * 3,
        out_specs=(VMEM,) * 2,
        scratch_shapes=[pltpu.VMEM((ROWS, pixels), f32)],
        compiler_params=asked,
        name="masks",
    )(grads, node_refs, skin)
    spread, direction = lax.optimization_barrier((spread, direction))
    earlier = shifted(direction, devices // FRAMES, devices)
    following = shifted(direction, -(devices // FRAMES), devices)
    sums, *pieces = pl.pallas_call(
        functools.partial(near_kernel, held, piece, rows),
        out_shape=(array(8),) + (array(3 * piece),) * cams,
        in_specs=[VMEM] * 3,
        out_specs=(VMEM,) * (1 + cams),
        scratch_shapes=[pltpu.VMEM((rows, lanes), f32)],
        compiler_params=asked,
        name="near",
    )(joined, earlier, following)

    products, squares = pl.pallas_call(
        functools.partial(data_kernel, sizes),
        out_shape=(array(devices * back_rows), array(8)),
        in_specs=[VMEM] * 3,
        out_specs=(VMEM,) * 2,
        scratch_shapes=[
            pltpu.VMEM((slots * ROWS, lanes), f32),
            pltpu.VMEM((slots * ROWS, lanes), f32),
        ],
        compiler_params=asked,
        name="data_products",
    )(arrived, spread, masked)
    products, *pieces = lax.optimization_barrier((products, *pieces))
    received = exchange(products, AXES)
    mine = pieces[:1] + [turned(pieces[distance], cams, distance) for distance in range(1, cams)]

    blocks = pl.pallas_call(
        functools.partial(image_kernel, sizes),
        out_shape=array(devices * (piece + 1)),
        in_specs=[SMEM] + [VMEM] * (3 + cams),
        out_specs=VMEM,
        scratch_shapes=[pltpu.VMEM((cams * piece, lanes), f32)],
        compiler_params=asked,
        name="image",
    )(by_slot, received, sums, squares, *mine)
    returned = exchange(blocks, AXES)
    outs = pl.pallas_call(
        functools.partial(update_kernel, sizes),
        out_shape=(array(rows),) * 3,
        in_specs=[VMEM] * 3,
        out_specs=(VMEM,) * 3,
        compiler_params=asked,
        name="update",
    )(returned, iterate, joined)
    return tuple(jnp.transpose(v.reshape(params, held, lanes), (1, 0, 2)) for v in outs)


def solution(mesh):
    split = P(AXES, None, None)
    pixel_split = P(None, AXES)
    in_specs = (split,) * 4 + (P("nodes", None, None),) + (pixel_split,) * 3 + (split,)
    return jax.shard_map(
        on_device, mesh=mesh, in_specs=in_specs, out_specs=(split,) * 3, check_vma=False
    )
```

```python
import functools

import jax
import jax.numpy as jnp
from jax import lax
from jax.experimental import pallas as pl
from jax.experimental.pallas import tpu as pltpu
from jax.sharding import PartitionSpec as P

FRAMES = 8
AXES = ("nodes", "cams")
temporal_weight = 0.5
rigid_weight = 0.1
NN = (((1,), (0,)), ((), ()))
NT = (((1,), (1,)), ((), ()))
LANES = 128
ROWS = 16
f32 = jnp.float32
bf16 = jnp.bfloat16

VMEM = pl.BlockSpec(memory_space=pltpu.VMEM)
SMEM = pl.BlockSpec(memory_space=pltpu.SMEM)


def limit(slots, pixels):
    need = 8 * 2**20 + slots * ROWS * pixels * 3
    return pltpu.CompilerParams(vmem_limit_bytes=min(need, 56 * 2**20))


def halves(value):
    high = value.astype(bf16)
    low = (value - high.astype(f32)).astype(bf16)
    return high, low


def rows_sum(value):
    return jnp.sum(value, axis=0, keepdims=True)


def loop(count, body):
    lax.fori_loop(0, count, lambda i, carry: (body(i), carry)[1], 0, unroll=count <= 32)


def position(c, part, half_pieces):
    return (c % 2) * half_pieces * part + (c // 2) * part


def pack_kernel(sizes, owners, cams, extra, source, out, halves_of, lists):
    rows, slot_count, piece, pieces, half_pieces = sizes
    half_rows = half_pieces * piece
    lists[...] = jnp.zeros_like(lists)
    for s in range(slot_count):
        row, lane = divmod(s * owners, LANES)
        moved = source[rows + s : rows + s + 1, :]
        if lane:
            moved = pltpu.roll(moved, lane, 1)
        lists[row : row + 1, :] = lists[row : row + 1, :] + moved
    size = half_rows + extra
    halves_of[...] = jnp.zeros_like(halves_of)
    for c in range(pieces):
        at = (c % 2) * size + (c // 2) * piece
        halves_of[at : at + piece, :] = source[c * piece : (c + 1) * piece, :]
    for parity in range(2):
        at = parity * size + half_rows
        halves_of[at : at + extra, :] = lists[0:extra, :]

    def write(owner):
        for c in range(cams):
            at = (c % 2) * size
            out[pl.ds((owner * cams + c) * size, size), :] = halves_of[at : at + size, :]

    loop(owners, write)


def near_kernel(held, piece, rows, joined, sums_out, *pieces):
    *pieces, near_rows = pieces
    value = joined[0:rows, :]
    left = joined[rows : 2 * rows, :]
    scale = joined[2 * rows : 3 * rows, :]
    high, low = halves(value)
    stack = jnp.concatenate([high.astype(f32), low.astype(f32), jnp.ones((16, LANES), f32)], axis=0)
    stack = stack.astype(bf16)
    node_rows = lax.broadcasted_iota(jnp.int32, (LANES, LANES), 0).astype(f32)
    patch_row = lax.broadcasted_iota(jnp.int32, (rows, LANES), 0) % held
    edges = (joined.shape[0] - 3 * rows) // held
    rigid = jnp.zeros_like(value)
    for q in range(held):
        hits = jnp.zeros((LANES, LANES), f32)
        for r in range(edges):
            at = 3 * rows + r * held + q
            hits = hits + jnp.where(node_rows == joined[at : at + 1, :], 1.0, 0.0)
        hits = hits.astype(bf16)
        pulled = lax.dot_general(stack, hits, NN, preferred_element_type=f32)
        pushed = lax.dot_general(stack, hits, NT, preferred_element_type=f32)
        degree = pushed[2 * rows : 2 * rows + 1]
        both = pulled + pushed
        part = value * (degree + float(edges)) - (both[:rows] + both[rows : 2 * rows])
        rigid = jnp.where(patch_row == q, part, rigid)
    near = rigid_weight * rigid + (2.0 * temporal_weight) * value
    near_rows[...] = near
    cams = len(pieces)
    cam = lax.axis_index("cams")
    for distance, out in enumerate(pieces):
        target = lax.rem(cam + distance, cams) * piece
        offset = jnp.minimum(target, rows - piece)
        out[0:piece, :] = joined[pl.ds(rows + offset, piece), :]
        out[piece : 2 * piece, :] = joined[pl.ds(2 * rows + offset, piece), :]
        part = near_rows[pl.ds(offset, piece), :]
        out[2 * piece : 3 * piece, :] = part
        if cams * piece > rows:

            @pl.when(target >= rows)
            def _():
                out[...] = jnp.zeros_like(out)

    sums_out[0:1, :] = rows_sum(left * (scale * left))
    sums_out[1:2, :] = rows_sum(value * near)


def masks_kernel(part, half_pieces, grads, node_refs, skin, spread_out, masked, grads_pad):
    params, pixels = grads.shape
    slots = masked.shape[0] // ROWS
    chunk = 512
    grads_pad[...] = jnp.zeros_like(grads_pad)
    values = grads[...].astype(f32)
    for c in range(params // part):
        at = position(c, part, half_pieces)
        grads_pad[at : at + part, :] = values[c * part : (c + 1) * part]
    node_rows = lax.broadcasted_iota(jnp.int32, (LANES, chunk), 0)
    for at in range(0, pixels, chunk):
        cols = slice(at, at + chunk)
        refs = node_refs[:, cols]
        node = lax.bitwise_and(refs, LANES - 1)
        slot_of = lax.shift_right_logical(refs[0:1], 7)
        weights = skin[:, cols].astype(f32)
        grad16 = grads_pad[:, cols]
        spread = jnp.where(node_rows == node[0:1], weights[0:1], 0.0)
        for k in range(1, refs.shape[0]):
            spread = spread + jnp.where(node_rows == node[k : k + 1], weights[k : k + 1], 0.0)
        spread_out[:, cols] = spread

        def mask(slot):
            piece = jnp.where(slot_of == slot, grad16, 0.0).astype(bf16)
            masked[pl.ds(pl.multiple_of(slot * ROWS, ROWS), ROWS), cols] = piece

        loop(slots, mask)


def data_kernel(
    sizes, gathered, other, sums, spread, masked,
    out, frames_out, lists, list_rows, table_rows, products, sem,
):
    owners, cams, slot_count, held, params, part, half_pieces, extra, back_rows, step = sizes
    devices = owners * cams
    piece = held * part
    half = half_pieces * part
    block_rows = half * held + extra
    slots = owners * slot_count
    pixels = spread.shape[1]
    receiver = lax.axis_index("nodes")
    cam = lax.axis_index("cams")
    for owner in range(owners):
        at = owner * cams * block_rows + half * held
        list_rows[owner * extra : (owner + 1) * extra, :] = gathered[at : at + extra, :]
    copy = pltpu.make_async_copy(list_rows, lists, sem)
    copy.start()
    table_rows[...] = jnp.zeros_like(table_rows)
    curvature = sums[1:2, :]
    inside = cam * part < params
    offset = jnp.minimum(cam // 2, half_pieces - 1) * piece
    for c in range(cams):
        device = receiver * cams + c
        value = gathered[pl.ds(device * block_rows + offset, piece), :]
        before = gathered[pl.ds(jnp.maximum(device - step, 0) * block_rows + offset, piece), :]
        after = gathered[
            pl.ds(jnp.minimum(device + step, devices - 1) * block_rows + offset, piece), :
        ]
        earlier = jnp.where(jnp.logical_and(inside, device >= step), before, 0.0)
        following = jnp.where(jnp.logical_and(inside, device + step < devices), after, 0.0)
        frames = -temporal_weight * (earlier + following)
        frames_out[c * piece : (c + 1) * piece, :] = frames
        curvature = curvature + rows_sum(value * frames)
    mine_at = lax.rem(cam, 2) * half
    other_at = half - mine_at
    copy.wait()

    def fetch(slot):
        owner = slot // slot_count
        entry = (slot % slot_count) * owners + receiver
        listed = lists[owner * extra + entry // LANES, entry % LANES].astype(jnp.int32)
        listed = jnp.maximum(listed, 0)
        device = owner * cams + listed // held
        where = pl.ds(device * block_rows + listed % held, half, stride=held)
        table_rows[pl.ds(slot * ROWS + mine_at, half), :] = gathered[where, :]
        table_rows[pl.ds(slot * ROWS + other_at, half), :] = other[where, :]

    loop(slots, fetch)
    high, low = halves(table_rows[...].T)
    table = jnp.concatenate([high, low], axis=0)

    chunk = 512
    for at in range(0, pixels, chunk):
        cols = slice(at, at + chunk)
        live = masked[:, cols]
        weights = spread[:, cols]
        pulled = lax.dot_general(table, live, NN, preferred_element_type=f32)
        pulled = pulled[:LANES] + pulled[LANES:]
        projected = rows_sum(weights * pulled)
        squared = projected * projected
        for lane in range(0, chunk, LANES):
            curvature = curvature + squared[:, lane : lane + LANES]
        high, low = halves(weights * projected)
        both = jnp.concatenate([high, low], axis=0)
        back = lax.dot_general(live, both, NT, preferred_element_type=f32)
        back = back[:, :LANES] + back[:, LANES:]
        if at == 0:
            products[...] = back
        else:
            products[...] += back

    middle = LANES // 2
    lane_of = lax.broadcasted_iota(jnp.int32, (1, LANES), 1)
    start = sums[0:1, :]
    start = start + pltpu.roll(start, middle, 1)
    curvature = curvature + pltpu.roll(curvature, middle, 1)
    scalars = jnp.where(lane_of < middle, start, curvature)

    def give(owner):
        for c in range(cams):
            base = (owner * cams + c) * back_rows
            for s in range(slot_count):
                if c * part < params:
                    at = (owner * slot_count + s) * ROWS + position(c, part, half_pieces)
                    value = products[pl.ds(at, part), :]
                else:
                    value = jnp.zeros((part, LANES), f32)
                out[pl.ds(base + s * part, part), :] = value
            out[pl.ds(base + slot_count * part, 1), :] = scalars

    loop(owners, give)


def image_kernel(sizes, send_list, received, frames, *refs):
    owners, cams, slot_count, held, params, part, half_pieces, extra, back_rows, step = sizes
    mine, (scalars, blocks, image) = refs[:cams], refs[cams:]
    cam = lax.axis_index("cams")
    piece = held * part
    image[...] = jnp.zeros_like(image)
    last = jnp.zeros((1, LANES), f32)

    def collect(owner, last):
        at = owner * cams * back_rows
        total = received[pl.ds(at, back_rows), :]
        for c in range(1, cams):
            total = total + received[pl.ds(at + c * back_rows, back_rows), :]
        for s in range(slot_count):
            listed = jnp.maximum(send_list[s, 0, owner], 0)
            where = pl.ds((listed // held) * piece + listed % held, part, stride=held)
            image[where, :] = image[where, :] + total[s * part : (s + 1) * part]
        return last + total[back_rows - 1 : back_rows]

    last = lax.fori_loop(0, owners, collect, last, unroll=owners <= 32)
    half = LANES // 2
    lane_of = lax.broadcasted_iota(jnp.int32, (1, LANES), 1)
    start = jnp.sum(jnp.where(lane_of < half, last, 0.0), axis=1, keepdims=True)
    curvature = jnp.sum(jnp.where(lane_of < half, 0.0, last), axis=1, keepdims=True)
    length = start / curvature
    norms = jnp.zeros((1, LANES), f32)
    for distance, block in enumerate(mine):
        rows = pl.ds(lax.rem(cam + cams - distance, cams) * piece, piece)
        residual, precond, near = (block[k * piece : (k + 1) * piece, :] for k in range(3))
        value = image[rows, :] + near + frames[rows, :]
        image[rows, :] = value
        left = residual - length * value
        norms = norms + rows_sum(left * (precond * left))
    scalars[0:1, :] = jnp.broadcast_to(start, (1, LANES))
    scalars[1:2, :] = jnp.broadcast_to(length, (1, LANES))

    def tell(owner):
        for c in range(cams):
            base = (owner * cams + c) * (piece + 1)
            blocks[pl.ds(base, 1), :] = norms
            blocks[pl.ds(base + 1, piece), :] = image[c * piece : (c + 1) * piece, :]

    loop(owners, tell)


def update_kernel(
    sizes, arrived, scalars, iterate, residual, direction, precond,
    new_iterate, new_residual, new_direction,
):
    owners, cams, slot_count, held, params, part, half_pieces, extra, back_rows, step = sizes
    piece = held * part
    rows = iterate.shape[0]
    own = lax.axis_index("nodes")
    norms = arrived[0:1, :]
    for device in range(1, owners * cams):
        norms = norms + arrived[device * (piece + 1) : device * (piece + 1) + 1, :]
    start, length = scalars[0:1, :], scalars[1:2, :]
    ratio = jnp.sum(norms, axis=1, keepdims=True) / start
    for c in range(rows // piece):
        here = slice(c * piece, (c + 1) * piece)
        image = arrived[pl.ds((own * cams + c) * (piece + 1) + 1, piece), :]
        value = direction[here, :]
        left = residual[here, :] - length * image
        new_iterate[here, :] = iterate[here, :] + length * value
        new_residual[here, :] = left
        new_direction[here, :] = precond[here, :] * left + ratio * value


def flat(value):
    return jnp.transpose(value, (1, 0, 2)).reshape(-1, value.shape[2])


def exchange(blocks, axes):
    rows, lanes = blocks.shape
    peers = lax.axis_size(axes)
    blocks = blocks.reshape(peers, rows // peers, 1, lanes)
    blocks = lax.all_to_all(blocks, axes, split_axis=0, concat_axis=0, tiled=True)
    return blocks.reshape(rows, lanes)


def on_device(iterate, residual, direction, precond, send_list, grads, node_refs, skin, rigid_nbr):
    held, params, lanes = direction.shape
    pixels = grads.shape[1]
    owners = lax.axis_size("nodes")
    cams = lax.axis_size("cams")
    devices = owners * cams
    slot_count = send_list.shape[2]
    slots = owners * slot_count
    asked = limit(slots, pixels)
    rows = held * params
    extra = -(-slots // lanes)
    part = next(n for n in range(1, params + 1) if params % n == 0 and n * cams >= params)
    piece = held * part
    back_rows = slot_count * part + 1
    half_pieces = -(-(params // part) // 2)
    sizes = (
        owners, cams, slot_count, held, params, part, half_pieces, extra, back_rows, devices // FRAMES
    )

    def array(count):
        return jax.ShapeDtypeStruct((count, lanes), f32)

    iterate, residual, direction, precond = (flat(v) for v in (iterate, residual, direction, precond))
    by_slot = jnp.transpose(send_list, (2, 0, 1))
    filler = -(rows + slot_count) % 8
    listed = jnp.pad(by_slot.astype(f32), ((0, filler), (0, 0), (0, lanes - owners)))
    source = jnp.concatenate([direction.reshape(rows, 1, lanes), listed], axis=0)
    size = half_pieces * piece + extra
    packed = pl.pallas_call(
        functools.partial(
            pack_kernel, (rows, slot_count, piece, params // part, half_pieces), owners, cams, extra
        ),
        out_shape=array(devices * size),
        in_specs=[VMEM],
        out_specs=VMEM,
        scratch_shapes=[
            pltpu.VMEM((-(-2 * size // 8) * 8, lanes), f32),
            pltpu.VMEM((-(-extra // 8) * 8, lanes), f32),
        ],
        compiler_params=asked,
        name="pack",
    )(source.reshape(-1, lanes))
    packed, rigid_nbr, node_refs = lax.optimization_barrier((packed, rigid_nbr, node_refs))
    gathered = exchange(packed, AXES)
    other = lax.ppermute(gathered, "cams", [(c, c ^ 1) for c in range(cams)])

    nbr = flat(rigid_nbr)
    joined = jnp.concatenate([direction, residual, precond, nbr.astype(f32)], axis=0)
    sums, *pieces = pl.pallas_call(
        functools.partial(near_kernel, held, piece, rows),
        out_shape=(array(8),) + (array(3 * piece),) * cams,
        in_specs=[VMEM],
        out_specs=(VMEM,) * (1 + cams),
        scratch_shapes=[pltpu.VMEM((rows, lanes), f32)],
        compiler_params=asked,
        name="near",
    )(joined)
    spread, masked = pl.pallas_call(
        functools.partial(masks_kernel, part, half_pieces),
        out_shape=(
            jax.ShapeDtypeStruct((lanes, pixels), f32),
            jax.ShapeDtypeStruct((slots * ROWS, pixels), bf16),
        ),
        in_specs=[VMEM] * 3,
        out_specs=(VMEM,) * 2,
        scratch_shapes=[pltpu.VMEM((ROWS, pixels), f32)],
        compiler_params=asked,
        name="masks",
    )(grads, node_refs, skin)
    products, frames = pl.pallas_call(
        functools.partial(data_kernel, sizes),
        out_shape=(array(devices * back_rows), array(cams * piece)),
        in_specs=[VMEM] * 5,
        out_specs=(VMEM, VMEM),
        scratch_shapes=[
            pltpu.SMEM((owners * extra, lanes), f32),
            pltpu.VMEM((owners * extra, lanes), f32),
            pltpu.VMEM((slots * ROWS, lanes), f32),
            pltpu.VMEM((slots * ROWS, lanes), f32),
            pltpu.SemaphoreType.DMA,
        ],
        compiler_params=asked,
        name="data_products",
    )(gathered, other, sums, spread, masked)
    received = exchange(products, AXES)
    frames, *pieces = lax.optimization_barrier((frames, *pieces))
    mine = [pieces[0]]
    for distance in range(1, cams):
        pairs = [(c, (c + distance) % cams) for c in range(cams)]
        mine.append(lax.ppermute(pieces[distance], "cams", pairs))

    scalars, blocks = pl.pallas_call(
        functools.partial(image_kernel, sizes),
        out_shape=(array(8), array(devices * (piece + 1))),
        in_specs=[SMEM] + [VMEM] * (2 + cams),
        out_specs=(VMEM,) * 2,
        scratch_shapes=[pltpu.VMEM((cams * piece, lanes), f32)],
        compiler_params=asked,
        name="image",
    )(by_slot, received, frames, *mine)
    arrived = exchange(blocks, AXES)
    outs = pl.pallas_call(
        functools.partial(update_kernel, sizes),
        out_shape=(array(rows),) * 3,
        in_specs=[VMEM] * 6,
        out_specs=(VMEM,) * 3,
        compiler_params=asked,
        name="update",
    )(arrived, scalars, iterate, residual, direction, precond)
    return tuple(jnp.transpose(v.reshape(params, held, lanes), (1, 0, 2)) for v in outs)


def solution(mesh):
    split = P(AXES, None, None)
    pixel_split = P(None, AXES)
    in_specs = (split,) * 4 + (P("nodes", None, None),) + (pixel_split,) * 3 + (split,)
    return jax.shard_map(
        on_device, mesh=mesh, in_specs=in_specs, out_specs=(split,) * 3, check_vma=False
    )
```

```python
import functools

import jax
import jax.numpy as jnp
from jax import lax
from jax.experimental import pallas as pl
from jax.experimental.pallas import tpu as pltpu
from jax.sharding import PartitionSpec as P

FRAMES = 8
AXES = ("nodes", "cams")
temporal_weight = 0.5
rigid_weight = 0.1
NN = (((1,), (0,)), ((), ()))
NT = (((1,), (1,)), ((), ()))
LANES = 128
ROWS = 16
f32 = jnp.float32
bf16 = jnp.bfloat16

VMEM = pl.BlockSpec(memory_space=pltpu.VMEM)
SMEM = pl.BlockSpec(memory_space=pltpu.SMEM)


def limit(slots, pixels):
    need = 8 * 2**20 + slots * ROWS * pixels * 3
    return pltpu.CompilerParams(vmem_limit_bytes=min(need, 56 * 2**20))


def halves(value):
    high = value.astype(bf16)
    low = (value - high.astype(f32)).astype(bf16)
    return high, low


def rows_sum(value):
    return jnp.sum(value, axis=0, keepdims=True)


def loop(count, body):
    lax.fori_loop(0, count, lambda i, carry: (body(i), carry)[1], 0, unroll=count <= 32)


def position(c, part, half_pieces):
    return (c % 2) * half_pieces * part + (c // 2) * part


def pack_kernel(sizes, owners, cams, extra, source, out, halves_of, lists):
    rows, slot_count, piece, pieces, half_pieces = sizes
    half_rows = half_pieces * piece
    lists[...] = jnp.zeros_like(lists)
    for s in range(slot_count):
        row, lane = divmod(s * owners, LANES)
        moved = source[rows + s : rows + s + 1, :]
        if lane:
            moved = pltpu.roll(moved, lane, 1)
        lists[row : row + 1, :] = lists[row : row + 1, :] + moved
    size = half_rows + extra
    halves_of[...] = jnp.zeros_like(halves_of)
    for c in range(pieces):
        at = (c % 2) * size + (c // 2) * piece
        halves_of[at : at + piece, :] = source[c * piece : (c + 1) * piece, :]
    for parity in range(2):
        at = parity * size + half_rows
        halves_of[at : at + extra, :] = lists[0:extra, :]

    def write(owner):
        for c in range(cams):
            at = (c % 2) * size
            out[pl.ds((owner * cams + c) * size, size), :] = halves_of[at : at + size, :]

    loop(owners, write)


def near_kernel(held, piece, rows, joined, sums_out, *pieces):
    *pieces, near_rows = pieces
    value = joined[0:rows, :]
    left = joined[rows : 2 * rows, :]
    scale = joined[2 * rows : 3 * rows, :]
    high, low = halves(value)
    stack = jnp.concatenate([high.astype(f32), low.astype(f32), jnp.ones((16, LANES), f32)], axis=0)
    stack = stack.astype(bf16)
    node_rows = lax.broadcasted_iota(jnp.int32, (LANES, LANES), 0).astype(f32)
    patch_row = lax.broadcasted_iota(jnp.int32, (rows, LANES), 0) % held
    edges = (joined.shape[0] - 3 * rows) // held
    rigid = jnp.zeros_like(value)
    for q in range(held):
        hits = jnp.zeros((LANES, LANES), f32)
        for r in range(edges):
            at = 3 * rows + r * held + q
            hits = hits + jnp.where(node_rows == joined[at : at + 1, :], 1.0, 0.0)
        hits = hits.astype(bf16)
        pulled = lax.dot_general(stack, hits, NN, preferred_element_type=f32)
        pushed = lax.dot_general(stack, hits, NT, preferred_element_type=f32)
        degree = pushed[2 * rows : 2 * rows + 1]
        both = pulled + pushed
        part = value * (degree + float(edges)) - (both[:rows] + both[rows : 2 * rows])
        rigid = jnp.where(patch_row == q, part, rigid)
    near = rigid_weight * rigid + (2.0 * temporal_weight) * value
    near_rows[...] = near
    cams = len(pieces)
    cam = lax.axis_index("cams")
    for distance, out in enumerate(pieces):
        target = lax.rem(cam + distance, cams) * piece
        offset = jnp.minimum(target, rows - piece)
        out[0:piece, :] = joined[pl.ds(rows + offset, piece), :]
        out[piece : 2 * piece, :] = joined[pl.ds(2 * rows + offset, piece), :]
        part = near_rows[pl.ds(offset, piece), :]
        out[2 * piece : 3 * piece, :] = part
        if cams * piece > rows:

            @pl.when(target >= rows)
            def _():
                out[...] = jnp.zeros_like(out)

    sums_out[0:1, :] = rows_sum(left * (scale * left))
    sums_out[1:2, :] = rows_sum(value * near)


def masks_kernel(part, half_pieces, grads, node_refs, skin, spread_out, masked, grads_pad):
    params, pixels = grads.shape
    slots = masked.shape[0] // ROWS
    chunk = 512
    grads_pad[...] = jnp.zeros_like(grads_pad)
    values = grads[...].astype(f32)
    for c in range(params // part):
        at = position(c, part, half_pieces)
        grads_pad[at : at + part, :] = values[c * part : (c + 1) * part]
    node_rows = lax.broadcasted_iota(jnp.int32, (LANES, chunk), 0)
    for at in range(0, pixels, chunk):
        cols = slice(at, at + chunk)
        refs = node_refs[:, cols]
        node = lax.bitwise_and(refs, LANES - 1)
        slot_of = lax.shift_right_logical(refs[0:1], 7)
        weights = skin[:, cols].astype(f32)
        grad16 = grads_pad[:, cols]
        spread = jnp.where(node_rows == node[0:1], weights[0:1], 0.0)
        for k in range(1, refs.shape[0]):
            spread = spread + jnp.where(node_rows == node[k : k + 1], weights[k : k + 1], 0.0)
        spread_out[:, cols] = spread

        def mask(slot):
            piece = jnp.where(slot_of == slot, grad16, 0.0).astype(bf16)
            masked[pl.ds(pl.multiple_of(slot * ROWS, ROWS), ROWS), cols] = piece

        loop(slots, mask)


def data_kernel(
    sizes, gathered, other, sums, spread, masked,
    out, frames_out, lists, list_rows, table_rows, products, sem,
):
    owners, cams, slot_count, held, params, part, half_pieces, extra, back_rows, step = sizes
    devices = owners * cams
    piece = held * part
    half = half_pieces * part
    block_rows = half * held + extra
    slots = owners * slot_count
    pixels = spread.shape[1]
    receiver = lax.axis_index("nodes")
    cam = lax.axis_index("cams")
    for owner in range(owners):
        at = owner * cams * block_rows + half * held
        list_rows[owner * extra : (owner + 1) * extra, :] = gathered[at : at + extra, :]
    copy = pltpu.make_async_copy(list_rows, lists, sem)
    copy.start()
    table_rows[...] = jnp.zeros_like(table_rows)
    curvature = sums[1:2, :]
    inside = cam * part < params
    offset = jnp.minimum(cam // 2, half_pieces - 1) * piece
    for c in range(cams):
        device = receiver * cams + c
        value = gathered[pl.ds(device * block_rows + offset, piece), :]
        before = gathered[pl.ds(jnp.maximum(device - step, 0) * block_rows + offset, piece), :]
        after = gathered[
            pl.ds(jnp.minimum(device + step, devices - 1) * block_rows + offset, piece), :
        ]
        earlier = jnp.where(jnp.logical_and(inside, device >= step), before, 0.0)
        following = jnp.where(jnp.logical_and(inside, device + step < devices), after, 0.0)
        frames = -temporal_weight * (earlier + following)
        frames_out[c * piece : (c + 1) * piece, :] = frames
        curvature = curvature + rows_sum(value * frames)
    mine_at = lax.rem(cam, 2) * half
    other_at = half - mine_at
    copy.wait()

    def fetch(slot):
        owner = slot // slot_count
        entry = (slot % slot_count) * owners + receiver
        listed = lists[owner * extra + entry // LANES, entry % LANES].astype(jnp.int32)
        listed = jnp.maximum(listed, 0)
        device = owner * cams + listed // held
        where = pl.ds(device * block_rows + listed % held, half, stride=held)
        table_rows[pl.ds(slot * ROWS + mine_at, half), :] = gathered[where, :]
        table_rows[pl.ds(slot * ROWS + other_at, half), :] = other[where, :]

    loop(slots, fetch)
    high, low = halves(table_rows[...].T)
    table = jnp.concatenate([high, low], axis=0)

    chunk = 512
    for at in range(0, pixels, chunk):
        cols = slice(at, at + chunk)
        live = masked[:, cols]
        weights = spread[:, cols]
        pulled = lax.dot_general(table, live, NN, preferred_element_type=f32)
        pulled = pulled[:LANES] + pulled[LANES:]
        projected = rows_sum(weights * pulled)
        squared = projected * projected
        for lane in range(0, chunk, LANES):
            curvature = curvature + squared[:, lane : lane + LANES]
        high, low = halves(weights * projected)
        both = jnp.concatenate([high, low], axis=0)
        back = lax.dot_general(live, both, NT, preferred_element_type=f32)
        back = back[:, :LANES] + back[:, LANES:]
        if at == 0:
            products[...] = back
        else:
            products[...] += back

    middle = LANES // 2
    lane_of = lax.broadcasted_iota(jnp.int32, (1, LANES), 1)
    start = sums[0:1, :]
    start = start + pltpu.roll(start, middle, 1)
    curvature = curvature + pltpu.roll(curvature, middle, 1)
    scalars = jnp.where(lane_of < middle, start, curvature)

    def give(owner):
        for c in range(cams):
            base = (owner * cams + c) * back_rows
            for s in range(slot_count):
                if c * part < params:
                    at = (owner * slot_count + s) * ROWS + position(c, part, half_pieces)
                    value = products[pl.ds(at, part), :]
                else:
                    value = jnp.zeros((part, LANES), f32)
                out[pl.ds(base + s * part, part), :] = value
            out[pl.ds(base + slot_count * part, 1), :] = scalars

    loop(owners, give)


def image_kernel(sizes, send_list, received, frames, *refs):
    owners, cams, slot_count, held, params, part, half_pieces, extra, back_rows, step = sizes
    mine, (scalars, blocks, image) = refs[:cams], refs[cams:]
    cam = lax.axis_index("cams")
    piece = held * part
    image[...] = jnp.zeros_like(image)
    last = jnp.zeros((1, LANES), f32)

    def collect(owner, last):
        at = owner * cams * back_rows
        total = received[pl.ds(at, back_rows), :]
        for c in range(1, cams):
            total = total + received[pl.ds(at + c * back_rows, back_rows), :]
        for s in range(slot_count):
            listed = jnp.maximum(send_list[s, 0, owner], 0)
            where = pl.ds((listed // held) * piece + listed % held, part, stride=held)
            image[where, :] = image[where, :] + total[s * part : (s + 1) * part]
        return last + total[back_rows - 1 : back_rows]

    last = lax.fori_loop(0, owners, collect, last, unroll=owners <= 32)
    half = LANES // 2
    lane_of = lax.broadcasted_iota(jnp.int32, (1, LANES), 1)
    start = jnp.sum(jnp.where(lane_of < half, last, 0.0), axis=1, keepdims=True)
    curvature = jnp.sum(jnp.where(lane_of < half, 0.0, last), axis=1, keepdims=True)
    length = start / curvature
    norms = jnp.zeros((1, LANES), f32)
    for distance, block in enumerate(mine):
        rows = pl.ds(lax.rem(cam + cams - distance, cams) * piece, piece)
        residual, precond, near = (block[k * piece : (k + 1) * piece, :] for k in range(3))
        value = image[rows, :] + near + frames[rows, :]
        image[rows, :] = value
        left = residual - length * value
        norms = norms + rows_sum(left * (precond * left))
    scalars[0:1, :] = jnp.broadcast_to(start, (1, LANES))
    scalars[1:2, :] = jnp.broadcast_to(length, (1, LANES))

    def tell(owner):
        for c in range(cams):
            base = (owner * cams + c) * (piece + 1)
            blocks[pl.ds(base, 1), :] = norms
            blocks[pl.ds(base + 1, piece), :] = image[c * piece : (c + 1) * piece, :]

    loop(owners, tell)


def update_kernel(
    sizes, arrived, scalars, iterate, residual, direction, precond,
    new_iterate, new_residual, new_direction,
):
    owners, cams, slot_count, held, params, part, half_pieces, extra, back_rows, step = sizes
    piece = held * part
    rows = iterate.shape[0]
    own = lax.axis_index("nodes")
    norms = arrived[0:1, :]
    for device in range(1, owners * cams):
        norms = norms + arrived[device * (piece + 1) : device * (piece + 1) + 1, :]
    start, length = scalars[0:1, :], scalars[1:2, :]
    ratio = jnp.sum(norms, axis=1, keepdims=True) / start
    for c in range(rows // piece):
        here = slice(c * piece, (c + 1) * piece)
        image = arrived[pl.ds((own * cams + c) * (piece + 1) + 1, piece), :]
        value = direction[here, :]
        left = residual[here, :] - length * image
        new_iterate[here, :] = iterate[here, :] + length * value
        new_residual[here, :] = left
        new_direction[here, :] = precond[here, :] * left + ratio * value


def flat(value):
    return jnp.transpose(value, (1, 0, 2)).reshape(-1, value.shape[2])


def exchange(blocks, axes):
    rows, lanes = blocks.shape
    peers = lax.axis_size(axes)
    blocks = blocks.reshape(peers, rows // peers, 1, lanes)
    blocks = lax.all_to_all(blocks, axes, split_axis=0, concat_axis=0, tiled=True)
    return blocks.reshape(rows, lanes)


def on_device(iterate, residual, direction, precond, send_list, grads, node_refs, skin, rigid_nbr):
    held, params, lanes = direction.shape
    pixels = grads.shape[1]
    owners = lax.axis_size("nodes")
    cams = lax.axis_size("cams")
    devices = owners * cams
    slot_count = send_list.shape[2]
    slots = owners * slot_count
    asked = limit(slots, pixels)
    rows = held * params
    extra = -(-slots // lanes)
    part = next(n for n in range(1, params + 1) if params % n == 0 and n * cams >= params)
    piece = held * part
    back_rows = slot_count * part + 1
    half_pieces = -(-(params // part) // 2)
    sizes = (
        owners, cams, slot_count, held, params, part, half_pieces, extra, back_rows, devices // FRAMES
    )

    def array(count):
        return jax.ShapeDtypeStruct((count, lanes), f32)

    iterate, residual, direction, precond = (flat(v) for v in (iterate, residual, direction, precond))
    by_slot = jnp.transpose(send_list, (2, 0, 1))
    filler = -(rows + slot_count) % 8
    listed = jnp.pad(by_slot.astype(f32), ((0, filler), (0, 0), (0, lanes - owners)))
    source = jnp.concatenate([direction.reshape(rows, 1, lanes), listed], axis=0)
    size = half_pieces * piece + extra
    packed = pl.pallas_call(
        functools.partial(
            pack_kernel, (rows, slot_count, piece, params // part, half_pieces), owners, cams, extra
        ),
        out_shape=array(devices * size),
        in_specs=[VMEM],
        out_specs=VMEM,
        scratch_shapes=[
            pltpu.VMEM((-(-2 * size // 8) * 8, lanes), f32),
            pltpu.VMEM((-(-extra // 8) * 8, lanes), f32),
        ],
        compiler_params=asked,
        name="pack",
    )(source.reshape(-1, lanes))
    packed, rigid_nbr, node_refs = lax.optimization_barrier((packed, rigid_nbr, node_refs))
    gathered = exchange(packed, AXES)

    nbr = flat(rigid_nbr)
    joined = jnp.concatenate([direction, residual, precond, nbr.astype(f32)], axis=0)
    sums, *pieces = pl.pallas_call(
        functools.partial(near_kernel, held, piece, rows),
        out_shape=(array(8),) + (array(3 * piece),) * cams,
        in_specs=[VMEM],
        out_specs=(VMEM,) * (1 + cams),
        scratch_shapes=[pltpu.VMEM((rows, lanes), f32)],
        compiler_params=asked,
        name="near",
    )(joined)
    spread, masked = pl.pallas_call(
        functools.partial(masks_kernel, part, half_pieces),
        out_shape=(
            jax.ShapeDtypeStruct((lanes, pixels), f32),
            jax.ShapeDtypeStruct((slots * ROWS, pixels), bf16),
        ),
        in_specs=[VMEM] * 3,
        out_specs=(VMEM,) * 2,
        scratch_shapes=[pltpu.VMEM((ROWS, pixels), f32)],
        compiler_params=asked,
        name="masks",
    )(grads, node_refs, skin)
    gathered, spread, sums = lax.optimization_barrier((gathered, spread, sums))
    other = lax.ppermute(gathered, "cams", [(c, c ^ 1) for c in range(cams)])

    products, frames = pl.pallas_call(
        functools.partial(data_kernel, sizes),
        out_shape=(array(devices * back_rows), array(cams * piece)),
        in_specs=[VMEM] * 5,
        out_specs=(VMEM, VMEM),
        scratch_shapes=[
            pltpu.SMEM((owners * extra, lanes), f32),
            pltpu.VMEM((owners * extra, lanes), f32),
            pltpu.VMEM((slots * ROWS, lanes), f32),
            pltpu.VMEM((slots * ROWS, lanes), f32),
            pltpu.SemaphoreType.DMA,
        ],
        compiler_params=asked,
        name="data_products",
    )(gathered, other, sums, spread, masked)
    received = exchange(products, AXES)
    frames, *pieces = lax.optimization_barrier((frames, *pieces))
    mine = [pieces[0]]
    for distance in range(1, cams):
        pairs = [(c, (c + distance) % cams) for c in range(cams)]
        mine.append(lax.ppermute(pieces[distance], "cams", pairs))

    scalars, blocks = pl.pallas_call(
        functools.partial(image_kernel, sizes),
        out_shape=(array(8), array(devices * (piece + 1))),
        in_specs=[SMEM] + [VMEM] * (2 + cams),
        out_specs=(VMEM,) * 2,
        scratch_shapes=[pltpu.VMEM((cams * piece, lanes), f32)],
        compiler_params=asked,
        name="image",
    )(by_slot, received, frames, *mine)
    arrived = exchange(blocks, AXES)
    outs = pl.pallas_call(
        functools.partial(update_kernel, sizes),
        out_shape=(array(rows),) * 3,
        in_specs=[VMEM] * 6,
        out_specs=(VMEM,) * 3,
        compiler_params=asked,
        name="update",
    )(arrived, scalars, iterate, residual, direction, precond)
    return tuple(jnp.transpose(v.reshape(params, held, lanes), (1, 0, 2)) for v in outs)


def solution(mesh):
    split = P(AXES, None, None)
    pixel_split = P(None, AXES)
    in_specs = (split,) * 4 + (P("nodes", None, None),) + (pixel_split,) * 3 + (split,)
    return jax.shard_map(
        on_device, mesh=mesh, in_specs=in_specs, out_specs=(split,) * 3, check_vma=False
    )
```

```python
import functools

import jax
import jax.numpy as jnp
from jax import lax
from jax.experimental import pallas as pl
from jax.experimental.pallas import tpu as pltpu
from jax.sharding import PartitionSpec as P

FRAMES = 8
AXES = ("nodes", "cams")
temporal_weight = 0.5
rigid_weight = 0.1
NN = (((1,), (0,)), ((), ()))
NT = (((1,), (1,)), ((), ()))
LANES = 128
HALF = 8
f32 = jnp.float32
bf16 = jnp.bfloat16

VMEM = pl.BlockSpec(memory_space=pltpu.VMEM)
SMEM = pl.BlockSpec(memory_space=pltpu.SMEM)


def limit(slots, pixels):
    need = 8 * 2**20 + slots * 2 * HALF * pixels * 3
    return pltpu.CompilerParams(vmem_limit_bytes=min(need, 56 * 2**20))


def halves(value):
    high = value.astype(bf16)
    low = (value - high.astype(f32)).astype(bf16)
    return high, low


def rows_sum(value):
    return jnp.sum(value, axis=0, keepdims=True)


def loop(count, body):
    lax.fori_loop(0, count, lambda i, carry: (body(i), carry)[1], 0, unroll=count <= 32)


def pack_kernel(sizes, owners, cams, extra, source, out, halves_of, lists):
    rows, slot_count, piece, pieces, half_pieces = sizes
    half_rows = half_pieces * piece
    lists[...] = jnp.zeros_like(lists)
    for s in range(slot_count):
        row, lane = divmod(s * owners, LANES)
        moved = source[rows + s : rows + s + 1, :]
        if lane:
            moved = pltpu.roll(moved, lane, 1)
        lists[row : row + 1, :] = lists[row : row + 1, :] + moved
    size = half_rows + extra
    halves_of[...] = jnp.zeros_like(halves_of)
    for c in range(pieces):
        at = (c % 2) * size + (c // 2) * piece
        halves_of[at : at + piece, :] = source[c * piece : (c + 1) * piece, :]
    for parity in range(2):
        at = parity * size + half_rows
        halves_of[at : at + extra, :] = lists[0:extra, :]

    def write(owner):
        for c in range(cams):
            at = (c % 2) * size
            out[pl.ds((owner * cams + c) * size, size), :] = halves_of[at : at + size, :]

    loop(owners, write)


def near_kernel(held, piece, rows, joined, sums_out, *pieces):
    *pieces, near_rows = pieces
    value = joined[0:rows, :]
    left = joined[rows : 2 * rows, :]
    scale = joined[2 * rows : 3 * rows, :]
    high, low = halves(value)
    stack = jnp.concatenate([high.astype(f32), low.astype(f32), jnp.ones((16, LANES), f32)], axis=0)
    stack = stack.astype(bf16)
    node_rows = lax.broadcasted_iota(jnp.int32, (LANES, LANES), 0).astype(f32)
    patch_row = lax.broadcasted_iota(jnp.int32, (rows, LANES), 0) % held
    edges = (joined.shape[0] - 3 * rows) // held
    rigid = jnp.zeros_like(value)
    for q in range(held):
        hits = jnp.zeros((LANES, LANES), f32)
        for r in range(edges):
            at = 3 * rows + r * held + q
            hits = hits + jnp.where(node_rows == joined[at : at + 1, :], 1.0, 0.0)
        hits = hits.astype(bf16)
        pulled = lax.dot_general(stack, hits, NN, preferred_element_type=f32)
        pushed = lax.dot_general(stack, hits, NT, preferred_element_type=f32)
        degree = pushed[2 * rows : 2 * rows + 1]
        both = pulled + pushed
        part = value * (degree + float(edges)) - (both[:rows] + both[rows : 2 * rows])
        rigid = jnp.where(patch_row == q, part, rigid)
    near = rigid_weight * rigid + (2.0 * temporal_weight) * value
    near_rows[...] = near
    cams = len(pieces)
    cam = lax.axis_index("cams")
    for distance, out in enumerate(pieces):
        target = lax.rem(cam + distance, cams) * piece
        offset = jnp.minimum(target, rows - piece)
        out[0:piece, :] = joined[pl.ds(rows + offset, piece), :]
        out[piece : 2 * piece, :] = joined[pl.ds(2 * rows + offset, piece), :]
        part = near_rows[pl.ds(offset, piece), :]
        out[2 * piece : 3 * piece, :] = part
        if cams * piece > rows:

            @pl.when(target >= rows)
            def _():
                out[...] = jnp.zeros_like(out)

    sums_out[0:1, :] = rows_sum(left * (scale * left))
    sums_out[1:2, :] = rows_sum(value * near)


def masks_kernel(part, half_pieces, grads, node_refs, skin, spread_out, masked, grads_pad):
    params, pixels = grads.shape
    side = masked.shape[0] // 2
    chunk = 512
    grads_pad[...] = jnp.zeros_like(grads_pad)
    values = grads[...].astype(f32)
    for c in range(params // part):
        for copy in range(2):
            at = (2 * (c % 2) + copy) * HALF + (c // 2) * part
            grads_pad[at : at + part, :] = values[c * part : (c + 1) * part]
    node_rows = lax.broadcasted_iota(jnp.int32, (LANES, chunk), 0)
    upper = lax.broadcasted_iota(jnp.int32, (2 * HALF, chunk), 0) // HALF
    for at in range(0, pixels, chunk):
        cols = slice(at, at + chunk)
        refs = node_refs[:, cols]
        node = lax.bitwise_and(refs, LANES - 1)
        slot_of = lax.shift_right_logical(refs[0:1], 7) - upper
        weights = skin[:, cols].astype(f32)
        even, odd = grads_pad[0 : 2 * HALF, cols], grads_pad[2 * HALF :, cols]
        spread = jnp.where(node_rows == node[0:1], weights[0:1], 0.0)
        for k in range(1, refs.shape[0]):
            spread = spread + jnp.where(node_rows == node[k : k + 1], weights[k : k + 1], 0.0)
        spread_out[:, cols] = spread

        def mask(pair):
            here = slot_of == 2 * pair
            rows = pl.multiple_of(2 * HALF * pair, 2 * HALF)
            masked[pl.ds(rows, 2 * HALF), cols] = jnp.where(here, even, 0.0).astype(bf16)
            rows = pl.multiple_of(side + 2 * HALF * pair, 2 * HALF)
            masked[pl.ds(rows, 2 * HALF), cols] = jnp.where(here, odd, 0.0).astype(bf16)

        loop(side // (2 * HALF), mask)


def table_kernel(sizes, gathered, table_out, frames_out, sums_out, lists, list_rows, sem):
    owners, cams, slot_count, held, params, part, half_pieces, extra, back_rows, step = sizes
    devices = owners * cams
    piece = held * part
    half = half_pieces * part
    block_rows = half * held + extra
    receiver = lax.axis_index("nodes")
    cam = lax.axis_index("cams")
    for owner in range(owners):
        at = owner * cams * block_rows + half * held
        list_rows[owner * extra : (owner + 1) * extra, :] = gathered[at : at + extra, :]
    copy = pltpu.make_async_copy(list_rows, lists, sem)
    copy.start()
    table_out[...] = jnp.zeros_like(table_out)
    curvature = jnp.zeros((1, LANES), f32)
    inside = cam * part < params
    offset = jnp.minimum(cam // 2, half_pieces - 1) * piece
    for c in range(cams):
        device = receiver * cams + c
        value = gathered[pl.ds(device * block_rows + offset, piece), :]
        before = gathered[pl.ds(jnp.maximum(device - step, 0) * block_rows + offset, piece), :]
        after = gathered[
            pl.ds(jnp.minimum(device + step, devices - 1) * block_rows + offset, piece), :
        ]
        earlier = jnp.where(jnp.logical_and(inside, device >= step), before, 0.0)
        following = jnp.where(jnp.logical_and(inside, device + step < devices), after, 0.0)
        frames = -temporal_weight * (earlier + following)
        frames_out[c * piece : (c + 1) * piece, :] = frames
        curvature = curvature + rows_sum(value * frames)
    sums_out[0:1, :] = curvature
    copy.wait()

    def fetch(slot):
        owner = slot // slot_count
        entry = (slot % slot_count) * owners + receiver
        listed = lists[owner * extra + entry // LANES, entry % LANES].astype(jnp.int32)
        listed = jnp.maximum(listed, 0)
        device = owner * cams + listed // held
        where = pl.ds(device * block_rows + listed % held, half, stride=held)
        table_out[pl.ds(pl.multiple_of(slot * HALF, HALF), half), :] = gathered[where, :]

    loop(owners * slot_count, fetch)


def pull(table, masked, parity, cols):
    side = masked.shape[0] // 2
    live = masked[pl.ds(pl.multiple_of(parity * side, 2 * HALF), side), cols]
    pulled = lax.dot_general(table, live, NN, preferred_element_type=f32)
    return pulled[:LANES] + pulled[LANES:]


def turned_halves(table):
    return jnp.concatenate(halves(table[...].T), axis=0)


def own_kernel(table, masked, pulled_out):
    parity = lax.rem(lax.axis_index("cams"), 2)
    turned_table = turned_halves(table)
    chunk = 512
    for at in range(0, masked.shape[1], chunk):
        cols = slice(at, at + chunk)
        pulled_out[:, cols] = pull(turned_table, masked, parity, cols)


def data_kernel(sizes, pulled_own, table, near_sums, frame_sums, spread, masked, out, products):
    owners, cams, slot_count, held, params, part, half_pieces, extra, back_rows, step = sizes
    side = masked.shape[0] // 2
    parity = 1 - lax.rem(lax.axis_index("cams"), 2)
    turned_table = turned_halves(table)
    curvature = near_sums[1:2, :] + frame_sums[0:1, :]
    chunk = 512
    for at in range(0, spread.shape[1], chunk):
        cols = slice(at, at + chunk)
        weights = spread[:, cols]
        pulled = pulled_own[:, cols] + pull(turned_table, masked, parity, cols)
        projected = rows_sum(weights * pulled)
        squared = projected * projected
        for lane in range(0, chunk, LANES):
            curvature = curvature + squared[:, lane : lane + LANES]
        both = jnp.concatenate(halves(weights * projected), axis=0)
        back = lax.dot_general(masked[:, cols], both, NT, preferred_element_type=f32)
        back = back[:, :LANES] + back[:, LANES:]
        if at == 0:
            products[...] = back
        else:
            products[...] += back

    middle = LANES // 2
    lane_of = lax.broadcasted_iota(jnp.int32, (1, LANES), 1)
    start = near_sums[0:1, :]
    start = start + pltpu.roll(start, middle, 1)
    curvature = curvature + pltpu.roll(curvature, middle, 1)
    scalars = jnp.where(lane_of < middle, start, curvature)

    def give(owner):
        for c in range(cams):
            base = (owner * cams + c) * back_rows
            for s in range(slot_count):
                if c * part < params:
                    at = (c % 2) * side + (owner * slot_count + s) * HALF + (c // 2) * part
                    value = products[pl.ds(at, part), :]
                else:
                    value = jnp.zeros((part, LANES), f32)
                out[pl.ds(base + s * part, part), :] = value
            out[pl.ds(base + slot_count * part, 1), :] = scalars

    loop(owners, give)


def image_kernel(sizes, send_list, received, frames, *refs):
    owners, cams, slot_count, held, params, part, half_pieces, extra, back_rows, step = sizes
    mine, (scalars, blocks, image, *parts) = refs[:cams], refs[cams:]
    cam = lax.axis_index("cams")
    piece = held * part
    for place in parts:
        place[...] = jnp.zeros_like(place)
    last = jnp.zeros((1, LANES), f32)

    def collect(owner, last):
        at = owner * cams * back_rows
        total = received[pl.ds(at, back_rows), :]
        for c in range(1, cams):
            total = total + received[pl.ds(at + c * back_rows, back_rows), :]
        for s in range(slot_count):
            listed = jnp.maximum(send_list[s, 0, owner], 0)
            where = pl.ds((listed // held) * piece + listed % held, part, stride=held)
            parts[s][where, :] = parts[s][where, :] + total[s * part : (s + 1) * part]
        return last + total[back_rows - 1 : back_rows]

    last = lax.fori_loop(0, owners, collect, last, unroll=owners <= 32)
    half = LANES // 2
    lane_of = lax.broadcasted_iota(jnp.int32, (1, LANES), 1)
    start = jnp.sum(jnp.where(lane_of < half, last, 0.0), axis=1, keepdims=True)
    curvature = jnp.sum(jnp.where(lane_of < half, 0.0, last), axis=1, keepdims=True)
    length = start / curvature
    norms = jnp.zeros((1, LANES), f32)
    image[...] = functools.reduce(jnp.add, [place[...] for place in parts])
    for distance, block in enumerate(mine):
        rows = pl.ds(lax.rem(cam + cams - distance, cams) * piece, piece)
        residual, precond, near = (block[k * piece : (k + 1) * piece, :] for k in range(3))
        value = image[rows, :] + near + frames[rows, :]
        image[rows, :] = value
        left = residual - length * value
        norms = norms + rows_sum(left * (precond * left))
    scalars[0:1, :] = jnp.broadcast_to(start, (1, LANES))
    scalars[1:2, :] = jnp.broadcast_to(length, (1, LANES))

    def tell(owner):
        for c in range(cams):
            base = (owner * cams + c) * (piece + 1)
            blocks[pl.ds(base, 1), :] = norms
            blocks[pl.ds(base + 1, piece), :] = image[c * piece : (c + 1) * piece, :]

    loop(owners, tell)


def update_kernel(
    sizes, arrived, scalars, iterate, residual, direction, precond,
    new_iterate, new_residual, new_direction,
):
    owners, cams, slot_count, held, params, part, half_pieces, extra, back_rows, step = sizes
    piece = held * part
    rows = iterate.shape[0]
    own = lax.axis_index("nodes")
    norms = arrived[0:1, :]
    for device in range(1, owners * cams):
        norms = norms + arrived[device * (piece + 1) : device * (piece + 1) + 1, :]
    start, length = scalars[0:1, :], scalars[1:2, :]
    ratio = jnp.sum(norms, axis=1, keepdims=True) / start
    for c in range(rows // piece):
        here = slice(c * piece, (c + 1) * piece)
        image = arrived[pl.ds((own * cams + c) * (piece + 1) + 1, piece), :]
        value = direction[here, :]
        left = residual[here, :] - length * image
        new_iterate[here, :] = iterate[here, :] + length * value
        new_residual[here, :] = left
        new_direction[here, :] = precond[here, :] * left + ratio * value


def flat(value):
    return jnp.transpose(value, (1, 0, 2)).reshape(-1, value.shape[2])


def exchange(blocks, axes):
    rows, lanes = blocks.shape
    peers = lax.axis_size(axes)
    blocks = blocks.reshape(peers, rows // peers, 1, lanes)
    blocks = lax.all_to_all(blocks, axes, split_axis=0, concat_axis=0, tiled=True)
    return blocks.reshape(rows, lanes)


def on_device(iterate, residual, direction, precond, send_list, grads, node_refs, skin, rigid_nbr):
    held, params, lanes = direction.shape
    pixels = grads.shape[1]
    owners = lax.axis_size("nodes")
    cams = lax.axis_size("cams")
    devices = owners * cams
    slot_count = send_list.shape[2]
    slots = owners * slot_count
    asked = limit(slots, pixels)
    rows = held * params
    extra = -(-slots // lanes)
    part = next(n for n in range(1, params + 1) if params % n == 0 and n * cams >= params)
    piece = held * part
    back_rows = slot_count * part + 1
    half_pieces = -(-(params // part) // 2)
    side = (slots + slots % 2) * HALF
    sizes = (
        owners, cams, slot_count, held, params, part, half_pieces, extra, back_rows, devices // FRAMES
    )

    def array(count):
        return jax.ShapeDtypeStruct((count, lanes), f32)

    iterate, residual, direction, precond = (flat(v) for v in (iterate, residual, direction, precond))
    by_slot = jnp.transpose(send_list, (2, 0, 1))
    filler = -(rows + slot_count) % 8
    listed = jnp.pad(by_slot.astype(f32), ((0, filler), (0, 0), (0, lanes - owners)))
    source = jnp.concatenate([direction.reshape(rows, 1, lanes), listed], axis=0)
    size = half_pieces * piece + extra
    packed = pl.pallas_call(
        functools.partial(
            pack_kernel, (rows, slot_count, piece, params // part, half_pieces), owners, cams, extra
        ),
        out_shape=array(devices * size),
        in_specs=[VMEM],
        out_specs=VMEM,
        scratch_shapes=[
            pltpu.VMEM((-(-2 * size // 8) * 8, lanes), f32),
            pltpu.VMEM((-(-extra // 8) * 8, lanes), f32),
        ],
        compiler_params=asked,
        name="pack",
    )(source.reshape(-1, lanes))
    packed, rigid_nbr, node_refs = lax.optimization_barrier((packed, rigid_nbr, node_refs))
    gathered = exchange(packed, AXES)

    nbr = flat(rigid_nbr)
    joined = jnp.concatenate([direction, residual, precond, nbr.astype(f32)], axis=0)
    sums, *pieces = pl.pallas_call(
        functools.partial(near_kernel, held, piece, rows),
        out_shape=(array(8),) + (array(3 * piece),) * cams,
        in_specs=[VMEM],
        out_specs=(VMEM,) * (1 + cams),
        scratch_shapes=[pltpu.VMEM((rows, lanes), f32)],
        compiler_params=asked,
        name="near",
    )(joined)
    spread, masked = pl.pallas_call(
        functools.partial(masks_kernel, part, half_pieces),
        out_shape=(
            jax.ShapeDtypeStruct((lanes, pixels), f32),
            jax.ShapeDtypeStruct((2 * side, pixels), bf16),
        ),
        in_specs=[VMEM] * 3,
        out_specs=(VMEM,) * 2,
        scratch_shapes=[pltpu.VMEM((4 * HALF, pixels), f32)],
        compiler_params=asked,
        name="masks",
    )(grads, node_refs, skin)
    gathered, spread, sums = lax.optimization_barrier((gathered, spread, sums))
    table, frames, frame_sums = pl.pallas_call(
        functools.partial(table_kernel, sizes),
        out_shape=(array(side), array(cams * piece), array(8)),
        in_specs=[VMEM],
        out_specs=(VMEM,) * 3,
        scratch_shapes=[
            pltpu.SMEM((owners * extra, lanes), f32),
            pltpu.VMEM((owners * extra, lanes), f32),
            pltpu.SemaphoreType.DMA,
        ],
        compiler_params=asked,
        name="table",
    )(gathered)
    other = lax.ppermute(table, "cams", [(c, c ^ 1) for c in range(cams)])
    pulled = pl.pallas_call(
        own_kernel,
        out_shape=jax.ShapeDtypeStruct((lanes, pixels), f32),
        in_specs=[VMEM] * 2,
        out_specs=VMEM,
        compiler_params=asked,
        name="own_half",
    )(table, masked)
    products = pl.pallas_call(
        functools.partial(data_kernel, sizes),
        out_shape=array(devices * back_rows),
        in_specs=[VMEM] * 6,
        out_specs=VMEM,
        scratch_shapes=[pltpu.VMEM((2 * side, lanes), f32)],
        compiler_params=asked,
        name="data_products",
    )(pulled, other, sums, frame_sums, spread, masked)
    products, *pieces = lax.optimization_barrier((products, *pieces))
    received = exchange(products, AXES)
    mine = [pieces[0]]
    for distance in range(1, cams):
        pairs = [(c, (c + distance) % cams) for c in range(cams)]
        mine.append(lax.ppermute(pieces[distance], "cams", pairs))

    scalars, blocks = pl.pallas_call(
        functools.partial(image_kernel, sizes),
        out_shape=(array(8), array(devices * (piece + 1))),
        in_specs=[SMEM] + [VMEM] * (2 + cams),
        out_specs=(VMEM,) * 2,
        scratch_shapes=[pltpu.VMEM((cams * piece, lanes), f32)] * (1 + slot_count),
        compiler_params=asked,
        name="image",
    )(by_slot, received, frames, *mine)
    arrived = exchange(blocks, AXES)
    outs = pl.pallas_call(
        functools.partial(update_kernel, sizes),
        out_shape=(array(rows),) * 3,
        in_specs=[VMEM] * 6,
        out_specs=(VMEM,) * 3,
        compiler_params=asked,
        name="update",
    )(arrived, scalars, iterate, residual, direction, precond)
    return tuple(jnp.transpose(v.reshape(params, held, lanes), (1, 0, 2)) for v in outs)


def solution(mesh):
    split = P(AXES, None, None)
    pixel_split = P(None, AXES)
    in_specs = (split,) * 4 + (P("nodes", None, None),) + (pixel_split,) * 3 + (split,)
    return jax.shard_map(
        on_device, mesh=mesh, in_specs=in_specs, out_specs=(split,) * 3, check_vma=False
    )
```

```python
import functools

import jax
import jax.numpy as jnp
from jax import lax
from jax.experimental import pallas as pl
from jax.experimental.pallas import tpu as pltpu
from jax.sharding import PartitionSpec as P

FRAMES = 8
AXES = ("nodes", "cams")
temporal_weight = 0.5
rigid_weight = 0.1
NN = (((1,), (0,)), ((), ()))
NT = (((1,), (1,)), ((), ()))
LANES = 128
HALF = 8
f32 = jnp.float32
bf16 = jnp.bfloat16

VMEM = pl.BlockSpec(memory_space=pltpu.VMEM)
SMEM = pl.BlockSpec(memory_space=pltpu.SMEM)


def limit(slots, pixels):
    need = 8 * 2**20 + slots * 2 * HALF * pixels * 3
    return pltpu.CompilerParams(vmem_limit_bytes=min(need, 56 * 2**20))


def halves(value):
    high = value.astype(bf16)
    low = (value - high.astype(f32)).astype(bf16)
    return high, low


def rows_sum(value):
    return jnp.sum(value, axis=0, keepdims=True)


def loop(count, body):
    lax.fori_loop(0, count, lambda i, carry: (body(i), carry)[1], 0, unroll=count <= 32)


def pack_kernel(sizes, owners, cams, extra, source, out, halves_of, lists):
    rows, slot_count, piece, pieces, half_pieces = sizes
    half_rows = half_pieces * piece
    lists[...] = jnp.zeros_like(lists)
    for s in range(slot_count):
        row, lane = divmod(s * owners, LANES)
        moved = source[rows + s : rows + s + 1, :]
        if lane:
            moved = pltpu.roll(moved, lane, 1)
        lists[row : row + 1, :] = lists[row : row + 1, :] + moved
    size = half_rows + extra
    halves_of[...] = jnp.zeros_like(halves_of)
    for c in range(pieces):
        at = (c % 2) * size + (c // 2) * piece
        halves_of[at : at + piece, :] = source[c * piece : (c + 1) * piece, :]
    for parity in range(2):
        at = parity * size + half_rows
        halves_of[at : at + extra, :] = lists[0:extra, :]

    def write(owner):
        for c in range(cams):
            at = (c % 2) * size
            out[pl.ds((owner * cams + c) * size, size), :] = halves_of[at : at + size, :]

    loop(owners, write)


def near_kernel(sizes, rows, edges, send_list, joined, sums_out, choose, *pieces):
    owners, cams, slot_count, held, params, part, half_pieces, extra, back_rows, step = sizes
    piece = held * part
    *pieces, near_rows = pieces
    value = joined[0:rows, :]
    left = joined[rows : 2 * rows, :]
    scale = joined[2 * rows : 3 * rows, :]
    high, low = halves(value)
    stack = jnp.concatenate([high.astype(f32), low.astype(f32), jnp.ones((16, LANES), f32)], axis=0)
    stack = stack.astype(bf16)
    node_rows = lax.broadcasted_iota(jnp.int32, (LANES, LANES), 0).astype(f32)
    patch_row = lax.broadcasted_iota(jnp.int32, (rows, LANES), 0) % held
    rigid = jnp.zeros_like(value)
    for q in range(held):
        hits = jnp.zeros((LANES, LANES), f32)
        for r in range(edges):
            at = 3 * rows + r * held + q
            hits = hits + jnp.where(node_rows == joined[at : at + 1, :], 1.0, 0.0)
        hits = hits.astype(bf16)
        pulled = lax.dot_general(stack, hits, NN, preferred_element_type=f32)
        pushed = lax.dot_general(stack, hits, NT, preferred_element_type=f32)
        degree = pushed[2 * rows : 2 * rows + 1]
        both = pulled + pushed
        edge_sum = value * (degree + float(edges)) - (both[:rows] + both[rows : 2 * rows])
        rigid = jnp.where(patch_row == q, edge_sum, rigid)
    near = rigid_weight * rigid + (2.0 * temporal_weight) * value
    near_rows[...] = near
    cam = lax.axis_index("cams")
    for distance, out in enumerate(pieces):
        target = lax.rem(cam + distance, cams) * piece
        offset = jnp.minimum(target, rows - piece)
        out[0:piece, :] = joined[pl.ds(rows + offset, piece), :]
        out[piece : 2 * piece, :] = joined[pl.ds(2 * rows + offset, piece), :]
        out[2 * piece : 3 * piece, :] = near_rows[pl.ds(offset, piece), :]
        if cams * piece > rows:

            @pl.when(target >= rows)
            def _():
                out[...] = jnp.zeros_like(out)

    sums_out[0:1, :] = rows_sum(left * (scale * left))
    sums_out[1:2, :] = rows_sum(value * near)

    column = lax.broadcasted_iota(jnp.int32, (1, choose.shape[1]), 1)
    row = column % back_rows
    slot = column // (back_rows * cams) * slot_count + row // part
    slot = jnp.where(row < slot_count * part, slot, -1)
    listed = jnp.zeros_like(column)
    for owner in range(owners):
        for s in range(slot_count):
            patch = jnp.maximum(send_list[s, 0, owner], 0)
            listed = jnp.where(slot == owner * slot_count + s, patch, listed)
    target = listed // held * piece + row % part * held + listed % held
    target = jnp.where(slot >= 0, target, cams * piece)
    image_row = lax.broadcasted_iota(jnp.int32, choose.shape, 0)
    choose[...] = jnp.where(image_row == target, 1.0, 0.0).astype(bf16)


def masks_kernel(params, refs_count, part, half_pieces, pixel_rows, spread_out, masked, grads_pad):
    pixels = pixel_rows.shape[1]
    side = masked.shape[0] // 2
    chunk = 512
    grads_pad[...] = jnp.zeros_like(grads_pad)
    for c in range(params // part):
        for copy in range(2):
            at = (2 * (c % 2) + copy) * HALF + (c // 2) * part
            grads_pad[at : at + part, :] = pixel_rows[c * part : (c + 1) * part, :]
    node_rows = lax.broadcasted_iota(jnp.int32, (LANES, chunk), 0)
    upper = lax.broadcasted_iota(jnp.int32, (2 * HALF, chunk), 0) // HALF
    for at in range(0, pixels, chunk):
        cols = slice(at, at + chunk)
        weights = pixel_rows[params : params + refs_count, cols]
        refs = pixel_rows[params + refs_count : params + 2 * refs_count, cols].astype(jnp.int32)
        node = lax.bitwise_and(refs, LANES - 1)
        slot_of = lax.shift_right_logical(refs[0:1], 7) - upper
        even, odd = grads_pad[0 : 2 * HALF, cols], grads_pad[2 * HALF :, cols]
        spread = jnp.where(node_rows == node[0:1], weights[0:1], 0.0)
        for k in range(1, refs.shape[0]):
            spread = spread + jnp.where(node_rows == node[k : k + 1], weights[k : k + 1], 0.0)
        spread_out[:, cols] = spread

        def mask(pair):
            here = slot_of == 2 * pair
            rows = pl.multiple_of(2 * HALF * pair, 2 * HALF)
            masked[pl.ds(rows, 2 * HALF), cols] = jnp.where(here, even, 0.0).astype(bf16)
            rows = pl.multiple_of(side + 2 * HALF * pair, 2 * HALF)
            masked[pl.ds(rows, 2 * HALF), cols] = jnp.where(here, odd, 0.0).astype(bf16)

        loop(side // (2 * HALF), mask)


def table_kernel(sizes, gathered, table_out, frames_out, sums_out, lists, list_rows, sem):
    owners, cams, slot_count, held, params, part, half_pieces, extra, back_rows, step = sizes
    devices = owners * cams
    piece = held * part
    half = half_pieces * part
    block_rows = half * held + extra
    receiver = lax.axis_index("nodes")
    cam = lax.axis_index("cams")
    for owner in range(owners):
        at = owner * cams * block_rows + half * held
        list_rows[owner * extra : (owner + 1) * extra, :] = gathered[at : at + extra, :]
    copy = pltpu.make_async_copy(list_rows, lists, sem)
    copy.start()
    table_out[...] = jnp.zeros_like(table_out)
    curvature = jnp.zeros((1, LANES), f32)
    inside = cam * part < params
    offset = jnp.minimum(cam // 2, half_pieces - 1) * piece
    for c in range(cams):
        device = receiver * cams + c
        value = gathered[pl.ds(device * block_rows + offset, piece), :]
        before = gathered[pl.ds(jnp.maximum(device - step, 0) * block_rows + offset, piece), :]
        after = gathered[
            pl.ds(jnp.minimum(device + step, devices - 1) * block_rows + offset, piece), :
        ]
        earlier = jnp.where(jnp.logical_and(inside, device >= step), before, 0.0)
        following = jnp.where(jnp.logical_and(inside, device + step < devices), after, 0.0)
        frames = -temporal_weight * (earlier + following)
        frames_out[c * piece : (c + 1) * piece, :] = frames
        curvature = curvature + rows_sum(value * frames)
    sums_out[0:1, :] = curvature
    copy.wait()

    def fetch(slot):
        owner = slot // slot_count
        entry = (slot % slot_count) * owners + receiver
        listed = lists[owner * extra + entry // LANES, entry % LANES].astype(jnp.int32)
        listed = jnp.maximum(listed, 0)
        device = owner * cams + listed // held
        where = pl.ds(device * block_rows + listed % held, half, stride=held)
        table_out[pl.ds(pl.multiple_of(slot * HALF, HALF), half), :] = gathered[where, :]

    loop(owners * slot_count, fetch)


def pull(table, masked, parity, cols):
    side = masked.shape[0] // 2
    live = masked[pl.ds(pl.multiple_of(parity * side, 2 * HALF), side), cols]
    pulled = lax.dot_general(table, live, NN, preferred_element_type=f32)
    return pulled[:LANES] + pulled[LANES:]


def turned_halves(table):
    return jnp.concatenate(halves(table[...].T), axis=0)


def own_kernel(table, masked, pulled_out):
    parity = lax.rem(lax.axis_index("cams"), 2)
    turned_table = turned_halves(table)
    chunk = 512
    for at in range(0, masked.shape[1], chunk):
        cols = slice(at, at + chunk)
        pulled_out[:, cols] = pull(turned_table, masked, parity, cols)


def data_kernel(sizes, pulled_own, table, near_sums, frame_sums, spread, masked, out, products):
    owners, cams, slot_count, held, params, part, half_pieces, extra, back_rows, step = sizes
    side = masked.shape[0] // 2
    parity = 1 - lax.rem(lax.axis_index("cams"), 2)
    turned_table = turned_halves(table)
    curvature = near_sums[1:2, :] + frame_sums[0:1, :]
    chunk = 512
    for at in range(0, spread.shape[1], chunk):
        cols = slice(at, at + chunk)
        weights = spread[:, cols]
        pulled = pulled_own[:, cols] + pull(turned_table, masked, parity, cols)
        projected = rows_sum(weights * pulled)
        squared = projected * projected
        for lane in range(0, chunk, LANES):
            curvature = curvature + squared[:, lane : lane + LANES]
        both = jnp.concatenate(halves(weights * projected), axis=0)
        back = lax.dot_general(masked[:, cols], both, NT, preferred_element_type=f32)
        back = back[:, :LANES] + back[:, LANES:]
        if at == 0:
            products[...] = back
        else:
            products[...] += back

    middle = LANES // 2
    lane_of = lax.broadcasted_iota(jnp.int32, (1, LANES), 1)
    start = near_sums[0:1, :]
    start = start + pltpu.roll(start, middle, 1)
    curvature = curvature + pltpu.roll(curvature, middle, 1)
    scalars = jnp.where(lane_of < middle, start, curvature)

    def give(owner):
        for c in range(cams):
            base = (owner * cams + c) * back_rows
            for s in range(slot_count):
                if c * part < params:
                    at = (c % 2) * side + (owner * slot_count + s) * HALF + (c // 2) * part
                    value = products[pl.ds(at, part), :]
                else:
                    value = jnp.zeros((part, LANES), f32)
                out[pl.ds(base + s * part, part), :] = value
            out[pl.ds(base + slot_count * part, 1), :] = scalars

    loop(owners, give)


def image_kernel(sizes, choose, received, frames, *refs):
    owners, cams, slot_count, held, params, part, half_pieces, extra, back_rows, step = sizes
    mine, (scalars, blocks, image) = refs[:cams], refs[cams:]
    cam = lax.axis_index("cams")
    piece = held * part
    value = received[...]
    high, rest = halves(value)
    low = (value - high.astype(f32) - rest.astype(f32)).astype(bf16)
    total = sum(
        lax.dot_general(choose[...], term, NN, preferred_element_type=f32)
        for term in (high, rest, low)
    )
    image[...] = total[0 : cams * piece]
    last = total[cams * piece : cams * piece + 1]
    half = LANES // 2
    lane_of = lax.broadcasted_iota(jnp.int32, (1, LANES), 1)
    start = jnp.sum(jnp.where(lane_of < half, last, 0.0), axis=1, keepdims=True)
    curvature = jnp.sum(jnp.where(lane_of < half, 0.0, last), axis=1, keepdims=True)
    length = start / curvature
    norms = jnp.zeros((1, LANES), f32)
    for distance, block in enumerate(mine):
        rows = pl.ds(lax.rem(cam + cams - distance, cams) * piece, piece)
        residual, precond, near = (block[k * piece : (k + 1) * piece, :] for k in range(3))
        value = image[rows, :] + near + frames[rows, :]
        image[rows, :] = value
        left = residual - length * value
        norms = norms + rows_sum(left * (precond * left))
    scalars[0:1, :] = jnp.broadcast_to(start, (1, LANES))
    scalars[1:2, :] = jnp.broadcast_to(length, (1, LANES))

    def tell(owner):
        for c in range(cams):
            base = (owner * cams + c) * (piece + 1)
            blocks[pl.ds(base, 1), :] = norms
            blocks[pl.ds(base + 1, piece), :] = image[c * piece : (c + 1) * piece, :]

    loop(owners, tell)


def update_kernel(
    sizes, arrived, scalars, iterate, residual, direction, precond,
    new_iterate, new_residual, new_direction,
):
    owners, cams, slot_count, held, params, part, half_pieces, extra, back_rows, step = sizes
    piece = held * part
    rows = iterate.shape[0]
    own = lax.axis_index("nodes")
    norms = arrived[0:1, :]
    for device in range(1, owners * cams):
        norms = norms + arrived[device * (piece + 1) : device * (piece + 1) + 1, :]
    start, length = scalars[0:1, :], scalars[1:2, :]
    ratio = jnp.sum(norms, axis=1, keepdims=True) / start
    for c in range(rows // piece):
        here = slice(c * piece, (c + 1) * piece)
        image = arrived[pl.ds((own * cams + c) * (piece + 1) + 1, piece), :]
        value = direction[here, :]
        left = residual[here, :] - length * image
        new_iterate[here, :] = iterate[here, :] + length * value
        new_residual[here, :] = left
        new_direction[here, :] = precond[here, :] * left + ratio * value


def flat(value):
    return jnp.transpose(value, (1, 0, 2)).reshape(-1, value.shape[2])


def joined_rows(parts):
    count = -(-sum(part.shape[0] for part in parts) // 8) * 8
    width = max(part.shape[-1] for part in parts)
    total, at = None, 0
    for part in parts:
        sides = [(at, count - at - part.shape[0], 0)] + [(0, 0, 0)] * (part.ndim - 1)
        sides[-1] = (0, width - part.shape[-1], 0)
        value = lax.pad(part, jnp.zeros((), part.dtype), sides).astype(f32)
        total = value if total is None else total + value
        at += part.shape[0]
    return total


def exchange(blocks, axes):
    rows, lanes = blocks.shape
    peers = lax.axis_size(axes)
    blocks = blocks.reshape(peers, rows // peers, 1, lanes)
    blocks = lax.all_to_all(blocks, axes, split_axis=0, concat_axis=0, tiled=True)
    return blocks.reshape(rows, lanes)


def on_device(iterate, residual, direction, precond, send_list, grads, node_refs, skin, rigid_nbr):
    held, params, lanes = direction.shape
    pixels = grads.shape[1]
    owners = lax.axis_size("nodes")
    cams = lax.axis_size("cams")
    devices = owners * cams
    slot_count = send_list.shape[2]
    slots = owners * slot_count
    asked = limit(slots, pixels)
    rows = held * params
    extra = -(-slots // lanes)
    part = next(n for n in range(1, params + 1) if params % n == 0 and n * cams >= params)
    piece = held * part
    back_rows = slot_count * part + 1
    half_pieces = -(-(params // part) // 2)
    side = (slots + slots % 2) * HALF
    sizes = (
        owners, cams, slot_count, held, params, part, half_pieces, extra, back_rows, devices // FRAMES
    )

    def array(count):
        return jax.ShapeDtypeStruct((count, lanes), f32)

    iterate, residual, direction, precond = (flat(v) for v in (iterate, residual, direction, precond))
    by_slot = jnp.transpose(send_list, (2, 0, 1))
    source = joined_rows((direction.reshape(rows, 1, lanes), by_slot))
    size = half_pieces * piece + extra
    packed = pl.pallas_call(
        functools.partial(
            pack_kernel, (rows, slot_count, piece, params // part, half_pieces), owners, cams, extra
        ),
        out_shape=array(devices * size),
        in_specs=[VMEM],
        out_specs=VMEM,
        scratch_shapes=[
            pltpu.VMEM((-(-2 * size // 8) * 8, lanes), f32),
            pltpu.VMEM((-(-extra // 8) * 8, lanes), f32),
        ],
        compiler_params=asked,
        name="pack",
    )(source.reshape(-1, lanes))
    packed, rigid_nbr, node_refs = lax.optimization_barrier((packed, rigid_nbr, node_refs))
    gathered = exchange(packed, AXES)

    joined = joined_rows(
        [v.reshape(params, held, lanes) for v in (direction, residual, precond)]
        + [jnp.transpose(rigid_nbr, (1, 0, 2))]
    ).reshape(-1, lanes)
    image_rows = -(-(cams * piece + 1) // 16) * 16
    sums, choose, *pieces = pl.pallas_call(
        functools.partial(near_kernel, sizes, rows, rigid_nbr.shape[1]),
        out_shape=(array(8), jax.ShapeDtypeStruct((image_rows, devices * back_rows), bf16))
        + (array(3 * piece),) * cams,
        in_specs=[SMEM, VMEM],
        out_specs=(VMEM,) * (2 + cams),
        scratch_shapes=[pltpu.VMEM((rows, lanes), f32)],
        compiler_params=asked,
        name="near",
    )(by_slot, joined)
    spread, masked = pl.pallas_call(
        functools.partial(masks_kernel, params, node_refs.shape[0], part, half_pieces),
        out_shape=(
            jax.ShapeDtypeStruct((lanes, pixels), f32),
            jax.ShapeDtypeStruct((2 * side, pixels), bf16),
        ),
        in_specs=[VMEM],
        out_specs=(VMEM,) * 2,
        scratch_shapes=[pltpu.VMEM((4 * HALF, pixels), f32)],
        compiler_params=asked,
        name="masks",
    )(joined_rows((grads, skin, node_refs)))
    gathered, spread, sums = lax.optimization_barrier((gathered, spread, sums))
    table, frames, frame_sums = pl.pallas_call(
        functools.partial(table_kernel, sizes),
        out_shape=(array(side), array(cams * piece), array(8)),
        in_specs=[VMEM],
        out_specs=(VMEM,) * 3,
        scratch_shapes=[
            pltpu.SMEM((owners * extra, lanes), f32),
            pltpu.VMEM((owners * extra, lanes), f32),
            pltpu.SemaphoreType.DMA,
        ],
        compiler_params=asked,
        name="table",
    )(gathered)
    other = lax.ppermute(table, "cams", [(c, c ^ 1) for c in range(cams)])
    pulled = pl.pallas_call(
        own_kernel,
        out_shape=jax.ShapeDtypeStruct((lanes, pixels), f32),
        in_specs=[VMEM] * 2,
        out_specs=VMEM,
        compiler_params=asked,
        name="own_half",
    )(table, masked)
    products = pl.pallas_call(
        functools.partial(data_kernel, sizes),
        out_shape=array(devices * back_rows),
        in_specs=[VMEM] * 6,
        out_specs=VMEM,
        scratch_shapes=[pltpu.VMEM((2 * side, lanes), f32)],
        compiler_params=asked,
        name="data_products",
    )(pulled, other, sums, frame_sums, spread, masked)
    products, *pieces = lax.optimization_barrier((products, *pieces))
    received = exchange(products, AXES)
    mine = [pieces[0]]
    for distance in range(1, cams):
        pairs = [(c, (c + distance) % cams) for c in range(cams)]
        mine.append(lax.ppermute(pieces[distance], "cams", pairs))

    scalars, blocks = pl.pallas_call(
        functools.partial(image_kernel, sizes),
        out_shape=(array(8), array(devices * (piece + 1))),
        in_specs=[VMEM] * (3 + cams),
        out_specs=(VMEM,) * 2,
        scratch_shapes=[pltpu.VMEM((cams * piece, lanes), f32)],
        compiler_params=asked,
        name="image",
    )(choose, received, frames, *mine)
    arrived = exchange(blocks, AXES)
    outs = pl.pallas_call(
        functools.partial(update_kernel, sizes),
        out_shape=(array(rows),) * 3,
        in_specs=[VMEM] * 6,
        out_specs=(VMEM,) * 3,
        compiler_params=asked,
        name="update",
    )(arrived, scalars, iterate, residual, direction, precond)
    return tuple(jnp.transpose(v.reshape(params, held, lanes), (1, 0, 2)) for v in outs)


def solution(mesh):
    split = P(AXES, None, None)
    pixel_split = P(None, AXES)
    in_specs = (split,) * 4 + (P("nodes", None, None),) + (pixel_split,) * 3 + (split,)
    return jax.shard_map(
        on_device, mesh=mesh, in_specs=in_specs, out_specs=(split,) * 3, check_vma=False
    )
```

```python
import functools

import jax
import jax.numpy as jnp
from jax import lax
from jax.experimental import pallas as pl
from jax.experimental.pallas import tpu as pltpu
from jax.sharding import PartitionSpec as P

FRAMES = 8
AXES = ("nodes", "cams")
temporal_weight = 0.5
rigid_weight = 0.1
NN = (((1,), (0,)), ((), ()))
NT = (((1,), (1,)), ((), ()))
LANES = 128
HALF = 8
f32 = jnp.float32
bf16 = jnp.bfloat16

VMEM = pl.BlockSpec(memory_space=pltpu.VMEM)
SMEM = pl.BlockSpec(memory_space=pltpu.SMEM)


def limit(slots, pixels):
    need = 8 * 2**20 + slots * 2 * HALF * pixels * 3
    return pltpu.CompilerParams(vmem_limit_bytes=min(need, 56 * 2**20))


def halves(value):
    high = value.astype(bf16)
    low = (value - high.astype(f32)).astype(bf16)
    return high, low


def rows_sum(value):
    return jnp.sum(value, axis=0, keepdims=True)


def loop(count, body):
    lax.fori_loop(0, count, lambda i, carry: (body(i), carry)[1], 0, unroll=count <= 32)


def pack_kernel(sizes, owners, cams, extra, source, out, halves_of, lists):
    rows, slot_count, piece, pieces, half_pieces = sizes
    half_rows = half_pieces * piece
    lists[...] = jnp.zeros_like(lists)
    for s in range(slot_count):
        row, lane = divmod(s * owners, LANES)
        moved = source[rows + s : rows + s + 1, :]
        if lane:
            moved = pltpu.roll(moved, lane, 1)
        lists[row : row + 1, :] = lists[row : row + 1, :] + moved
    size = half_rows + extra
    halves_of[...] = jnp.zeros_like(halves_of)
    for c in range(pieces):
        at = (c % 2) * size + (c // 2) * piece
        halves_of[at : at + piece, :] = source[c * piece : (c + 1) * piece, :]
    for parity in range(2):
        at = parity * size + half_rows
        halves_of[at : at + extra, :] = lists[0:extra, :]

    def write(owner):
        for c in range(cams):
            at = (c % 2) * size
            out[pl.ds((owner * cams + c) * size, size), :] = halves_of[at : at + size, :]

    loop(owners, write)


def near_kernel(sizes, rows, edges, send_list, joined, sums_out, choose, *pieces):
    owners, cams, slot_count, held, params, part, half_pieces, extra, back_rows, step = sizes
    piece = held * part
    *pieces, near_rows = pieces
    value = joined[0:rows, :]
    left = joined[rows : 2 * rows, :]
    scale = joined[2 * rows : 3 * rows, :]
    high, low = halves(value)
    stack = jnp.concatenate([high.astype(f32), low.astype(f32), jnp.ones((16, LANES), f32)], axis=0)
    stack = stack.astype(bf16)
    node_rows = lax.broadcasted_iota(jnp.int32, (LANES, LANES), 0).astype(f32)
    patch_row = lax.broadcasted_iota(jnp.int32, (rows, LANES), 0) % held
    rigid = jnp.zeros_like(value)
    for q in range(held):
        hits = jnp.zeros((LANES, LANES), f32)
        for r in range(edges):
            at = 3 * rows + r * held + q
            hits = hits + jnp.where(node_rows == joined[at : at + 1, :], 1.0, 0.0)
        hits = hits.astype(bf16)
        pulled = lax.dot_general(stack, hits, NN, preferred_element_type=f32)
        pushed = lax.dot_general(stack, hits, NT, preferred_element_type=f32)
        degree = pushed[2 * rows : 2 * rows + 1]
        both = pulled + pushed
        edge_sum = value * (degree + float(edges)) - (both[:rows] + both[rows : 2 * rows])
        rigid = jnp.where(patch_row == q, edge_sum, rigid)
    near = rigid_weight * rigid + (2.0 * temporal_weight) * value
    near_rows[...] = near
    cam = lax.axis_index("cams")
    for distance, out in enumerate(pieces):
        target = lax.rem(cam + distance, cams) * piece
        offset = jnp.minimum(target, rows - piece)
        out[0:piece, :] = joined[pl.ds(rows + offset, piece), :]
        out[piece : 2 * piece, :] = joined[pl.ds(2 * rows + offset, piece), :]
        out[2 * piece : 3 * piece, :] = near_rows[pl.ds(offset, piece), :]
        if cams * piece > rows:

            @pl.when(target >= rows)
            def _():
                out[...] = jnp.zeros_like(out)

    sums_out[0:1, :] = rows_sum(left * (scale * left))
    sums_out[1:2, :] = rows_sum(value * near)

    column = lax.broadcasted_iota(jnp.int32, (1, choose.shape[1]), 1)
    row = column % back_rows
    slot = column // (back_rows * cams) * slot_count + row // part
    slot = jnp.where(row < slot_count * part, slot, -1)
    listed = jnp.zeros_like(column)
    for owner in range(owners):
        for s in range(slot_count):
            patch = jnp.maximum(send_list[s, 0, owner], 0)
            listed = jnp.where(slot == owner * slot_count + s, patch, listed)
    target = listed // held * piece + row % part * held + listed % held
    target = jnp.where(slot >= 0, target, cams * piece)
    image_row = lax.broadcasted_iota(jnp.int32, choose.shape, 0)
    choose[...] = jnp.where(image_row == target, 1.0, 0.0).astype(bf16)


def masks_kernel(params, refs_count, part, half_pieces, pixel_rows, spread_out, masked, grads_pad):
    pixels = pixel_rows.shape[1]
    side = masked.shape[0] // 2
    chunk = 512
    grads_pad[...] = jnp.zeros_like(grads_pad)
    for c in range(params // part):
        for copy in range(2):
            at = (2 * (c % 2) + copy) * HALF + (c // 2) * part
            grads_pad[at : at + part, :] = pixel_rows[c * part : (c + 1) * part, :]
    node_rows = lax.broadcasted_iota(jnp.int32, (LANES, chunk), 0)
    upper = lax.broadcasted_iota(jnp.int32, (2 * HALF, chunk), 0) // HALF
    for at in range(0, pixels, chunk):
        cols = slice(at, at + chunk)
        weights = pixel_rows[params : params + refs_count, cols]
        refs = pixel_rows[params + refs_count : params + 2 * refs_count, cols].astype(jnp.int32)
        node = lax.bitwise_and(refs, LANES - 1)
        slot_of = lax.shift_right_logical(refs[0:1], 7) - upper
        even, odd = grads_pad[0 : 2 * HALF, cols], grads_pad[2 * HALF :, cols]
        spread = jnp.where(node_rows == node[0:1], weights[0:1], 0.0)
        for k in range(1, refs.shape[0]):
            spread = spread + jnp.where(node_rows == node[k : k + 1], weights[k : k + 1], 0.0)
        spread_out[:, cols] = spread

        def mask(pair):
            here = slot_of == 2 * pair
            rows = pl.multiple_of(2 * HALF * pair, 2 * HALF)
            masked[pl.ds(rows, 2 * HALF), cols] = jnp.where(here, even, 0.0).astype(bf16)
            rows = pl.multiple_of(side + 2 * HALF * pair, 2 * HALF)
            masked[pl.ds(rows, 2 * HALF), cols] = jnp.where(here, odd, 0.0).astype(bf16)

        loop(side // (2 * HALF), mask)


def table_kernel(sizes, gathered, table_out, frames_out, sums_out):
    owners, cams, slot_count, held, params, part, half_pieces, extra, back_rows, step = sizes
    devices = owners * cams
    piece = held * part
    half = half_pieces * part
    block_rows = half * held + extra
    receiver = lax.axis_index("nodes")
    cam = lax.axis_index("cams")
    curvature = jnp.zeros((1, LANES), f32)
    inside = cam * part < params
    offset = jnp.minimum(cam // 2, half_pieces - 1) * piece
    for c in range(cams):
        device = receiver * cams + c
        value = gathered[pl.ds(device * block_rows + offset, piece), :]
        before = gathered[pl.ds(jnp.maximum(device - step, 0) * block_rows + offset, piece), :]
        after = gathered[
            pl.ds(jnp.minimum(device + step, devices - 1) * block_rows + offset, piece), :
        ]
        earlier = jnp.where(jnp.logical_and(inside, device >= step), before, 0.0)
        following = jnp.where(jnp.logical_and(inside, device + step < devices), after, 0.0)
        frames = -temporal_weight * (earlier + following)
        frames_out[c * piece : (c + 1) * piece, :] = frames
        curvature = curvature + rows_sum(value * frames)
    sums_out[0:1, :] = curvature

    owner_rows = cams * block_rows
    table_row = lax.broadcasted_iota(jnp.int32, (slot_count * HALF, 1), 0)
    within = table_row % HALF
    lane_of = lax.broadcasted_iota(jnp.int32, (slot_count * HALF, LANES), 1)
    entry = table_row // HALF * owners + receiver
    column = lax.broadcasted_iota(jnp.int32, (slot_count * HALF, owner_rows), 1)
    list_row = [lane_of + line * LANES == entry for line in range(extra)]

    def fetch(owner):
        at = owner * owner_rows
        listed = jnp.zeros((slot_count * HALF, LANES), f32)
        for line in range(extra):
            row = gathered[pl.ds(at + half * held + line, 1), :]
            listed = listed + jnp.where(list_row[line], row, 0.0)
        listed = jnp.maximum(jnp.sum(listed, axis=1, keepdims=True), 0.0).astype(jnp.int32)
        source = listed // held * block_rows + listed % held + within * held
        source = jnp.where(within < half, source, -1)
        choose = jnp.where(column == source, 1.0, 0.0).astype(bf16)
        high, low = halves(gathered[pl.ds(at, owner_rows), :])
        picked = lax.dot_general(choose, high, NN, preferred_element_type=f32)
        picked = picked + lax.dot_general(choose, low, NN, preferred_element_type=f32)
        rows = pl.multiple_of(owner * slot_count * HALF, HALF)
        table_out[pl.ds(rows, slot_count * HALF), :] = picked

    filled = owners * slot_count * HALF
    if table_out.shape[0] > filled:
        table_out[filled:, :] = jnp.zeros((table_out.shape[0] - filled, LANES), f32)
    loop(owners, fetch)


def pull(table, masked, parity, cols):
    side = masked.shape[0] // 2
    live = masked[pl.ds(pl.multiple_of(parity * side, 2 * HALF), side), cols]
    pulled = lax.dot_general(table, live, NN, preferred_element_type=f32)
    return pulled[:LANES] + pulled[LANES:]


def turned_halves(table):
    return jnp.concatenate(halves(table[...].T), axis=0)


def own_kernel(table, masked, pulled_out):
    parity = lax.rem(lax.axis_index("cams"), 2)
    turned_table = turned_halves(table)
    chunk = 512
    for at in range(0, masked.shape[1], chunk):
        cols = slice(at, at + chunk)
        pulled_out[:, cols] = pull(turned_table, masked, parity, cols)


def data_kernel(sizes, pulled_own, table, near_sums, frame_sums, spread, masked, out, products):
    owners, cams, slot_count, held, params, part, half_pieces, extra, back_rows, step = sizes
    side = masked.shape[0] // 2
    parity = 1 - lax.rem(lax.axis_index("cams"), 2)
    turned_table = turned_halves(table)
    curvature = near_sums[1:2, :] + frame_sums[0:1, :]
    chunk = 512
    for at in range(0, spread.shape[1], chunk):
        cols = slice(at, at + chunk)
        weights = spread[:, cols]
        pulled = pulled_own[:, cols] + pull(turned_table, masked, parity, cols)
        projected = rows_sum(weights * pulled)
        squared = projected * projected
        for lane in range(0, chunk, LANES):
            curvature = curvature + squared[:, lane : lane + LANES]
        both = jnp.concatenate(halves(weights * projected), axis=0)
        back = lax.dot_general(masked[:, cols], both, NT, preferred_element_type=f32)
        back = back[:, :LANES] + back[:, LANES:]
        if at == 0:
            products[...] = back
        else:
            products[...] += back

    middle = LANES // 2
    lane_of = lax.broadcasted_iota(jnp.int32, (1, LANES), 1)
    start = near_sums[0:1, :]
    start = start + pltpu.roll(start, middle, 1)
    curvature = curvature + pltpu.roll(curvature, middle, 1)
    scalars = jnp.where(lane_of < middle, start, curvature)

    def give(owner):
        for c in range(cams):
            base = (owner * cams + c) * back_rows
            for s in range(slot_count):
                if c * part < params:
                    at = (c % 2) * side + (owner * slot_count + s) * HALF + (c // 2) * part
                    value = products[pl.ds(at, part), :]
                else:
                    value = jnp.zeros((part, LANES), f32)
                out[pl.ds(base + s * part, part), :] = value
            out[pl.ds(base + slot_count * part, 1), :] = scalars

    loop(owners, give)


def image_kernel(sizes, choose, received, frames, *refs):
    owners, cams, slot_count, held, params, part, half_pieces, extra, back_rows, step = sizes
    mine, (scalars, blocks, image) = refs[:cams], refs[cams:]
    cam = lax.axis_index("cams")
    piece = held * part
    value = received[...]
    high, rest = halves(value)
    low = (value - high.astype(f32) - rest.astype(f32)).astype(bf16)
    total = sum(
        lax.dot_general(choose[...], term, NN, preferred_element_type=f32)
        for term in (high, rest, low)
    )
    image[...] = total[0 : cams * piece]
    last = total[cams * piece : cams * piece + 1]
    half = LANES // 2
    lane_of = lax.broadcasted_iota(jnp.int32, (1, LANES), 1)
    start = jnp.sum(jnp.where(lane_of < half, last, 0.0), axis=1, keepdims=True)
    curvature = jnp.sum(jnp.where(lane_of < half, 0.0, last), axis=1, keepdims=True)
    length = start / curvature
    norms = jnp.zeros((1, LANES), f32)
    for distance, block in enumerate(mine):
        rows = pl.ds(lax.rem(cam + cams - distance, cams) * piece, piece)
        residual, precond, near = (block[k * piece : (k + 1) * piece, :] for k in range(3))
        value = image[rows, :] + near + frames[rows, :]
        image[rows, :] = value
        left = residual - length * value
        norms = norms + rows_sum(left * (precond * left))
    scalars[0:1, :] = jnp.broadcast_to(start, (1, LANES))
    scalars[1:2, :] = jnp.broadcast_to(length, (1, LANES))

    def tell(owner):
        for c in range(cams):
            base = (owner * cams + c) * (piece + 1)
            blocks[pl.ds(base, 1), :] = norms
            blocks[pl.ds(base + 1, piece), :] = image[c * piece : (c + 1) * piece, :]

    loop(owners, tell)


def update_kernel(
    sizes, arrived, scalars, iterate, residual, direction, precond,
    new_iterate, new_residual, new_direction,
):
    owners, cams, slot_count, held, params, part, half_pieces, extra, back_rows, step = sizes
    piece = held * part
    rows = iterate.shape[0]
    own = lax.axis_index("nodes")
    norms = arrived[0:1, :]
    for device in range(1, owners * cams):
        norms = norms + arrived[device * (piece + 1) : device * (piece + 1) + 1, :]
    start, length = scalars[0:1, :], scalars[1:2, :]
    ratio = jnp.sum(norms, axis=1, keepdims=True) / start
    for c in range(rows // piece):
        here = slice(c * piece, (c + 1) * piece)
        image = arrived[pl.ds((own * cams + c) * (piece + 1) + 1, piece), :]
        value = direction[here, :]
        left = residual[here, :] - length * image
        new_iterate[here, :] = iterate[here, :] + length * value
        new_residual[here, :] = left
        new_direction[here, :] = precond[here, :] * left + ratio * value


def flat(value):
    return jnp.transpose(value, (1, 0, 2)).reshape(-1, value.shape[2])


def joined_rows(parts):
    count = -(-sum(part.shape[0] for part in parts) // 8) * 8
    width = max(part.shape[-1] for part in parts)
    total, at = None, 0
    for part in parts:
        sides = [(at, count - at - part.shape[0], 0)] + [(0, 0, 0)] * (part.ndim - 1)
        sides[-1] = (0, width - part.shape[-1], 0)
        value = lax.pad(part, jnp.zeros((), part.dtype), sides).astype(f32)
        total = value if total is None else total + value
        at += part.shape[0]
    return total


def exchange(blocks, axes):
    rows, lanes = blocks.shape
    peers = lax.axis_size(axes)
    blocks = blocks.reshape(peers, rows // peers, 1, lanes)
    blocks = lax.all_to_all(blocks, axes, split_axis=0, concat_axis=0, tiled=True)
    return blocks.reshape(rows, lanes)


def on_device(iterate, residual, direction, precond, send_list, grads, node_refs, skin, rigid_nbr):
    held, params, lanes = direction.shape
    pixels = grads.shape[1]
    owners = lax.axis_size("nodes")
    cams = lax.axis_size("cams")
    devices = owners * cams
    slot_count = send_list.shape[2]
    slots = owners * slot_count
    asked = limit(slots, pixels)
    rows = held * params
    extra = -(-slots // lanes)
    part = next(n for n in range(1, params + 1) if params % n == 0 and n * cams >= params)
    piece = held * part
    back_rows = slot_count * part + 1
    half_pieces = -(-(params // part) // 2)
    side = (slots + slots % 2) * HALF
    sizes = (
        owners, cams, slot_count, held, params, part, half_pieces, extra, back_rows, devices // FRAMES
    )

    def array(count):
        return jax.ShapeDtypeStruct((count, lanes), f32)

    iterate, residual, direction, precond = (flat(v) for v in (iterate, residual, direction, precond))
    by_slot = jnp.transpose(send_list, (2, 0, 1))
    source = joined_rows((direction.reshape(rows, 1, lanes), by_slot))
    size = half_pieces * piece + extra
    packed = pl.pallas_call(
        functools.partial(
            pack_kernel, (rows, slot_count, piece, params // part, half_pieces), owners, cams, extra
        ),
        out_shape=array(devices * size),
        in_specs=[VMEM],
        out_specs=VMEM,
        scratch_shapes=[
            pltpu.VMEM((-(-2 * size // 8) * 8, lanes), f32),
            pltpu.VMEM((-(-extra // 8) * 8, lanes), f32),
        ],
        compiler_params=asked,
        name="pack",
    )(source.reshape(-1, lanes))
    packed, rigid_nbr, node_refs = lax.optimization_barrier((packed, rigid_nbr, node_refs))
    gathered = exchange(packed, AXES)

    joined = joined_rows(
        [v.reshape(params, held, lanes) for v in (direction, residual, precond)]
        + [jnp.transpose(rigid_nbr, (1, 0, 2))]
    ).reshape(-1, lanes)
    image_rows = -(-(cams * piece + 1) // 16) * 16
    sums, choose, *pieces = pl.pallas_call(
        functools.partial(near_kernel, sizes, rows, rigid_nbr.shape[1]),
        out_shape=(array(8), jax.ShapeDtypeStruct((image_rows, devices * back_rows), bf16))
        + (array(3 * piece),) * cams,
        in_specs=[SMEM, VMEM],
        out_specs=(VMEM,) * (2 + cams),
        scratch_shapes=[pltpu.VMEM((rows, lanes), f32)],
        compiler_params=asked,
        name="near",
    )(by_slot, joined)
    spread, masked = pl.pallas_call(
        functools.partial(masks_kernel, params, node_refs.shape[0], part, half_pieces),
        out_shape=(
            jax.ShapeDtypeStruct((lanes, pixels), f32),
            jax.ShapeDtypeStruct((2 * side, pixels), bf16),
        ),
        in_specs=[VMEM],
        out_specs=(VMEM,) * 2,
        scratch_shapes=[pltpu.VMEM((4 * HALF, pixels), f32)],
        compiler_params=asked,
        name="masks",
    )(joined_rows((grads, skin, node_refs)))
    spread, *pieces = lax.optimization_barrier((spread, *pieces))
    mine = [pieces[0]]
    for distance in range(1, cams):
        turn = [(c, (c + distance) % cams) for c in range(cams)]
        mine.append(lax.ppermute(pieces[distance], "cams", turn))
    gathered, spread, sums, *mine = lax.optimization_barrier((gathered, spread, sums, *mine))
    table, frames, frame_sums = pl.pallas_call(
        functools.partial(table_kernel, sizes),
        out_shape=(array(side), array(cams * piece), array(8)),
        in_specs=[VMEM],
        out_specs=(VMEM,) * 3,
        compiler_params=asked,
        name="table",
    )(gathered)
    other = lax.ppermute(table, "cams", [(c, c ^ 1) for c in range(cams)])
    pulled = pl.pallas_call(
        own_kernel,
        out_shape=jax.ShapeDtypeStruct((lanes, pixels), f32),
        in_specs=[VMEM] * 2,
        out_specs=VMEM,
        compiler_params=asked,
        name="own_half",
    )(table, masked)
    products = pl.pallas_call(
        functools.partial(data_kernel, sizes),
        out_shape=array(devices * back_rows),
        in_specs=[VMEM] * 6,
        out_specs=VMEM,
        scratch_shapes=[pltpu.VMEM((2 * side, lanes), f32)],
        compiler_params=asked,
        name="data_products",
    )(pulled, other, sums, frame_sums, spread, masked)
    received = exchange(products, AXES)

    scalars, blocks = pl.pallas_call(
        functools.partial(image_kernel, sizes),
        out_shape=(array(8), array(devices * (piece + 1))),
        in_specs=[VMEM] * (3 + cams),
        out_specs=(VMEM,) * 2,
        scratch_shapes=[pltpu.VMEM((cams * piece, lanes), f32)],
        compiler_params=asked,
        name="image",
    )(choose, received, frames, *mine)
    arrived = exchange(blocks, AXES)
    outs = pl.pallas_call(
        functools.partial(update_kernel, sizes),
        out_shape=(array(rows),) * 3,
        in_specs=[VMEM] * 6,
        out_specs=(VMEM,) * 3,
        compiler_params=asked,
        name="update",
    )(arrived, scalars, iterate, residual, direction, precond)
    return tuple(jnp.transpose(v.reshape(params, held, lanes), (1, 0, 2)) for v in outs)


def solution(mesh):
    split = P(AXES, None, None)
    pixel_split = P(None, AXES)
    in_specs = (split,) * 4 + (P("nodes", None, None),) + (pixel_split,) * 3 + (split,)
    return jax.shard_map(
        on_device, mesh=mesh, in_specs=in_specs, out_specs=(split,) * 3, check_vma=False
    )
```

```python
import functools

import jax
import jax.numpy as jnp
from jax import lax
from jax.experimental import pallas as pl
from jax.experimental.pallas import tpu as pltpu
from jax.sharding import PartitionSpec as P

FRAMES = 8
AXES = ("nodes", "cams")
temporal_weight = 0.5
rigid_weight = 0.1
NN = (((1,), (0,)), ((), ()))
NT = (((1,), (1,)), ((), ()))
LANES = 128
HALF = 8
f32 = jnp.float32
bf16 = jnp.bfloat16

VMEM = pl.BlockSpec(memory_space=pltpu.VMEM)
SMEM = pl.BlockSpec(memory_space=pltpu.SMEM)


def limit(slots, pixels):
    need = 8 * 2**20 + slots * 2 * HALF * pixels * 3
    return pltpu.CompilerParams(vmem_limit_bytes=min(need, 56 * 2**20))


def halves(value):
    high = value.astype(bf16)
    low = (value - high.astype(f32)).astype(bf16)
    return high, low


def rows_sum(value):
    return jnp.sum(value, axis=0, keepdims=True)


def loop(count, body):
    lax.fori_loop(0, count, lambda i, carry: (body(i), carry)[1], 0, unroll=count <= 32)


def pack_kernel(sizes, owners, cams, extra, source, out, halves_of, lists):
    rows, slot_count, piece, pieces, half_pieces = sizes
    half_rows = half_pieces * piece
    lists[...] = jnp.zeros_like(lists)
    for s in range(slot_count):
        row, lane = divmod(s * owners, LANES)
        moved = source[rows + s : rows + s + 1, :]
        if lane:
            moved = pltpu.roll(moved, lane, 1)
        lists[row : row + 1, :] = lists[row : row + 1, :] + moved
    size = half_rows + extra
    halves_of[...] = jnp.zeros_like(halves_of)
    for c in range(pieces):
        at = (c % 2) * size + (c // 2) * piece
        halves_of[at : at + piece, :] = source[c * piece : (c + 1) * piece, :]
    for parity in range(2):
        at = parity * size + half_rows
        halves_of[at : at + extra, :] = lists[0:extra, :]

    def write(owner):
        for c in range(cams):
            at = (c % 2) * size
            out[pl.ds((owner * cams + c) * size, size), :] = halves_of[at : at + size, :]

    loop(owners, write)


def near_kernel(sizes, rows, edges, send_list, joined, sums_out, choose, *pieces):
    owners, cams, slot_count, held, params, part, half_pieces, extra, back_rows, step = sizes
    piece = held * part
    *pieces, near_rows = pieces
    value = joined[0:rows, :]
    left = joined[rows : 2 * rows, :]
    scale = joined[2 * rows : 3 * rows, :]
    high, low = halves(value)
    stack = jnp.concatenate([high.astype(f32), low.astype(f32), jnp.ones((16, LANES), f32)], axis=0)
    stack = stack.astype(bf16)
    node_rows = lax.broadcasted_iota(jnp.int32, (LANES, LANES), 0).astype(f32)
    patch_row = lax.broadcasted_iota(jnp.int32, (rows, LANES), 0) % held
    rigid = jnp.zeros_like(value)
    for q in range(held):
        hits = jnp.zeros((LANES, LANES), f32)
        for r in range(edges):
            at = 3 * rows + r * held + q
            hits = hits + jnp.where(node_rows == joined[at : at + 1, :], 1.0, 0.0)
        hits = hits.astype(bf16)
        pulled = lax.dot_general(stack, hits, NN, preferred_element_type=f32)
        pushed = lax.dot_general(stack, hits, NT, preferred_element_type=f32)
        degree = pushed[2 * rows : 2 * rows + 1]
        both = pulled + pushed
        edge_sum = value * (degree + float(edges)) - (both[:rows] + both[rows : 2 * rows])
        rigid = jnp.where(patch_row == q, edge_sum, rigid)
    near = rigid_weight * rigid + (2.0 * temporal_weight) * value
    near_rows[...] = near
    cam = lax.axis_index("cams")
    for distance, out in enumerate(pieces):
        target = lax.rem(cam + distance, cams) * piece
        offset = jnp.minimum(target, rows - piece)
        out[0:piece, :] = joined[pl.ds(rows + offset, piece), :]
        out[piece : 2 * piece, :] = joined[pl.ds(2 * rows + offset, piece), :]
        out[2 * piece : 3 * piece, :] = near_rows[pl.ds(offset, piece), :]
        if cams * piece > rows:

            @pl.when(target >= rows)
            def _():
                out[...] = jnp.zeros_like(out)

    sums_out[0:1, :] = rows_sum(left * (scale * left))
    sums_out[1:2, :] = rows_sum(value * near)

    column = lax.broadcasted_iota(jnp.int32, (1, choose.shape[1]), 1)
    row = column % back_rows
    slot = column // (back_rows * cams) * slot_count + row // part
    listed = jnp.zeros_like(column)
    for owner in range(owners):
        for s in range(slot_count):
            patch = jnp.maximum(send_list[s, 0, owner], 0)
            listed = jnp.where(slot == owner * slot_count + s, patch, listed)
    target = listed // held * piece + row % part * held + listed % held
    image_row = lax.broadcasted_iota(jnp.int32, choose.shape, 0)
    choose[...] = jnp.where(image_row == target, 1.0, 0.0).astype(bf16)


def masks_kernel(params, refs_count, part, half_pieces, pixel_rows, spread_out, masked, grads_pad):
    pixels = pixel_rows.shape[1]
    side = masked.shape[0] // 2
    chunk = 512
    grads_pad[...] = jnp.zeros_like(grads_pad)
    for c in range(params // part):
        for copy in range(2):
            at = (2 * (c % 2) + copy) * HALF + (c // 2) * part
            grads_pad[at : at + part, :] = pixel_rows[c * part : (c + 1) * part, :]
    node_rows = lax.broadcasted_iota(jnp.int32, (LANES, chunk), 0)
    upper = lax.broadcasted_iota(jnp.int32, (2 * HALF, chunk), 0) // HALF
    for at in range(0, pixels, chunk):
        cols = slice(at, at + chunk)
        weights = pixel_rows[params : params + refs_count, cols]
        refs = pixel_rows[params + refs_count : params + 2 * refs_count, cols].astype(jnp.int32)
        node = lax.bitwise_and(refs, LANES - 1)
        slot_of = lax.shift_right_logical(refs[0:1], 7) - upper
        even, odd = grads_pad[0 : 2 * HALF, cols], grads_pad[2 * HALF :, cols]
        spread = jnp.where(node_rows == node[0:1], weights[0:1], 0.0)
        for k in range(1, refs.shape[0]):
            spread = spread + jnp.where(node_rows == node[k : k + 1], weights[k : k + 1], 0.0)
        spread_out[:, cols] = spread

        def mask(pair):
            here = slot_of == 2 * pair
            rows = pl.multiple_of(2 * HALF * pair, 2 * HALF)
            masked[pl.ds(rows, 2 * HALF), cols] = jnp.where(here, even, 0.0).astype(bf16)
            rows = pl.multiple_of(side + 2 * HALF * pair, 2 * HALF)
            masked[pl.ds(rows, 2 * HALF), cols] = jnp.where(here, odd, 0.0).astype(bf16)

        loop(side // (2 * HALF), mask)


def table_kernel(sizes, gathered, table_out, frames_out, sums_out):
    owners, cams, slot_count, held, params, part, half_pieces, extra, back_rows, step = sizes
    devices = owners * cams
    piece = held * part
    half = half_pieces * part
    block_rows = half * held + extra
    receiver = lax.axis_index("nodes")
    cam = lax.axis_index("cams")
    curvature = jnp.zeros((1, LANES), f32)
    inside = cam * part < params
    offset = jnp.minimum(cam // 2, half_pieces - 1) * piece
    for c in range(cams):
        device = receiver * cams + c
        value = gathered[pl.ds(device * block_rows + offset, piece), :]
        before = gathered[pl.ds(jnp.maximum(device - step, 0) * block_rows + offset, piece), :]
        after = gathered[
            pl.ds(jnp.minimum(device + step, devices - 1) * block_rows + offset, piece), :
        ]
        earlier = jnp.where(jnp.logical_and(inside, device >= step), before, 0.0)
        following = jnp.where(jnp.logical_and(inside, device + step < devices), after, 0.0)
        frames = -temporal_weight * (earlier + following)
        frames_out[c * piece : (c + 1) * piece, :] = frames
        curvature = curvature + rows_sum(value * frames)
    sums_out[0:1, :] = curvature

    owner_rows = cams * block_rows
    table_row = lax.broadcasted_iota(jnp.int32, (slot_count * HALF, 1), 0)
    within = table_row % HALF
    lane_of = lax.broadcasted_iota(jnp.int32, (slot_count * HALF, LANES), 1)
    entry = table_row // HALF * owners + receiver
    column = lax.broadcasted_iota(jnp.int32, (slot_count * HALF, owner_rows), 1)
    list_row = [lane_of + line * LANES == entry for line in range(extra)]

    def fetch(owner):
        at = owner * owner_rows
        listed = jnp.zeros((slot_count * HALF, LANES), f32)
        for line in range(extra):
            row = gathered[pl.ds(at + half * held + line, 1), :]
            listed = listed + jnp.where(list_row[line], row, 0.0)
        listed = jnp.maximum(jnp.sum(listed, axis=1, keepdims=True), 0.0).astype(jnp.int32)
        source = listed // held * block_rows + listed % held + within * held
        source = jnp.where(within < half, source, -1)
        choose = jnp.where(column == source, 1.0, 0.0).astype(bf16)
        high, low = halves(gathered[pl.ds(at, owner_rows), :])
        picked = lax.dot_general(choose, high, NN, preferred_element_type=f32)
        picked = picked + lax.dot_general(choose, low, NN, preferred_element_type=f32)
        rows = pl.multiple_of(owner * slot_count * HALF, HALF)
        table_out[pl.ds(rows, slot_count * HALF), :] = picked

    filled = owners * slot_count * HALF
    if table_out.shape[0] > filled:
        table_out[filled:, :] = jnp.zeros((table_out.shape[0] - filled, LANES), f32)
    loop(owners, fetch)


def pull(table, masked, parity, cols):
    side = masked.shape[0] // 2
    live = masked[pl.ds(pl.multiple_of(parity * side, 2 * HALF), side), cols]
    pulled = lax.dot_general(table, live, NN, preferred_element_type=f32)
    return pulled[:LANES] + pulled[LANES:]


def turned_halves(table):
    return jnp.concatenate(halves(table[...].T), axis=0)


def own_kernel(table, masked, pulled_out):
    parity = lax.rem(lax.axis_index("cams"), 2)
    turned_table = turned_halves(table)
    chunk = 512
    for at in range(0, masked.shape[1], chunk):
        cols = slice(at, at + chunk)
        pulled_out[:, cols] = pull(turned_table, masked, parity, cols)


def data_kernel(sizes, pulled_own, table, spread, masked, out, squares_out, products):
    owners, cams, slot_count, held, params, part, half_pieces, extra, back_rows, step = sizes
    side = masked.shape[0] // 2
    parity = 1 - lax.rem(lax.axis_index("cams"), 2)
    turned_table = turned_halves(table)
    squares = jnp.zeros((1, LANES), f32)
    chunk = 512
    for at in range(0, spread.shape[1], chunk):
        cols = slice(at, at + chunk)
        weights = spread[:, cols]
        pulled = pulled_own[:, cols] + pull(turned_table, masked, parity, cols)
        projected = rows_sum(weights * pulled)
        squared = projected * projected
        for lane in range(0, chunk, LANES):
            squares = squares + squared[:, lane : lane + LANES]
        both = jnp.concatenate(halves(weights * projected), axis=0)
        back = lax.dot_general(masked[:, cols], both, NT, preferred_element_type=f32)
        back = back[:, :LANES] + back[:, LANES:]
        if at == 0:
            products[...] = back
        else:
            products[...] += back

    squares_out[0:1, :] = squares

    def give(owner):
        for c in range(cams):
            base = (owner * cams + c) * back_rows
            for s in range(slot_count):
                if c * part < params:
                    at = (c % 2) * side + (owner * slot_count + s) * HALF + (c // 2) * part
                    value = products[pl.ds(at, part), :]
                else:
                    value = jnp.zeros((part, LANES), f32)
                out[pl.ds(base + s * part, part), :] = value

    loop(owners, give)


def image_kernel(sizes, choose, received, frames, near_sums, frame_sums, squares, *refs):
    owners, cams, slot_count, held, params, part, half_pieces, extra, back_rows, step = sizes
    mine, (blocks, image) = refs[:cams], refs[cams:]
    cam = lax.axis_index("cams")
    piece = held * part
    value = received[...]
    high, rest = halves(value)
    low = (value - high.astype(f32) - rest.astype(f32)).astype(bf16)
    total = sum(
        lax.dot_general(choose[...], term, NN, preferred_element_type=f32)
        for term in (high, rest, low)
    )
    image[...] = total[0 : cams * piece] + frames[...]
    cross = jnp.zeros((1, LANES), f32)
    square = jnp.zeros((1, LANES), f32)
    for distance, block in enumerate(mine):
        rows = pl.ds(lax.rem(cam + cams - distance, cams) * piece, piece)
        residual, precond, near = (block[k * piece : (k + 1) * piece, :] for k in range(3))
        value = image[rows, :] + near
        image[rows, :] = value
        cross = cross + rows_sum(value * (precond * residual))
        square = square + rows_sum(value * (precond * value))
    curvature = near_sums[1:2, :] + frame_sums[0:1, :] + squares[0:1, :]
    lane_of = lax.broadcasted_iota(jnp.int32, (1, LANES), 1)
    scalars = jnp.zeros((1, LANES), f32)
    for k, row in enumerate((near_sums[0:1, :], curvature, cross, square)):
        scalars = jnp.where(lane_of == k, jnp.sum(row, axis=1, keepdims=True), scalars)

    def tell(owner):
        for c in range(cams):
            base = (owner * cams + c) * (piece + 1)
            blocks[pl.ds(base, 1), :] = scalars
            blocks[pl.ds(base + 1, piece), :] = image[c * piece : (c + 1) * piece, :]

    loop(owners, tell)


def update_kernel(
    sizes, arrived, iterate, residual, direction, precond,
    new_iterate, new_residual, new_direction,
):
    owners, cams, slot_count, held, params, part, half_pieces, extra, back_rows, step = sizes
    piece = held * part
    rows = iterate.shape[0]
    own = lax.axis_index("nodes")
    scalars = arrived[0:1, :]
    for device in range(1, owners * cams):
        scalars = scalars + arrived[device * (piece + 1) : device * (piece + 1) + 1, :]
    lane_of = lax.broadcasted_iota(jnp.int32, (1, LANES), 1)
    start, curvature, cross, square = (
        jnp.sum(jnp.where(lane_of == k, scalars, 0.0), axis=1, keepdims=True) for k in range(4)
    )
    length = start / curvature
    norm = start - 2.0 * length * cross + length * length * square
    ratio = norm / start
    for c in range(rows // piece):
        here = slice(c * piece, (c + 1) * piece)
        image = arrived[pl.ds((own * cams + c) * (piece + 1) + 1, piece), :]
        value = direction[here, :]
        left = residual[here, :] - length * image
        new_iterate[here, :] = iterate[here, :] + length * value
        new_residual[here, :] = left
        new_direction[here, :] = precond[here, :] * left + ratio * value


def flat(value):
    return jnp.transpose(value, (1, 0, 2)).reshape(-1, value.shape[2])


def joined_rows(parts):
    count = -(-sum(part.shape[0] for part in parts) // 8) * 8
    width = max(part.shape[-1] for part in parts)
    total, at = None, 0
    for part in parts:
        sides = [(at, count - at - part.shape[0], 0)] + [(0, 0, 0)] * (part.ndim - 1)
        sides[-1] = (0, width - part.shape[-1], 0)
        value = lax.pad(part, jnp.zeros((), part.dtype), sides).astype(f32)
        total = value if total is None else total + value
        at += part.shape[0]
    return total


def exchange(blocks, axes):
    rows, lanes = blocks.shape
    peers = lax.axis_size(axes)
    blocks = blocks.reshape(peers, rows // peers, 1, lanes)
    blocks = lax.all_to_all(blocks, axes, split_axis=0, concat_axis=0, tiled=True)
    return blocks.reshape(rows, lanes)


def on_device(iterate, residual, direction, precond, send_list, grads, node_refs, skin, rigid_nbr):
    held, params, lanes = direction.shape
    pixels = grads.shape[1]
    owners = lax.axis_size("nodes")
    cams = lax.axis_size("cams")
    devices = owners * cams
    slot_count = send_list.shape[2]
    slots = owners * slot_count
    asked = limit(slots, pixels)
    rows = held * params
    extra = -(-slots // lanes)
    part = next(n for n in range(1, params + 1) if params % n == 0 and n * cams >= params)
    piece = held * part
    back_rows = slot_count * part
    half_pieces = -(-(params // part) // 2)
    side = (slots + slots % 2) * HALF
    sizes = (
        owners, cams, slot_count, held, params, part, half_pieces, extra, back_rows, devices // FRAMES
    )

    def array(count):
        return jax.ShapeDtypeStruct((count, lanes), f32)

    iterate, residual, direction, precond = (flat(v) for v in (iterate, residual, direction, precond))
    by_slot = jnp.transpose(send_list, (2, 0, 1))
    source = joined_rows((direction.reshape(rows, 1, lanes), by_slot))
    size = half_pieces * piece + extra
    packed = pl.pallas_call(
        functools.partial(
            pack_kernel, (rows, slot_count, piece, params // part, half_pieces), owners, cams, extra
        ),
        out_shape=array(devices * size),
        in_specs=[VMEM],
        out_specs=VMEM,
        scratch_shapes=[
            pltpu.VMEM((-(-2 * size // 8) * 8, lanes), f32),
            pltpu.VMEM((-(-extra // 8) * 8, lanes), f32),
        ],
        compiler_params=asked,
        name="pack",
    )(source.reshape(-1, lanes))
    packed, rigid_nbr, node_refs = lax.optimization_barrier((packed, rigid_nbr, node_refs))
    gathered = exchange(packed, AXES)

    joined = joined_rows(
        [v.reshape(params, held, lanes) for v in (direction, residual, precond)]
        + [jnp.transpose(rigid_nbr, (1, 0, 2))]
    ).reshape(-1, lanes)
    image_rows = -(-cams * piece // 16) * 16
    sums, choose, *pieces = pl.pallas_call(
        functools.partial(near_kernel, sizes, rows, rigid_nbr.shape[1]),
        out_shape=(array(8), jax.ShapeDtypeStruct((image_rows, devices * back_rows), bf16))
        + (array(3 * piece),) * cams,
        in_specs=[SMEM, VMEM],
        out_specs=(VMEM,) * (2 + cams),
        scratch_shapes=[pltpu.VMEM((rows, lanes), f32)],
        compiler_params=asked,
        name="near",
    )(by_slot, joined)
    spread, masked = pl.pallas_call(
        functools.partial(masks_kernel, params, node_refs.shape[0], part, half_pieces),
        out_shape=(
            jax.ShapeDtypeStruct((lanes, pixels), f32),
            jax.ShapeDtypeStruct((2 * side, pixels), bf16),
        ),
        in_specs=[VMEM],
        out_specs=(VMEM,) * 2,
        scratch_shapes=[pltpu.VMEM((4 * HALF, pixels), f32)],
        compiler_params=asked,
        name="masks",
    )(joined_rows((grads, skin, node_refs)))
    gathered, spread, sums = lax.optimization_barrier((gathered, spread, sums))
    table, frames, frame_sums = pl.pallas_call(
        functools.partial(table_kernel, sizes),
        out_shape=(array(side), array(cams * piece), array(8)),
        in_specs=[VMEM],
        out_specs=(VMEM,) * 3,
        compiler_params=asked,
        name="table",
    )(gathered)
    other = lax.ppermute(table, "cams", [(c, c ^ 1) for c in range(cams)])
    pulled = pl.pallas_call(
        own_kernel,
        out_shape=jax.ShapeDtypeStruct((lanes, pixels), f32),
        in_specs=[VMEM] * 2,
        out_specs=VMEM,
        compiler_params=asked,
        name="own_half",
    )(table, masked)
    products, squares = pl.pallas_call(
        functools.partial(data_kernel, sizes),
        out_shape=(array(devices * back_rows), array(8)),
        in_specs=[VMEM] * 4,
        out_specs=(VMEM,) * 2,
        scratch_shapes=[pltpu.VMEM((2 * side, lanes), f32)],
        compiler_params=asked,
        name="data_products",
    )(pulled, other, spread, masked)
    products, *pieces = lax.optimization_barrier((products, *pieces))
    received = exchange(products, AXES)
    mine = [pieces[0]]
    for distance in range(1, cams):
        turn = [(c, (c + distance) % cams) for c in range(cams)]
        mine.append(lax.ppermute(pieces[distance], "cams", turn))

    blocks = pl.pallas_call(
        functools.partial(image_kernel, sizes),
        out_shape=array(devices * (piece + 1)),
        in_specs=[VMEM] * (6 + cams),
        out_specs=VMEM,
        scratch_shapes=[pltpu.VMEM((cams * piece, lanes), f32)],
        compiler_params=asked,
        name="image",
    )(choose, received, frames, sums, frame_sums, squares, *mine)
    arrived = exchange(blocks, AXES)
    outs = pl.pallas_call(
        functools.partial(update_kernel, sizes),
        out_shape=(array(rows),) * 3,
        in_specs=[VMEM] * 5,
        out_specs=(VMEM,) * 3,
        compiler_params=asked,
        name="update",
    )(arrived, iterate, residual, direction, precond)
    return tuple(jnp.transpose(v.reshape(params, held, lanes), (1, 0, 2)) for v in outs)


def solution(mesh):
    split = P(AXES, None, None)
    pixel_split = P(None, AXES)
    in_specs = (split,) * 4 + (P("nodes", None, None),) + (pixel_split,) * 3 + (split,)
    return jax.shard_map(
        on_device, mesh=mesh, in_specs=in_specs, out_specs=(split,) * 3, check_vma=False
    )
```

```python
import dataclasses
import functools

import jax
import jax.numpy as jnp
from jax import lax
from jax.experimental import pallas as pl
from jax.experimental.pallas import tpu as pltpu
from jax.sharding import PartitionSpec as P

FRAMES = 8
AXES = ("nodes", "cams")
temporal_weight = 0.5
rigid_weight = 0.1
NN = (((1,), (0,)), ((), ()))
NT = (((1,), (1,)), ((), ()))
LANES = 128
HALF = 8
f32 = jnp.float32
bf16 = jnp.bfloat16

VMEM = pl.BlockSpec(memory_space=pltpu.VMEM)
SMEM = pl.BlockSpec(memory_space=pltpu.SMEM)


def limit(slots, pixels):
    need = 8 * 2**20 + slots * 2 * HALF * pixels * 3
    return pltpu.CompilerParams(vmem_limit_bytes=min(need, 56 * 2**20))


def halves(value):
    high = value.astype(bf16)
    low = (value - high.astype(f32)).astype(bf16)
    return high, low


def rows_sum(value):
    return jnp.sum(value, axis=0, keepdims=True)


def loop(count, body):
    lax.fori_loop(0, count, lambda i, carry: (body(i), carry)[1], 0, unroll=count <= 32)


def pack_kernel(sizes, owners, cams, extra, source, out, halves_of, lists):
    rows, slot_count, piece, pieces, half_pieces = sizes
    half_rows = half_pieces * piece
    lists[...] = jnp.zeros_like(lists)
    for s in range(slot_count):
        row, lane = divmod(s * owners, LANES)
        moved = source[rows + s]
        if lane:
            moved = pltpu.roll(moved, lane, 1)
        lists[row : row + 1, :] = lists[row : row + 1, :] + moved
    size = half_rows + extra
    halves_of[...] = jnp.zeros_like(halves_of)
    for c in range(pieces):
        at = (c % 2) * size + (c // 2) * piece
        for line in range(piece):
            halves_of[at + line : at + line + 1, :] = source[c * piece + line]
    for parity in range(2):
        at = parity * size + half_rows
        halves_of[at : at + extra, :] = lists[0:extra, :]

    def write(owner):
        for c in range(cams):
            at = (c % 2) * size
            out[pl.ds((owner * cams + c) * size, size), :] = halves_of[at : at + size, :]

    loop(owners, write)


def near_kernel(sizes, rows, edges, send_list, joined, sums_out, choose, *pieces):
    owners, cams, slot_count, held, params, part, half_pieces, extra, back_rows, step = sizes
    piece = held * part
    *pieces, near_rows = pieces
    value = joined[0:rows, :]
    left = joined[rows : 2 * rows, :]
    scale = joined[2 * rows : 3 * rows, :]
    high, low = halves(value)
    stack = jnp.concatenate([high.astype(f32), low.astype(f32), jnp.ones((16, LANES), f32)], axis=0)
    stack = stack.astype(bf16)
    node_rows = lax.broadcasted_iota(jnp.int32, (LANES, LANES), 0).astype(f32)
    patch_row = lax.broadcasted_iota(jnp.int32, (rows, LANES), 0) % held
    rigid = jnp.zeros_like(value)
    for q in range(held):
        hits = jnp.zeros((LANES, LANES), f32)
        for r in range(edges):
            at = 3 * rows + r * held + q
            hits = hits + jnp.where(node_rows == joined[at : at + 1, :], 1.0, 0.0)
        hits = hits.astype(bf16)
        pulled = lax.dot_general(stack, hits, NN, preferred_element_type=f32)
        pushed = lax.dot_general(stack, hits, NT, preferred_element_type=f32)
        degree = pushed[2 * rows : 2 * rows + 1]
        both = pulled + pushed
        edge_sum = value * (degree + float(edges)) - (both[:rows] + both[rows : 2 * rows])
        rigid = jnp.where(patch_row == q, edge_sum, rigid)
    near = rigid_weight * rigid + (2.0 * temporal_weight) * value
    near_rows[...] = near
    cam = lax.axis_index("cams")
    for distance, out in enumerate(pieces):
        target = lax.rem(cam + distance, cams) * piece
        offset = jnp.minimum(target, rows - piece)
        out[0:piece, :] = joined[pl.ds(rows + offset, piece), :]
        out[piece : 2 * piece, :] = joined[pl.ds(2 * rows + offset, piece), :]
        out[2 * piece : 3 * piece, :] = near_rows[pl.ds(offset, piece), :]
        if cams * piece > rows:

            @pl.when(target >= rows)
            def _():
                out[...] = jnp.zeros_like(out)

    sums_out[0:1, :] = rows_sum(left * (scale * left))
    sums_out[1:2, :] = rows_sum(value * near)

    column = lax.broadcasted_iota(jnp.int32, (1, choose.shape[1]), 1)
    row = column % back_rows
    slot = column // (back_rows * cams) * slot_count + row // part
    listed = jnp.zeros_like(column)
    for owner in range(owners):
        for s in range(slot_count):
            patch = jnp.maximum(send_list[s, 0, owner], 0)
            listed = jnp.where(slot == owner * slot_count + s, patch, listed)
    target = listed // held * piece + row % part * held + listed % held
    image_row = lax.broadcasted_iota(jnp.int32, choose.shape, 0)
    choose[...] = jnp.where(image_row == target, 1.0, 0.0).astype(bf16)


def masks_kernel(params, refs_count, part, half_pieces, pixel_rows, spread_out, masked, grads_pad):
    pixels = pixel_rows.shape[1]
    side = masked.shape[0] // 2
    chunk = 512
    grads_pad[...] = jnp.zeros_like(grads_pad)
    for c in range(params // part):
        for copy in range(2):
            at = (2 * (c % 2) + copy) * HALF + (c // 2) * part
            grads_pad[at : at + part, :] = pixel_rows[c * part : (c + 1) * part, :]
    node_rows = lax.broadcasted_iota(jnp.int32, (LANES, chunk), 0)
    upper = lax.broadcasted_iota(jnp.int32, (2 * HALF, chunk), 0) // HALF
    for at in range(0, pixels, chunk):
        cols = slice(at, at + chunk)
        weights = pixel_rows[params : params + refs_count, cols]
        refs = pixel_rows[params + refs_count : params + 2 * refs_count, cols].astype(jnp.int32)
        node = lax.bitwise_and(refs, LANES - 1)
        slot_of = lax.shift_right_logical(refs[0:1], 7) - upper
        even, odd = grads_pad[0 : 2 * HALF, cols], grads_pad[2 * HALF :, cols]
        spread = jnp.where(node_rows == node[0:1], weights[0:1], 0.0)
        for k in range(1, refs.shape[0]):
            spread = spread + jnp.where(node_rows == node[k : k + 1], weights[k : k + 1], 0.0)
        spread_out[:, cols] = spread

        def mask(pair):
            here = slot_of == 2 * pair
            rows = pl.multiple_of(2 * HALF * pair, 2 * HALF)
            masked[pl.ds(rows, 2 * HALF), cols] = jnp.where(here, even, 0.0).astype(bf16)
            rows = pl.multiple_of(side + 2 * HALF * pair, 2 * HALF)
            masked[pl.ds(rows, 2 * HALF), cols] = jnp.where(here, odd, 0.0).astype(bf16)

        loop(side // (2 * HALF), mask)


def table_kernel(sizes, gathered, table_out, frames_out, sums_out):
    owners, cams, slot_count, held, params, part, half_pieces, extra, back_rows, step = sizes
    devices = owners * cams
    piece = held * part
    half = half_pieces * part
    block_rows = half * held + extra
    receiver = lax.axis_index("nodes")
    cam = lax.axis_index("cams")
    curvature = jnp.zeros((1, LANES), f32)
    inside = cam * part < params
    offset = jnp.minimum(cam // 2, half_pieces - 1) * piece
    for c in range(cams):
        device = receiver * cams + c
        value = gathered[pl.ds(device * block_rows + offset, piece), :]
        before = gathered[pl.ds(jnp.maximum(device - step, 0) * block_rows + offset, piece), :]
        after = gathered[
            pl.ds(jnp.minimum(device + step, devices - 1) * block_rows + offset, piece), :
        ]
        earlier = jnp.where(jnp.logical_and(inside, device >= step), before, 0.0)
        following = jnp.where(jnp.logical_and(inside, device + step < devices), after, 0.0)
        frames = -temporal_weight * (earlier + following)
        frames_out[c * piece : (c + 1) * piece, :] = frames
        curvature = curvature + rows_sum(value * frames)
    sums_out[0:1, :] = curvature

    owner_rows = cams * block_rows
    table_row = lax.broadcasted_iota(jnp.int32, (slot_count * HALF, 1), 0)
    within = table_row % HALF
    lane_of = lax.broadcasted_iota(jnp.int32, (slot_count * HALF, LANES), 1)
    entry = table_row // HALF * owners + receiver
    column = lax.broadcasted_iota(jnp.int32, (slot_count * HALF, owner_rows), 1)
    list_row = [lane_of + line * LANES == entry for line in range(extra)]

    def fetch(owner):
        at = owner * owner_rows
        listed = jnp.zeros((slot_count * HALF, LANES), f32)
        for line in range(extra):
            row = gathered[pl.ds(at + half * held + line, 1), :]
            listed = listed + jnp.where(list_row[line], row, 0.0)
        listed = jnp.maximum(jnp.sum(listed, axis=1, keepdims=True), 0.0).astype(jnp.int32)
        source = listed // held * block_rows + listed % held + within * held
        source = jnp.where(within < half, source, -1)
        choose = jnp.where(column == source, 1.0, 0.0).astype(bf16)
        high, low = halves(gathered[pl.ds(at, owner_rows), :])
        picked = lax.dot_general(choose, high, NN, preferred_element_type=f32)
        picked = picked + lax.dot_general(choose, low, NN, preferred_element_type=f32)
        rows = pl.multiple_of(owner * slot_count * HALF, HALF)
        table_out[pl.ds(rows, slot_count * HALF), :] = picked

    filled = owners * slot_count * HALF
    if table_out.shape[0] > filled:
        table_out[filled:, :] = jnp.zeros((table_out.shape[0] - filled, LANES), f32)
    loop(owners, fetch)


def pull(table, masked, parity, cols):
    side = masked.shape[0] // 2
    live = masked[pl.ds(pl.multiple_of(parity * side, 2 * HALF), side), cols]
    pulled = lax.dot_general(table, live, NN, preferred_element_type=f32)
    return pulled[:LANES] + pulled[LANES:]


def turned_halves(table):
    return jnp.concatenate(halves(table[...].T), axis=0)


def own_kernel(table, masked, pulled_out):
    parity = lax.rem(lax.axis_index("cams"), 2)
    turned_table = turned_halves(table)
    chunk = 512
    for at in range(0, masked.shape[1], chunk):
        cols = slice(at, at + chunk)
        pulled_out[:, cols] = pull(turned_table, masked, parity, cols)


def data_kernel(sizes, pulled_own, table, spread, masked, out, squares_out, products):
    owners, cams, slot_count, held, params, part, half_pieces, extra, back_rows, step = sizes
    side = masked.shape[0] // 2
    parity = 1 - lax.rem(lax.axis_index("cams"), 2)
    turned_table = turned_halves(table)
    squares = jnp.zeros((1, LANES), f32)
    chunk = 512
    for at in range(0, spread.shape[1], chunk):
        cols = slice(at, at + chunk)
        weights = spread[:, cols]
        pulled = pulled_own[:, cols] + pull(turned_table, masked, parity, cols)
        projected = rows_sum(weights * pulled)
        squared = projected * projected
        for lane in range(0, chunk, LANES):
            squares = squares + squared[:, lane : lane + LANES]
        both = jnp.concatenate(halves(weights * projected), axis=0)
        back = lax.dot_general(masked[:, cols], both, NT, preferred_element_type=f32)
        back = back[:, :LANES] + back[:, LANES:]
        if at == 0:
            products[...] = back
        else:
            products[...] += back

    squares_out[0:1, :] = squares

    def give(owner):
        for c in range(cams):
            base = (owner * cams + c) * back_rows
            for s in range(slot_count):
                if c * part < params:
                    at = (c % 2) * side + (owner * slot_count + s) * HALF + (c // 2) * part
                    value = products[pl.ds(at, part), :]
                else:
                    value = jnp.zeros((part, LANES), f32)
                out[pl.ds(base + s * part, part), :] = value

    loop(owners, give)


def image_kernel(sizes, choose, received, frames, near_sums, frame_sums, squares, *refs):
    owners, cams, slot_count, held, params, part, half_pieces, extra, back_rows, step = sizes
    mine, (blocks, image) = refs[:cams], refs[cams:]
    cam = lax.axis_index("cams")
    piece = held * part
    value = received[...]
    high, rest = halves(value)
    low = (value - high.astype(f32) - rest.astype(f32)).astype(bf16)
    total = sum(
        lax.dot_general(choose[...], term, NN, preferred_element_type=f32)
        for term in (high, rest, low)
    )
    image[...] = total[0 : cams * piece] + frames[...]
    cross = jnp.zeros((1, LANES), f32)
    square = jnp.zeros((1, LANES), f32)
    for distance, block in enumerate(mine):
        rows = pl.ds(lax.rem(cam + cams - distance, cams) * piece, piece)
        residual, precond, near = (block[k * piece : (k + 1) * piece, :] for k in range(3))
        value = image[rows, :] + near
        image[rows, :] = value
        cross = cross + rows_sum(value * (precond * residual))
        square = square + rows_sum(value * (precond * value))
    curvature = near_sums[1:2, :] + frame_sums[0:1, :] + squares[0:1, :]
    lane_of = lax.broadcasted_iota(jnp.int32, (1, LANES), 1)
    scalars = jnp.zeros((1, LANES), f32)
    for k, row in enumerate((near_sums[0:1, :], curvature, cross, square)):
        scalars = jnp.where(lane_of == k, jnp.sum(row, axis=1, keepdims=True), scalars)

    def tell(owner):
        for c in range(cams):
            base = (owner * cams + c) * (piece + 1)
            blocks[pl.ds(base, 1), :] = scalars
            blocks[pl.ds(base + 1, piece), :] = image[c * piece : (c + 1) * piece, :]

    loop(owners, tell)


def update_kernel(
    sizes, arrived, iterate, residual, direction, precond,
    new_iterate, new_residual, new_direction,
):
    owners, cams, slot_count, held, params, part, half_pieces, extra, back_rows, step = sizes
    piece = held * part
    rows = iterate.shape[0]
    own = lax.axis_index("nodes")
    scalars = arrived[0:1, :]
    for device in range(1, owners * cams):
        scalars = scalars + arrived[device * (piece + 1) : device * (piece + 1) + 1, :]
    lane_of = lax.broadcasted_iota(jnp.int32, (1, LANES), 1)
    start, curvature, cross, square = (
        jnp.sum(jnp.where(lane_of == k, scalars, 0.0), axis=1, keepdims=True) for k in range(4)
    )
    length = start / curvature
    norm = start - 2.0 * length * cross + length * length * square
    ratio = norm / start
    for c in range(rows // piece):
        here = slice(c * piece, (c + 1) * piece)
        image = arrived[pl.ds((own * cams + c) * (piece + 1) + 1, piece), :]
        value = direction[here, :]
        left = residual[here, :] - length * image
        new_iterate[here, :] = iterate[here, :] + length * value
        new_residual[here, :] = left
        new_direction[here, :] = precond[here, :] * left + ratio * value


def flat(value):
    return jnp.transpose(value, (1, 0, 2)).reshape(-1, value.shape[2])


def joined_rows(parts):
    count = -(-sum(part.shape[0] for part in parts) // 8) * 8
    width = max(part.shape[-1] for part in parts)
    total, at = None, 0
    for part in parts:
        sides = [(at, count - at - part.shape[0], 0)] + [(0, 0, 0)] * (part.ndim - 1)
        sides[-1] = (0, width - part.shape[-1], 0)
        value = lax.pad(part, jnp.zeros((), part.dtype), sides).astype(f32)
        total = value if total is None else total + value
        at += part.shape[0]
    return total


def exchange(blocks, axes):
    rows, lanes = blocks.shape
    peers = lax.axis_size(axes)
    blocks = blocks.reshape(peers, rows // peers, 1, lanes)
    blocks = lax.all_to_all(blocks, axes, split_axis=0, concat_axis=0, tiled=True)
    return blocks.reshape(rows, lanes)


def on_device(iterate, residual, direction, precond, send_list, grads, node_refs, skin, rigid_nbr):
    held, params, lanes = direction.shape
    pixels = grads.shape[1]
    owners = lax.axis_size("nodes")
    cams = lax.axis_size("cams")
    devices = owners * cams
    slot_count = send_list.shape[2]
    slots = owners * slot_count
    asked = limit(slots, pixels)
    rows = held * params
    extra = -(-slots // lanes)
    part = next(n for n in range(1, params + 1) if params % n == 0 and n * cams >= params)
    piece = held * part
    back_rows = slot_count * part
    half_pieces = -(-(params // part) // 2)
    side = (slots + slots % 2) * HALF
    sizes = (
        owners, cams, slot_count, held, params, part, half_pieces, extra, back_rows, devices // FRAMES
    )

    def array(count):
        return jax.ShapeDtypeStruct((count, lanes), f32)

    iterate, residual, direction, precond = (flat(v) for v in (iterate, residual, direction, precond))
    by_slot = jnp.transpose(send_list, (2, 0, 1))
    source = joined_rows((direction.reshape(rows, 1, lanes), by_slot))
    size = half_pieces * piece + extra
    packed = pl.pallas_call(
        functools.partial(
            pack_kernel, (rows, slot_count, piece, params // part, half_pieces), owners, cams, extra
        ),
        out_shape=array(devices * size),
        in_specs=[VMEM],
        out_specs=VMEM,
        scratch_shapes=[
            pltpu.VMEM((-(-2 * size // 8) * 8, lanes), f32),
            pltpu.VMEM((-(-extra // 8) * 8, lanes), f32),
        ],
        compiler_params=dataclasses.replace(asked, allow_input_fusion=(True,)),
        name="pack",
    )(source)
    packed, rigid_nbr, node_refs = lax.optimization_barrier((packed, rigid_nbr, node_refs))
    gathered = exchange(packed, AXES)

    joined = joined_rows(
        [v.reshape(params, held, lanes) for v in (direction, residual, precond)]
        + [jnp.transpose(rigid_nbr, (1, 0, 2))]
    ).reshape(-1, lanes)
    image_rows = -(-cams * piece // 16) * 16
    sums, choose, *pieces = pl.pallas_call(
        functools.partial(near_kernel, sizes, rows, rigid_nbr.shape[1]),
        out_shape=(array(8), jax.ShapeDtypeStruct((image_rows, devices * back_rows), bf16))
        + (array(3 * piece),) * cams,
        in_specs=[SMEM, VMEM],
        out_specs=(VMEM,) * (2 + cams),
        scratch_shapes=[pltpu.VMEM((rows, lanes), f32)],
        compiler_params=asked,
        name="near",
    )(by_slot, joined)
    spread, masked = pl.pallas_call(
        functools.partial(masks_kernel, params, node_refs.shape[0], part, half_pieces),
        out_shape=(
            jax.ShapeDtypeStruct((lanes, pixels), f32),
            jax.ShapeDtypeStruct((2 * side, pixels), bf16),
        ),
        in_specs=[VMEM],
        out_specs=(VMEM,) * 2,
        scratch_shapes=[pltpu.VMEM((4 * HALF, pixels), f32)],
        compiler_params=asked,
        name="masks",
    )(joined_rows((grads, skin, node_refs)))
    gathered, spread, sums = lax.optimization_barrier((gathered, spread, sums))
    table, frames, frame_sums = pl.pallas_call(
        functools.partial(table_kernel, sizes),
        out_shape=(array(side), array(cams * piece), array(8)),
        in_specs=[VMEM],
        out_specs=(VMEM,) * 3,
        compiler_params=asked,
        name="table",
    )(gathered)
    other = lax.ppermute(table, "cams", [(c, c ^ 1) for c in range(cams)])
    pulled = pl.pallas_call(
        own_kernel,
        out_shape=jax.ShapeDtypeStruct((lanes, pixels), f32),
        in_specs=[VMEM] * 2,
        out_specs=VMEM,
        compiler_params=asked,
        name="own_half",
    )(table, masked)
    products, squares = pl.pallas_call(
        functools.partial(data_kernel, sizes),
        out_shape=(array(devices * back_rows), array(8)),
        in_specs=[VMEM] * 4,
        out_specs=(VMEM,) * 2,
        scratch_shapes=[pltpu.VMEM((2 * side, lanes), f32)],
        compiler_params=asked,
        name="data_products",
    )(pulled, other, spread, masked)
    products, *pieces = lax.optimization_barrier((products, *pieces))
    received = exchange(products, AXES)
    mine = [pieces[0]]
    for distance in range(1, cams):
        turn = [(c, (c + distance) % cams) for c in range(cams)]
        mine.append(lax.ppermute(pieces[distance], "cams", turn))

    blocks = pl.pallas_call(
        functools.partial(image_kernel, sizes),
        out_shape=array(devices * (piece + 1)),
        in_specs=[VMEM] * (6 + cams),
        out_specs=VMEM,
        scratch_shapes=[pltpu.VMEM((cams * piece, lanes), f32)],
        compiler_params=asked,
        name="image",
    )(choose, received, frames, sums, frame_sums, squares, *mine)
    arrived = exchange(blocks, AXES)
    outs = pl.pallas_call(
        functools.partial(update_kernel, sizes),
        out_shape=(array(rows),) * 3,
        in_specs=[VMEM] * 5,
        out_specs=(VMEM,) * 3,
        compiler_params=asked,
        name="update",
    )(arrived, iterate, residual, direction, precond)
    return tuple(jnp.transpose(v.reshape(params, held, lanes), (1, 0, 2)) for v in outs)


def solution(mesh):
    split = P(AXES, None, None)
    pixel_split = P(None, AXES)
    in_specs = (split,) * 4 + (P("nodes", None, None),) + (pixel_split,) * 3 + (split,)
    return jax.shard_map(
        on_device, mesh=mesh, in_specs=in_specs, out_specs=(split,) * 3, check_vma=False
    )
```

```python
import functools

import jax
import jax.numpy as jnp
from jax import lax
from jax.experimental import pallas as pl
from jax.experimental.pallas import tpu as pltpu
from jax.sharding import PartitionSpec as P

FRAMES = 8
AXES = ("nodes", "cams")
temporal_weight = 0.5
rigid_weight = 0.1
NN = (((1,), (0,)), ((), ()))
NT = (((1,), (1,)), ((), ()))
LANES = 128
HALF = 8
f32 = jnp.float32
bf16 = jnp.bfloat16

VMEM = pl.BlockSpec(memory_space=pltpu.VMEM)
SMEM = pl.BlockSpec(memory_space=pltpu.SMEM)


def limit(slots, pixels):
    need = 8 * 2**20 + slots * 2 * HALF * pixels * 3
    return pltpu.CompilerParams(vmem_limit_bytes=min(need, 56 * 2**20))


def halves(value):
    high = value.astype(bf16)
    low = (value - high.astype(f32)).astype(bf16)
    return high, low


def rows_sum(value):
    return jnp.sum(value, axis=0, keepdims=True)


def loop(count, body):
    lax.fori_loop(0, count, lambda i, carry: (body(i), carry)[1], 0, unroll=count <= 32)


def pack_kernel(sizes, owners, cams, extra, source, out, halves_of, lists):
    rows, slot_count, piece, pieces, half_pieces = sizes
    half_rows = half_pieces * piece
    lists[...] = jnp.zeros_like(lists)
    for s in range(slot_count):
        row, lane = divmod(s * owners, LANES)
        moved = source[rows + s : rows + s + 1, :]
        if lane:
            moved = pltpu.roll(moved, lane, 1)
        lists[row : row + 1, :] = lists[row : row + 1, :] + moved
    size = half_rows + extra
    halves_of[...] = jnp.zeros_like(halves_of)
    for c in range(pieces):
        at = (c % 2) * size + (c // 2) * piece
        halves_of[at : at + piece, :] = source[c * piece : (c + 1) * piece, :]
    for parity in range(2):
        at = parity * size + half_rows
        halves_of[at : at + extra, :] = lists[0:extra, :]

    def write(owner):
        for c in range(cams):
            at = (c % 2) * size
            out[pl.ds((owner * cams + c) * size, size), :] = halves_of[at : at + size, :]

    loop(owners, write)


def near_kernel(sizes, rows, edges, send_list, joined, sums_out, choose, *pieces):
    owners, cams, slot_count, held, params, part, half_pieces, extra, back_rows, step = sizes
    piece = held * part
    *pieces, near_rows = pieces
    value = joined[0:rows, :]
    left = joined[rows : 2 * rows, :]
    scale = joined[2 * rows : 3 * rows, :]
    high, low = halves(value)
    stack = jnp.concatenate([high.astype(f32), low.astype(f32), jnp.ones((16, LANES), f32)], axis=0)
    stack = stack.astype(bf16)
    node_rows = lax.broadcasted_iota(jnp.int32, (LANES, LANES), 0).astype(f32)
    patch_row = lax.broadcasted_iota(jnp.int32, (rows, LANES), 0) % held
    rigid = jnp.zeros_like(value)
    for q in range(held):
        hits = jnp.zeros((LANES, LANES), f32)
        for r in range(edges):
            at = 3 * rows + r * held + q
            hits = hits + jnp.where(node_rows == joined[at : at + 1, :], 1.0, 0.0)
        hits = hits.astype(bf16)
        pulled = lax.dot_general(stack, hits, NN, preferred_element_type=f32)
        pushed = lax.dot_general(stack, hits, NT, preferred_element_type=f32)
        degree = pushed[2 * rows : 2 * rows + 1]
        both = pulled + pushed
        edge_sum = value * (degree + float(edges)) - (both[:rows] + both[rows : 2 * rows])
        rigid = jnp.where(patch_row == q, edge_sum, rigid)
    near = rigid_weight * rigid + (2.0 * temporal_weight) * value
    near_rows[...] = near
    cam = lax.axis_index("cams")
    for distance, out in enumerate(pieces):
        target = lax.rem(cam + distance, cams) * piece
        offset = jnp.minimum(target, rows - piece)
        out[0:piece, :] = joined[pl.ds(rows + offset, piece), :]
        out[piece : 2 * piece, :] = joined[pl.ds(2 * rows + offset, piece), :]
        out[2 * piece : 3 * piece, :] = near_rows[pl.ds(offset, piece), :]
        if cams * piece > rows:

            @pl.when(target >= rows)
            def _():
                out[...] = jnp.zeros_like(out)

    sums_out[0:1, :] = rows_sum(left * (scale * left))
    sums_out[1:2, :] = rows_sum(value * near)

    column = lax.broadcasted_iota(jnp.int32, (1, choose.shape[1]), 1)
    row = column % back_rows
    slot = column // (back_rows * (cams // 2)) * slot_count + row // part
    listed = jnp.zeros_like(column)
    for owner in range(owners):
        for s in range(slot_count):
            patch = jnp.maximum(send_list[s, 0, owner], 0)
            listed = jnp.where(slot == owner * slot_count + s, patch, listed)
    target = listed // held * piece + row % part * held + listed % held
    image_row = lax.broadcasted_iota(jnp.int32, choose.shape, 0)
    choose[...] = jnp.where(image_row == target, 1.0, 0.0).astype(bf16)


def masks_kernel(params, refs_count, part, half_pieces, pixel_rows, spread_out, masked, grads_pad):
    pixels = pixel_rows.shape[1]
    side = masked.shape[0] // 2
    chunk = 512
    grads_pad[...] = jnp.zeros_like(grads_pad)
    for c in range(params // part):
        for copy in range(2):
            at = (2 * (c % 2) + copy) * HALF + (c // 2) * part
            grads_pad[at : at + part, :] = pixel_rows[c * part : (c + 1) * part, :]
    node_rows = lax.broadcasted_iota(jnp.int32, (LANES, chunk), 0)
    upper = lax.broadcasted_iota(jnp.int32, (2 * HALF, chunk), 0) // HALF
    for at in range(0, pixels, chunk):
        cols = slice(at, at + chunk)
        weights = pixel_rows[params : params + refs_count, cols]
        refs = pixel_rows[params + refs_count : params + 2 * refs_count, cols].astype(jnp.int32)
        node = lax.bitwise_and(refs, LANES - 1)
        slot_of = lax.shift_right_logical(refs[0:1], 7) - upper
        even, odd = grads_pad[0 : 2 * HALF, cols], grads_pad[2 * HALF :, cols]
        spread = jnp.where(node_rows == node[0:1], weights[0:1], 0.0)
        for k in range(1, refs.shape[0]):
            spread = spread + jnp.where(node_rows == node[k : k + 1], weights[k : k + 1], 0.0)
        spread_out[:, cols] = spread

        def mask(pair):
            here = slot_of == 2 * pair
            rows = pl.multiple_of(2 * HALF * pair, 2 * HALF)
            masked[pl.ds(rows, 2 * HALF), cols] = jnp.where(here, even, 0.0).astype(bf16)
            rows = pl.multiple_of(side + 2 * HALF * pair, 2 * HALF)
            masked[pl.ds(rows, 2 * HALF), cols] = jnp.where(here, odd, 0.0).astype(bf16)

        loop(side // (2 * HALF), mask)


def table_kernel(sizes, gathered, table_out, frames_out, sums_out):
    owners, cams, slot_count, held, params, part, half_pieces, extra, back_rows, step = sizes
    devices = owners * cams
    piece = held * part
    half = half_pieces * part
    block_rows = half * held + extra
    receiver = lax.axis_index("nodes")
    cam = lax.axis_index("cams")
    curvature = jnp.zeros((1, LANES), f32)
    inside = cam * part < params
    offset = jnp.minimum(cam // 2, half_pieces - 1) * piece
    for c in range(cams):
        device = receiver * cams + c
        value = gathered[pl.ds(device * block_rows + offset, piece), :]
        before = gathered[pl.ds(jnp.maximum(device - step, 0) * block_rows + offset, piece), :]
        after = gathered[
            pl.ds(jnp.minimum(device + step, devices - 1) * block_rows + offset, piece), :
        ]
        earlier = jnp.where(jnp.logical_and(inside, device >= step), before, 0.0)
        following = jnp.where(jnp.logical_and(inside, device + step < devices), after, 0.0)
        frames = -temporal_weight * (earlier + following)
        frames_out[c * piece : (c + 1) * piece, :] = frames
        curvature = curvature + rows_sum(value * frames)
    sums_out[0:1, :] = curvature

    owner_rows = cams * block_rows
    table_row = lax.broadcasted_iota(jnp.int32, (slot_count * HALF, 1), 0)
    within = table_row % HALF
    lane_of = lax.broadcasted_iota(jnp.int32, (slot_count * HALF, LANES), 1)
    entry = table_row // HALF * owners + receiver
    column = lax.broadcasted_iota(jnp.int32, (slot_count * HALF, owner_rows), 1)
    list_row = [lane_of + line * LANES == entry for line in range(extra)]

    def fetch(owner):
        at = owner * owner_rows
        listed = jnp.zeros((slot_count * HALF, LANES), f32)
        for line in range(extra):
            row = gathered[pl.ds(at + half * held + line, 1), :]
            listed = listed + jnp.where(list_row[line], row, 0.0)
        listed = jnp.maximum(jnp.sum(listed, axis=1, keepdims=True), 0.0).astype(jnp.int32)
        source = listed // held * block_rows + listed % held + within * held
        source = jnp.where(within < half, source, -1)
        choose = jnp.where(column == source, 1.0, 0.0).astype(bf16)
        high, low = halves(gathered[pl.ds(at, owner_rows), :])
        picked = lax.dot_general(choose, high, NN, preferred_element_type=f32)
        picked = picked + lax.dot_general(choose, low, NN, preferred_element_type=f32)
        rows = pl.multiple_of(owner * slot_count * HALF, HALF)
        table_out[pl.ds(rows, slot_count * HALF), :] = picked

    filled = owners * slot_count * HALF
    if table_out.shape[0] > filled:
        table_out[filled:, :] = jnp.zeros((table_out.shape[0] - filled, LANES), f32)
    loop(owners, fetch)


def pull(table, masked, parity, cols):
    side = masked.shape[0] // 2
    live = masked[pl.ds(pl.multiple_of(parity * side, 2 * HALF), side), cols]
    pulled = lax.dot_general(table, live, NN, preferred_element_type=f32)
    return pulled[:LANES] + pulled[LANES:]


def turned_halves(table):
    return jnp.concatenate(halves(table[...].T), axis=0)


def own_kernel(table, masked, pulled_out):
    parity = lax.rem(lax.axis_index("cams"), 2)
    turned_table = turned_halves(table)
    chunk = 512
    for at in range(0, masked.shape[1], chunk):
        cols = slice(at, at + chunk)
        pulled_out[:, cols] = pull(turned_table, masked, parity, cols)


def data_kernel(sizes, pulled_own, table, spread, masked, keep, pass_on, squares_out, products, out):
    owners, cams, slot_count, held, params, part, half_pieces, extra, back_rows, step = sizes
    side = masked.shape[0] // 2
    parity = 1 - lax.rem(lax.axis_index("cams"), 2)
    turned_table = turned_halves(table)
    squares = jnp.zeros((1, LANES), f32)
    chunk = 512
    for at in range(0, spread.shape[1], chunk):
        cols = slice(at, at + chunk)
        weights = spread[:, cols]
        pulled = pulled_own[:, cols] + pull(turned_table, masked, parity, cols)
        projected = rows_sum(weights * pulled)
        squared = projected * projected
        for lane in range(0, chunk, LANES):
            squares = squares + squared[:, lane : lane + LANES]
        both = jnp.concatenate(halves(weights * projected), axis=0)
        back = lax.dot_general(masked[:, cols], both, NT, preferred_element_type=f32)
        back = back[:, :LANES] + back[:, LANES:]
        if at == 0:
            products[...] = back
        else:
            products[...] += back

    squares_out[0:1, :] = squares

    count = keep.shape[0]

    def give(owner):
        for c in range(cams):
            base = (c % 2) * count + (owner * (cams // 2) + c // 2) * back_rows
            for s in range(slot_count):
                if c * part < params:
                    at = (c % 2) * side + (owner * slot_count + s) * HALF + (c // 2) * part
                    value = products[pl.ds(at, part), :]
                else:
                    value = jnp.zeros((part, LANES), f32)
                out[pl.ds(base + s * part, part), :] = value

    loop(owners, give)
    keep[...] = out[pl.ds(pl.multiple_of((1 - parity) * count, 8), count), :]
    pass_on[...] = out[pl.ds(pl.multiple_of(parity * count, 8), count), :]


def sum_kernel(kept, passed, out):
    out[...] = kept[...] + passed[...]


def image_kernel(sizes, choose, received, frames, near_sums, frame_sums, squares, *refs):
    owners, cams, slot_count, held, params, part, half_pieces, extra, back_rows, step = sizes
    mine, (blocks, image) = refs[:cams], refs[cams:]
    cam = lax.axis_index("cams")
    piece = held * part
    value = received[...]
    high, rest = halves(value)
    low = (value - high.astype(f32) - rest.astype(f32)).astype(bf16)
    total = sum(
        lax.dot_general(choose[...], term, NN, preferred_element_type=f32)
        for term in (high, rest, low)
    )
    image[...] = total[0 : cams * piece] + frames[...]
    cross = jnp.zeros((1, LANES), f32)
    square = jnp.zeros((1, LANES), f32)
    for distance, block in enumerate(mine):
        rows = pl.ds(lax.rem(cam + cams - distance, cams) * piece, piece)
        residual, precond, near = (block[k * piece : (k + 1) * piece, :] for k in range(3))
        value = image[rows, :] + near
        image[rows, :] = value
        cross = cross + rows_sum(value * (precond * residual))
        square = square + rows_sum(value * (precond * value))
    curvature = near_sums[1:2, :] + frame_sums[0:1, :] + squares[0:1, :]
    lane_of = lax.broadcasted_iota(jnp.int32, (1, LANES), 1)
    scalars = jnp.zeros((1, LANES), f32)
    for k, row in enumerate((near_sums[0:1, :], curvature, cross, square)):
        scalars = jnp.where(lane_of == k, jnp.sum(row, axis=1, keepdims=True), scalars)

    def tell(owner):
        for c in range(cams):
            base = (owner * cams + c) * (piece + 1)
            blocks[pl.ds(base, 1), :] = scalars
            blocks[pl.ds(base + 1, piece), :] = image[c * piece : (c + 1) * piece, :]

    loop(owners, tell)


def update_kernel(
    sizes, arrived, iterate, residual, direction, precond,
    new_iterate, new_residual, new_direction,
):
    owners, cams, slot_count, held, params, part, half_pieces, extra, back_rows, step = sizes
    piece = held * part
    rows = iterate.shape[0]
    own = lax.axis_index("nodes")
    scalars = arrived[0:1, :]
    for device in range(1, owners * cams):
        scalars = scalars + arrived[device * (piece + 1) : device * (piece + 1) + 1, :]
    lane_of = lax.broadcasted_iota(jnp.int32, (1, LANES), 1)
    start, curvature, cross, square = (
        jnp.sum(jnp.where(lane_of == k, scalars, 0.0), axis=1, keepdims=True) for k in range(4)
    )
    length = start / curvature
    norm = start - 2.0 * length * cross + length * length * square
    ratio = norm / start
    for c in range(rows // piece):
        here = slice(c * piece, (c + 1) * piece)
        image = arrived[pl.ds((own * cams + c) * (piece + 1) + 1, piece), :]
        value = direction[here, :]
        left = residual[here, :] - length * image
        new_iterate[here, :] = iterate[here, :] + length * value
        new_residual[here, :] = left
        new_direction[here, :] = precond[here, :] * left + ratio * value


def flat(value):
    return jnp.transpose(value, (1, 0, 2)).reshape(-1, value.shape[2])


def joined_rows(parts):
    count = -(-sum(part.shape[0] for part in parts) // 8) * 8
    width = max(part.shape[-1] for part in parts)
    total, at = None, 0
    for part in parts:
        sides = [(at, count - at - part.shape[0], 0)] + [(0, 0, 0)] * (part.ndim - 1)
        sides[-1] = (0, width - part.shape[-1], 0)
        value = lax.pad(part, jnp.zeros((), part.dtype), sides).astype(f32)
        total = value if total is None else total + value
        at += part.shape[0]
    return total


def exchange(blocks, axes):
    rows, lanes = blocks.shape
    peers = lax.axis_size(axes)
    blocks = blocks.reshape(peers, rows // peers, 1, lanes)
    blocks = lax.all_to_all(blocks, axes, split_axis=0, concat_axis=0, tiled=True)
    return blocks.reshape(rows, lanes)


def on_device(iterate, residual, direction, precond, send_list, grads, node_refs, skin, rigid_nbr):
    held, params, lanes = direction.shape
    pixels = grads.shape[1]
    owners = lax.axis_size("nodes")
    cams = lax.axis_size("cams")
    devices = owners * cams
    slot_count = send_list.shape[2]
    slots = owners * slot_count
    asked = limit(slots, pixels)
    rows = held * params
    extra = -(-slots // lanes)
    part = next(n for n in range(1, params + 1) if params % n == 0 and n * cams >= params)
    piece = held * part
    back_rows = slot_count * part
    half_pieces = -(-(params // part) // 2)
    side = (slots + slots % 2) * HALF
    sizes = (
        owners, cams, slot_count, held, params, part, half_pieces, extra, back_rows, devices // FRAMES
    )

    def array(count):
        return jax.ShapeDtypeStruct((count, lanes), f32)

    iterate, residual, direction, precond = (flat(v) for v in (iterate, residual, direction, precond))
    by_slot = jnp.transpose(send_list, (2, 0, 1))
    source = joined_rows((direction.reshape(rows, 1, lanes), by_slot))
    size = half_pieces * piece + extra
    packed = pl.pallas_call(
        functools.partial(
            pack_kernel, (rows, slot_count, piece, params // part, half_pieces), owners, cams, extra
        ),
        out_shape=array(devices * size),
        in_specs=[VMEM],
        out_specs=VMEM,
        scratch_shapes=[
            pltpu.VMEM((-(-2 * size // 8) * 8, lanes), f32),
            pltpu.VMEM((-(-extra // 8) * 8, lanes), f32),
        ],
        compiler_params=asked,
        name="pack",
    )(source.reshape(-1, lanes))
    packed, rigid_nbr, node_refs = lax.optimization_barrier((packed, rigid_nbr, node_refs))
    gathered = exchange(packed, AXES)

    joined = joined_rows(
        [v.reshape(params, held, lanes) for v in (direction, residual, precond)]
        + [jnp.transpose(rigid_nbr, (1, 0, 2))]
    ).reshape(-1, lanes)
    image_rows = -(-cams * piece // 16) * 16
    sums, choose, *pieces = pl.pallas_call(
        functools.partial(near_kernel, sizes, rows, rigid_nbr.shape[1]),
        out_shape=(array(8), jax.ShapeDtypeStruct((image_rows, devices // 2 * back_rows), bf16))
        + (array(3 * piece),) * cams,
        in_specs=[SMEM, VMEM],
        out_specs=(VMEM,) * (2 + cams),
        scratch_shapes=[pltpu.VMEM((rows, lanes), f32)],
        compiler_params=asked,
        name="near",
    )(by_slot, joined)
    spread, masked = pl.pallas_call(
        functools.partial(masks_kernel, params, node_refs.shape[0], part, half_pieces),
        out_shape=(
            jax.ShapeDtypeStruct((lanes, pixels), f32),
            jax.ShapeDtypeStruct((2 * side, pixels), bf16),
        ),
        in_specs=[VMEM],
        out_specs=(VMEM,) * 2,
        scratch_shapes=[pltpu.VMEM((4 * HALF, pixels), f32)],
        compiler_params=asked,
        name="masks",
    )(joined_rows((grads, skin, node_refs)))
    gathered, spread, sums = lax.optimization_barrier((gathered, spread, sums))
    table, frames, frame_sums = pl.pallas_call(
        functools.partial(table_kernel, sizes),
        out_shape=(array(side), array(cams * piece), array(8)),
        in_specs=[VMEM],
        out_specs=(VMEM,) * 3,
        compiler_params=asked,
        name="table",
    )(gathered)
    other = lax.ppermute(table, "cams", [(c, c ^ 1) for c in range(cams)])
    pulled = pl.pallas_call(
        own_kernel,
        out_shape=jax.ShapeDtypeStruct((lanes, pixels), f32),
        in_specs=[VMEM] * 2,
        out_specs=VMEM,
        compiler_params=asked,
        name="own_half",
    )(table, masked)
    count = devices // 2 * back_rows
    kept, passed, squares = pl.pallas_call(
        functools.partial(data_kernel, sizes),
        out_shape=(array(count), array(count), array(8)),
        in_specs=[VMEM] * 4,
        out_specs=(VMEM,) * 3,
        scratch_shapes=[pltpu.VMEM((2 * side, lanes), f32), pltpu.VMEM((2 * count, lanes), f32)],
        compiler_params=asked,
        name="data_products",
    )(pulled, other, spread, masked)
    passed = lax.ppermute(passed, "cams", [(c, c ^ 1) for c in range(cams)])
    products = pl.pallas_call(
        sum_kernel,
        out_shape=array(count),
        in_specs=[VMEM] * 2,
        out_specs=VMEM,
        compiler_params=asked,
        name="pair_sum",
    )(kept, passed)
    products, *pieces = lax.optimization_barrier((products, *pieces))
    alike = [[d for d in range(devices) if d % cams % 2 == parity] for parity in range(2)]
    received = lax.all_to_all(
        products.reshape(devices // 2, back_rows, 1, lanes),
        AXES, split_axis=0, concat_axis=0, axis_index_groups=alike, tiled=True,
    ).reshape(count, lanes)
    mine = [pieces[0]]
    for distance in range(1, cams):
        turn = [(c, (c + distance) % cams) for c in range(cams)]
        mine.append(lax.ppermute(pieces[distance], "cams", turn))

    blocks = pl.pallas_call(
        functools.partial(image_kernel, sizes),
        out_shape=array(devices * (piece + 1)),
        in_specs=[VMEM] * (6 + cams),
        out_specs=VMEM,
        scratch_shapes=[pltpu.VMEM((cams * piece, lanes), f32)],
        compiler_params=asked,
        name="image",
    )(choose, received, frames, sums, frame_sums, squares, *mine)
    arrived = exchange(blocks, AXES)
    outs = pl.pallas_call(
        functools.partial(update_kernel, sizes),
        out_shape=(array(rows),) * 3,
        in_specs=[VMEM] * 5,
        out_specs=(VMEM,) * 3,
        compiler_params=asked,
        name="update",
    )(arrived, iterate, residual, direction, precond)
    return tuple(jnp.transpose(v.reshape(params, held, lanes), (1, 0, 2)) for v in outs)


def solution(mesh):
    split = P(AXES, None, None)
    pixel_split = P(None, AXES)
    in_specs = (split,) * 4 + (P("nodes", None, None),) + (pixel_split,) * 3 + (split,)
    return jax.shard_map(
        on_device, mesh=mesh, in_specs=in_specs, out_specs=(split,) * 3, check_vma=False
    )
```

```python
import functools

import jax
import jax.numpy as jnp
from jax import lax
from jax.experimental import pallas as pl
from jax.experimental.pallas import tpu as pltpu
from jax.sharding import PartitionSpec as P

FRAMES = 8
AXES = ("nodes", "cams")
temporal_weight = 0.5
rigid_weight = 0.1
NN = (((1,), (0,)), ((), ()))
NT = (((1,), (1,)), ((), ()))
LANES = 128
HALF = 8
f32 = jnp.float32
bf16 = jnp.bfloat16

VMEM = pl.BlockSpec(memory_space=pltpu.VMEM)
SMEM = pl.BlockSpec(memory_space=pltpu.SMEM)


def limit(slots, pixels):
    need = 8 * 2**20 + slots * 2 * HALF * pixels * 3
    return pltpu.CompilerParams(vmem_limit_bytes=min(need, 56 * 2**20))


def halves(value):
    high = value.astype(bf16)
    low = (value - high.astype(f32)).astype(bf16)
    return high, low


def rows_sum(value):
    return jnp.sum(value, axis=0, keepdims=True)


def loop(count, body):
    lax.fori_loop(0, count, lambda i, carry: (body(i), carry)[1], 0, unroll=count <= 32)


def pack_kernel(sizes, owners, cams, extra, source, out, halves_of, lists):
    rows, slot_count, piece, pieces, half_pieces = sizes
    half_rows = half_pieces * piece
    lists[...] = jnp.zeros_like(lists)
    for s in range(slot_count):
        row, lane = divmod(s * owners, LANES)
        moved = source[rows + s : rows + s + 1, :]
        if lane:
            moved = pltpu.roll(moved, lane, 1)
        lists[row : row + 1, :] = lists[row : row + 1, :] + moved
    size = half_rows + extra
    halves_of[...] = jnp.zeros_like(halves_of)
    for c in range(pieces):
        at = (c % 2) * size + (c // 2) * piece
        halves_of[at : at + piece, :] = source[c * piece : (c + 1) * piece, :]
    for parity in range(2):
        at = parity * size + half_rows
        halves_of[at : at + extra, :] = lists[0:extra, :]

    def write(owner):
        for c in range(cams):
            at = (c % 2) * size
            out[pl.ds((owner * cams + c) * size, size), :] = halves_of[at : at + size, :]

    loop(owners, write)


def near_kernel(sizes, rows, edges, send_list, joined, sums_out, choose, *pieces):
    owners, cams, slot_count, held, params, part, half_pieces, extra, back_rows, step = sizes
    piece = held * part
    *pieces, near_rows = pieces
    value = joined[0:rows, :]
    left = joined[rows : 2 * rows, :]
    scale = joined[2 * rows : 3 * rows, :]
    high, low = halves(value)
    stack = jnp.concatenate([high.astype(f32), low.astype(f32), jnp.ones((16, LANES), f32)], axis=0)
    stack = stack.astype(bf16)
    node_rows = lax.broadcasted_iota(jnp.int32, (LANES, LANES), 0).astype(f32)
    patch_row = lax.broadcasted_iota(jnp.int32, (rows, LANES), 0) % held
    rigid = jnp.zeros_like(value)
    for q in range(held):
        hits = jnp.zeros((LANES, LANES), f32)
        for r in range(edges):
            at = 3 * rows + r * held + q
            hits = hits + jnp.where(node_rows == joined[at : at + 1, :], 1.0, 0.0)
        hits = hits.astype(bf16)
        pulled = lax.dot_general(stack, hits, NN, preferred_element_type=f32)
        pushed = lax.dot_general(stack, hits, NT, preferred_element_type=f32)
        degree = pushed[2 * rows : 2 * rows + 1]
        both = pulled + pushed
        edge_sum = value * (degree + float(edges)) - (both[:rows] + both[rows : 2 * rows])
        rigid = jnp.where(patch_row == q, edge_sum, rigid)
    near = rigid_weight * rigid + (2.0 * temporal_weight) * value
    near_rows[...] = near
    cam = lax.axis_index("cams")
    for distance, out in enumerate(pieces):
        target = lax.rem(cam + distance, cams) * piece
        offset = jnp.minimum(target, rows - piece)
        out[0:piece, :] = joined[pl.ds(rows + offset, piece), :]
        out[piece : 2 * piece, :] = joined[pl.ds(2 * rows + offset, piece), :]
        out[2 * piece : 3 * piece, :] = near_rows[pl.ds(offset, piece), :]
        if cams * piece > rows:

            @pl.when(target >= rows)
            def _():
                out[...] = jnp.zeros_like(out)

    sums_out[0:1, :] = rows_sum(left * (scale * left))
    sums_out[1:2, :] = rows_sum(value * near)

    column = lax.broadcasted_iota(jnp.int32, (1, choose.shape[1]), 1)
    row = column % back_rows
    slot = column // (back_rows * cams) * slot_count + row // part
    listed = jnp.zeros_like(column)
    for owner in range(owners):
        for s in range(slot_count):
            patch = jnp.maximum(send_list[s, 0, owner], 0)
            listed = jnp.where(slot == owner * slot_count + s, patch, listed)
    target = listed // held * piece + row % part * held + listed % held
    image_row = lax.broadcasted_iota(jnp.int32, choose.shape, 0)
    choose[...] = jnp.where(image_row == target, 1.0, 0.0).astype(bf16)


def masks_kernel(params, refs_count, part, half_pieces, pixel_rows, spread_out, masked, grads_pad):
    pixels = pixel_rows.shape[1]
    side = masked.shape[0] // 2
    chunk = 512
    grads_pad[...] = jnp.zeros_like(grads_pad)
    for c in range(params // part):
        for copy in range(2):
            at = (2 * (c % 2) + copy) * HALF + (c // 2) * part
            grads_pad[at : at + part, :] = pixel_rows[c * part : (c + 1) * part, :]
    node_rows = lax.broadcasted_iota(jnp.int32, (LANES, chunk), 0)
    upper = lax.broadcasted_iota(jnp.int32, (2 * HALF, chunk), 0) // HALF
    for at in range(0, pixels, chunk):
        cols = slice(at, at + chunk)
        weights = pixel_rows[params : params + refs_count, cols]
        refs = pixel_rows[params + refs_count : params + 2 * refs_count, cols].astype(jnp.int32)
        node = lax.bitwise_and(refs, LANES - 1)
        slot_of = lax.shift_right_logical(refs[0:1], 7) - upper
        even, odd = grads_pad[0 : 2 * HALF, cols], grads_pad[2 * HALF :, cols]
        spread = jnp.where(node_rows == node[0:1], weights[0:1], 0.0)
        for k in range(1, refs.shape[0]):
            spread = spread + jnp.where(node_rows == node[k : k + 1], weights[k : k + 1], 0.0)
        spread_out[:, cols] = spread

        def mask(pair):
            here = slot_of == 2 * pair
            rows = pl.multiple_of(2 * HALF * pair, 2 * HALF)
            masked[pl.ds(rows, 2 * HALF), cols] = jnp.where(here, even, 0.0).astype(bf16)
            rows = pl.multiple_of(side + 2 * HALF * pair, 2 * HALF)
            masked[pl.ds(rows, 2 * HALF), cols] = jnp.where(here, odd, 0.0).astype(bf16)

        loop(side // (2 * HALF), mask)


def table_kernel(sizes, gathered, table_out, frames_out, sums_out):
    owners, cams, slot_count, held, params, part, half_pieces, extra, back_rows, step = sizes
    devices = owners * cams
    piece = held * part
    half = half_pieces * part
    block_rows = half * held + extra
    receiver = lax.axis_index("nodes")
    cam = lax.axis_index("cams")
    curvature = jnp.zeros((1, LANES), f32)
    inside = cam * part < params
    offset = jnp.minimum(cam // 2, half_pieces - 1) * piece
    for c in range(cams):
        device = receiver * cams + c
        value = gathered[pl.ds(device * block_rows + offset, piece), :]
        before = gathered[pl.ds(jnp.maximum(device - step, 0) * block_rows + offset, piece), :]
        after = gathered[
            pl.ds(jnp.minimum(device + step, devices - 1) * block_rows + offset, piece), :
        ]
        earlier = jnp.where(jnp.logical_and(inside, device >= step), before, 0.0)
        following = jnp.where(jnp.logical_and(inside, device + step < devices), after, 0.0)
        frames = -temporal_weight * (earlier + following)
        frames_out[c * piece : (c + 1) * piece, :] = frames
        curvature = curvature + rows_sum(value * frames)
    sums_out[0:1, :] = curvature

    owner_rows = cams * block_rows
    table_row = lax.broadcasted_iota(jnp.int32, (slot_count * HALF, 1), 0)
    within = table_row % HALF
    lane_of = lax.broadcasted_iota(jnp.int32, (slot_count * HALF, LANES), 1)
    entry = table_row // HALF * owners + receiver
    column = lax.broadcasted_iota(jnp.int32, (slot_count * HALF, owner_rows), 1)
    list_row = [lane_of + line * LANES == entry for line in range(extra)]

    def fetch(owner):
        at = owner * owner_rows
        listed = jnp.zeros((slot_count * HALF, LANES), f32)
        for line in range(extra):
            row = gathered[pl.ds(at + half * held + line, 1), :]
            listed = listed + jnp.where(list_row[line], row, 0.0)
        listed = jnp.maximum(jnp.sum(listed, axis=1, keepdims=True), 0.0).astype(jnp.int32)
        source = listed // held * block_rows + listed % held + within * held
        source = jnp.where(within < half, source, -1)
        choose = jnp.where(column == source, 1.0, 0.0).astype(bf16)
        high, low = halves(gathered[pl.ds(at, owner_rows), :])
        picked = lax.dot_general(choose, high, NN, preferred_element_type=f32)
        picked = picked + lax.dot_general(choose, low, NN, preferred_element_type=f32)
        rows = pl.multiple_of(owner * slot_count * HALF, HALF)
        table_out[pl.ds(rows, slot_count * HALF), :] = picked

    filled = owners * slot_count * HALF
    if table_out.shape[0] > filled:
        table_out[filled:, :] = jnp.zeros((table_out.shape[0] - filled, LANES), f32)
    loop(owners, fetch)


def pull(table, masked, parity, cols):
    side = masked.shape[0] // 2
    live = masked[pl.ds(pl.multiple_of(parity * side, 2 * HALF), side), cols]
    pulled = lax.dot_general(table, live, NN, preferred_element_type=f32)
    return pulled[:LANES] + pulled[LANES:]


def turned_halves(table):
    return jnp.concatenate(halves(table[...].T), axis=0)


def own_kernel(table, masked, pulled_out):
    parity = lax.rem(lax.axis_index("cams"), 2)
    turned_table = turned_halves(table)
    chunk = min(1024, masked.shape[1])
    for at in range(0, masked.shape[1], chunk):
        cols = slice(at, at + chunk)
        pulled_out[:, cols] = pull(turned_table, masked, parity, cols)


def data_kernel(sizes, pulled_own, table, spread, masked, out, squares_out, products):
    owners, cams, slot_count, held, params, part, half_pieces, extra, back_rows, step = sizes
    side = masked.shape[0] // 2
    parity = 1 - lax.rem(lax.axis_index("cams"), 2)
    turned_table = turned_halves(table)
    squares = jnp.zeros((1, LANES), f32)
    chunk = min(1024, masked.shape[1])
    for at in range(0, spread.shape[1], chunk):
        cols = slice(at, at + chunk)
        weights = spread[:, cols]
        pulled = pulled_own[:, cols] + pull(turned_table, masked, parity, cols)
        projected = rows_sum(weights * pulled)
        squared = projected * projected
        for lane in range(0, chunk, LANES):
            squares = squares + squared[:, lane : lane + LANES]
        both = jnp.concatenate(halves(weights * projected), axis=0)
        back = lax.dot_general(masked[:, cols], both, NT, preferred_element_type=f32)
        back = back[:, :LANES] + back[:, LANES:]
        if at == 0:
            products[...] = back
        else:
            products[...] += back

    squares_out[0:1, :] = squares

    def give(owner):
        for c in range(cams):
            base = (owner * cams + c) * back_rows
            for s in range(slot_count):
                if c * part < params:
                    at = (c % 2) * side + (owner * slot_count + s) * HALF + (c // 2) * part
                    value = products[pl.ds(at, part), :]
                else:
                    value = jnp.zeros((part, LANES), f32)
                out[pl.ds(base + s * part, part), :] = value

    loop(owners, give)


def image_kernel(sizes, choose, received, frames, near_sums, frame_sums, squares, *refs):
    owners, cams, slot_count, held, params, part, half_pieces, extra, back_rows, step = sizes
    mine, (blocks, image) = refs[:cams], refs[cams:]
    cam = lax.axis_index("cams")
    piece = held * part
    value = received[...]
    high, rest = halves(value)
    low = (value - high.astype(f32) - rest.astype(f32)).astype(bf16)
    total = sum(
        lax.dot_general(choose[...], term, NN, preferred_element_type=f32)
        for term in (high, rest, low)
    )
    image[...] = total[0 : cams * piece] + frames[...]
    cross = jnp.zeros((1, LANES), f32)
    square = jnp.zeros((1, LANES), f32)
    for distance, block in enumerate(mine):
        rows = pl.ds(lax.rem(cam + cams - distance, cams) * piece, piece)
        residual, precond, near = (block[k * piece : (k + 1) * piece, :] for k in range(3))
        value = image[rows, :] + near
        image[rows, :] = value
        cross = cross + rows_sum(value * (precond * residual))
        square = square + rows_sum(value * (precond * value))
    curvature = near_sums[1:2, :] + frame_sums[0:1, :] + squares[0:1, :]
    lane_of = lax.broadcasted_iota(jnp.int32, (1, LANES), 1)
    scalars = jnp.zeros((1, LANES), f32)
    for k, row in enumerate((near_sums[0:1, :], curvature, cross, square)):
        scalars = jnp.where(lane_of == k, jnp.sum(row, axis=1, keepdims=True), scalars)

    def tell(owner):
        for c in range(cams):
            base = (owner * cams + c) * (piece + 1)
            blocks[pl.ds(base, 1), :] = scalars
            blocks[pl.ds(base + 1, piece), :] = image[c * piece : (c + 1) * piece, :]

    loop(owners, tell)


def update_kernel(
    sizes, arrived, iterate, residual, direction, precond,
    new_iterate, new_residual, new_direction,
):
    owners, cams, slot_count, held, params, part, half_pieces, extra, back_rows, step = sizes
    piece = held * part
    rows = iterate.shape[0]
    own = lax.axis_index("nodes")
    scalars = arrived[0:1, :]
    for device in range(1, owners * cams):
        scalars = scalars + arrived[device * (piece + 1) : device * (piece + 1) + 1, :]
    lane_of = lax.broadcasted_iota(jnp.int32, (1, LANES), 1)
    start, curvature, cross, square = (
        jnp.sum(jnp.where(lane_of == k, scalars, 0.0), axis=1, keepdims=True) for k in range(4)
    )
    length = start / curvature
    norm = start - 2.0 * length * cross + length * length * square
    ratio = norm / start
    for c in range(rows // piece):
        here = slice(c * piece, (c + 1) * piece)
        image = arrived[pl.ds((own * cams + c) * (piece + 1) + 1, piece), :]
        value = direction[here, :]
        left = residual[here, :] - length * image
        new_iterate[here, :] = iterate[here, :] + length * value
        new_residual[here, :] = left
        new_direction[here, :] = precond[here, :] * left + ratio * value


def flat(value):
    return jnp.transpose(value, (1, 0, 2)).reshape(-1, value.shape[2])


def joined_rows(parts):
    count = -(-sum(part.shape[0] for part in parts) // 8) * 8
    width = max(part.shape[-1] for part in parts)
    total, at = None, 0
    for part in parts:
        sides = [(at, count - at - part.shape[0], 0)] + [(0, 0, 0)] * (part.ndim - 1)
        sides[-1] = (0, width - part.shape[-1], 0)
        value = lax.pad(part, jnp.zeros((), part.dtype), sides).astype(f32)
        total = value if total is None else total + value
        at += part.shape[0]
    return total


def exchange(blocks, axes):
    rows, lanes = blocks.shape
    peers = lax.axis_size(axes)
    blocks = blocks.reshape(peers, rows // peers, 1, lanes)
    blocks = lax.all_to_all(blocks, axes, split_axis=0, concat_axis=0, tiled=True)
    return blocks.reshape(rows, lanes)


def on_device(iterate, residual, direction, precond, send_list, grads, node_refs, skin, rigid_nbr):
    held, params, lanes = direction.shape
    pixels = grads.shape[1]
    owners = lax.axis_size("nodes")
    cams = lax.axis_size("cams")
    devices = owners * cams
    slot_count = send_list.shape[2]
    slots = owners * slot_count
    asked = limit(slots, pixels)
    rows = held * params
    extra = -(-slots // lanes)
    part = next(n for n in range(1, params + 1) if params % n == 0 and n * cams >= params)
    piece = held * part
    back_rows = slot_count * part
    half_pieces = -(-(params // part) // 2)
    side = (slots + slots % 2) * HALF
    sizes = (
        owners, cams, slot_count, held, params, part, half_pieces, extra, back_rows, devices // FRAMES
    )

    def array(count):
        return jax.ShapeDtypeStruct((count, lanes), f32)

    iterate, residual, direction, precond = (flat(v) for v in (iterate, residual, direction, precond))
    by_slot = jnp.transpose(send_list, (2, 0, 1))
    source = joined_rows((direction.reshape(rows, 1, lanes), by_slot))
    size = half_pieces * piece + extra
    packed = pl.pallas_call(
        functools.partial(
            pack_kernel, (rows, slot_count, piece, params // part, half_pieces), owners, cams, extra
        ),
        out_shape=array(devices * size),
        in_specs=[VMEM],
        out_specs=VMEM,
        scratch_shapes=[
            pltpu.VMEM((-(-2 * size // 8) * 8, lanes), f32),
            pltpu.VMEM((-(-extra // 8) * 8, lanes), f32),
        ],
        compiler_params=asked,
        name="pack",
    )(source.reshape(-1, lanes))
    packed, rigid_nbr, node_refs = lax.optimization_barrier((packed, rigid_nbr, node_refs))
    gathered = exchange(packed, AXES)

    joined = joined_rows(
        [v.reshape(params, held, lanes) for v in (direction, residual, precond)]
        + [jnp.transpose(rigid_nbr, (1, 0, 2))]
    ).reshape(-1, lanes)
    image_rows = -(-cams * piece // 16) * 16
    sums, choose, *pieces = pl.pallas_call(
        functools.partial(near_kernel, sizes, rows, rigid_nbr.shape[1]),
        out_shape=(array(8), jax.ShapeDtypeStruct((image_rows, devices * back_rows), bf16))
        + (array(3 * piece),) * cams,
        in_specs=[SMEM, VMEM],
        out_specs=(VMEM,) * (2 + cams),
        scratch_shapes=[pltpu.VMEM((rows, lanes), f32)],
        compiler_params=asked,
        name="near",
    )(by_slot, joined)
    spread, masked = pl.pallas_call(
        functools.partial(masks_kernel, params, node_refs.shape[0], part, half_pieces),
        out_shape=(
            jax.ShapeDtypeStruct((lanes, pixels), f32),
            jax.ShapeDtypeStruct((2 * side, pixels), bf16),
        ),
        in_specs=[VMEM],
        out_specs=(VMEM,) * 2,
        scratch_shapes=[pltpu.VMEM((4 * HALF, pixels), f32)],
        compiler_params=asked,
        name="masks",
    )(joined_rows((grads, skin, node_refs)))
    gathered, spread, sums = lax.optimization_barrier((gathered, spread, sums))
    table, frames, frame_sums = pl.pallas_call(
        functools.partial(table_kernel, sizes),
        out_shape=(array(side), array(cams * piece), array(8)),
        in_specs=[VMEM],
        out_specs=(VMEM,) * 3,
        compiler_params=asked,
        name="table",
    )(gathered)
    other = lax.ppermute(table, "cams", [(c, c ^ 1) for c in range(cams)])
    pulled = pl.pallas_call(
        own_kernel,
        out_shape=jax.ShapeDtypeStruct((lanes, pixels), f32),
        in_specs=[VMEM] * 2,
        out_specs=VMEM,
        compiler_params=asked,
        name="own_half",
    )(table, masked)
    products, squares = pl.pallas_call(
        functools.partial(data_kernel, sizes),
        out_shape=(array(devices * back_rows), array(8)),
        in_specs=[VMEM] * 4,
        out_specs=(VMEM,) * 2,
        scratch_shapes=[pltpu.VMEM((2 * side, lanes), f32)],
        compiler_params=asked,
        name="data_products",
    )(pulled, other, spread, masked)
    products, *pieces = lax.optimization_barrier((products, *pieces))
    received = exchange(products, AXES)
    mine = [pieces[0]]
    for distance in range(1, cams):
        turn = [(c, (c + distance) % cams) for c in range(cams)]
        mine.append(lax.ppermute(pieces[distance], "cams", turn))

    blocks = pl.pallas_call(
        functools.partial(image_kernel, sizes),
        out_shape=array(devices * (piece + 1)),
        in_specs=[VMEM] * (6 + cams),
        out_specs=VMEM,
        scratch_shapes=[pltpu.VMEM((cams * piece, lanes), f32)],
        compiler_params=asked,
        name="image",
    )(choose, received, frames, sums, frame_sums, squares, *mine)
    arrived = exchange(blocks, AXES)
    outs = pl.pallas_call(
        functools.partial(update_kernel, sizes),
        out_shape=(array(rows),) * 3,
        in_specs=[VMEM] * 5,
        out_specs=(VMEM,) * 3,
        compiler_params=asked,
        name="update",
    )(arrived, iterate, residual, direction, precond)
    return tuple(jnp.transpose(v.reshape(params, held, lanes), (1, 0, 2)) for v in outs)


def solution(mesh):
    split = P(AXES, None, None)
    pixel_split = P(None, AXES)
    in_specs = (split,) * 4 + (P("nodes", None, None),) + (pixel_split,) * 3 + (split,)
    return jax.shard_map(
        on_device, mesh=mesh, in_specs=in_specs, out_specs=(split,) * 3, check_vma=False
    )
```

```python
import functools

import jax
import jax.numpy as jnp
from jax import lax
from jax.experimental import pallas as pl
from jax.experimental.pallas import tpu as pltpu
from jax.sharding import PartitionSpec as P

FRAMES = 8
AXES = ("nodes", "cams")
temporal_weight = 0.5
rigid_weight = 0.1
NN = (((1,), (0,)), ((), ()))
NT = (((1,), (1,)), ((), ()))
LANES = 128
HALF = 8
f32 = jnp.float32
bf16 = jnp.bfloat16

VMEM = pl.BlockSpec(memory_space=pltpu.VMEM)
SMEM = pl.BlockSpec(memory_space=pltpu.SMEM)


def limit(slots, pixels):
    need = 8 * 2**20 + slots * 2 * HALF * pixels * 3
    return pltpu.CompilerParams(vmem_limit_bytes=min(need, 56 * 2**20))


def halves(value):
    high = value.astype(bf16)
    low = (value - high.astype(f32)).astype(bf16)
    return high, low


def rows_sum(value):
    return jnp.sum(value, axis=0, keepdims=True)


def loop(count, body):
    lax.fori_loop(0, count, lambda i, carry: (body(i), carry)[1], 0, unroll=count <= 32)


def pack_kernel(sizes, owners, cams, extra, source, out, halves_of, lists):
    rows, slot_count, piece, pieces, half_pieces = sizes
    half_rows = half_pieces * piece
    lists[...] = jnp.zeros_like(lists)
    for s in range(slot_count):
        row, lane = divmod(s * owners, LANES)
        moved = source[rows + s : rows + s + 1, :]
        if lane:
            moved = pltpu.roll(moved, lane, 1)
        lists[row : row + 1, :] = lists[row : row + 1, :] + moved
    size = half_rows + extra
    halves_of[...] = jnp.zeros_like(halves_of)
    for c in range(pieces):
        at = (c % 2) * size + (c // 2) * piece
        halves_of[at : at + piece, :] = source[c * piece : (c + 1) * piece, :]
    for parity in range(2):
        at = parity * size + half_rows
        halves_of[at : at + extra, :] = lists[0:extra, :]

    def write(owner):
        for c in range(cams):
            at = (c % 2) * size
            out[pl.ds((owner * cams + c) * size, size), :] = halves_of[at : at + size, :]

    loop(owners, write)


def near_kernel(sizes, rows, edges, send_list, joined, sums_out, choose, *pieces):
    owners, cams, slot_count, held, params, part, half_pieces, extra, back_rows, step = sizes
    piece = held * part
    *pieces, near_rows = pieces
    value = joined[0:rows, :]
    left = joined[rows : 2 * rows, :]
    scale = joined[2 * rows : 3 * rows, :]
    high, low = halves(value)
    stack = jnp.concatenate([high.astype(f32), low.astype(f32), jnp.ones((16, LANES), f32)], axis=0)
    stack = stack.astype(bf16)
    node_rows = lax.broadcasted_iota(jnp.int32, (LANES, LANES), 0).astype(f32)
    patch_row = lax.broadcasted_iota(jnp.int32, (rows, LANES), 0) % held
    rigid = jnp.zeros_like(value)
    for q in range(held):
        hits = jnp.zeros((LANES, LANES), f32)
        for r in range(edges):
            at = 3 * rows + r * held + q
            hits = hits + jnp.where(node_rows == joined[at : at + 1, :], 1.0, 0.0)
        hits = hits.astype(bf16)
        pulled = lax.dot_general(stack, hits, NN, preferred_element_type=f32)
        pushed = lax.dot_general(stack, hits, NT, preferred_element_type=f32)
        degree = pushed[2 * rows : 2 * rows + 1]
        both = pulled + pushed
        edge_sum = value * (degree + float(edges)) - (both[:rows] + both[rows : 2 * rows])
        rigid = jnp.where(patch_row == q, edge_sum, rigid)
    near = rigid_weight * rigid + (2.0 * temporal_weight) * value
    near_rows[...] = near
    cam = lax.axis_index("cams")
    for distance, out in enumerate(pieces):
        target = lax.rem(cam + distance, cams) * piece
        offset = jnp.minimum(target, rows - piece)
        out[0:piece, :] = joined[pl.ds(rows + offset, piece), :]
        out[piece : 2 * piece, :] = joined[pl.ds(2 * rows + offset, piece), :]
        out[2 * piece : 3 * piece, :] = near_rows[pl.ds(offset, piece), :]
        if cams * piece > rows:

            @pl.when(target >= rows)
            def _():
                out[...] = jnp.zeros_like(out)

    sums_out[0:1, :] = rows_sum(left * (scale * left))
    sums_out[1:2, :] = rows_sum(value * near)

    column = lax.broadcasted_iota(jnp.int32, (1, choose.shape[1]), 1)
    row = column % back_rows
    slot = column // (back_rows * cams) * slot_count + row // part
    listed = jnp.zeros_like(column)
    for owner in range(owners):
        for s in range(slot_count):
            patch = jnp.maximum(send_list[s, 0, owner], 0)
            listed = jnp.where(slot == owner * slot_count + s, patch, listed)
    target = listed // held * piece + row % part * held + listed % held
    image_row = lax.broadcasted_iota(jnp.int32, choose.shape, 0)
    choose[...] = jnp.where(image_row == target, 1.0, 0.0).astype(bf16)


def masks_kernel(params, refs_count, part, half_pieces, pixel_rows, spread_out, masked, grads_pad):
    pixels = pixel_rows.shape[1]
    side = masked.shape[0] // 2
    chunk = 512
    grads_pad[...] = jnp.zeros_like(grads_pad)
    for c in range(params // part):
        for copy in range(2):
            at = (2 * (c % 2) + copy) * HALF + (c // 2) * part
            grads_pad[at : at + part, :] = pixel_rows[c * part : (c + 1) * part, :]
    node_rows = lax.broadcasted_iota(jnp.int32, (LANES, chunk), 0)
    upper = lax.broadcasted_iota(jnp.int32, (2 * HALF, chunk), 0) // HALF
    for at in range(0, pixels, chunk):
        cols = slice(at, at + chunk)
        weights = pixel_rows[params : params + refs_count, cols]
        refs = pixel_rows[params + refs_count : params + 2 * refs_count, cols].astype(jnp.int32)
        node = lax.bitwise_and(refs, LANES - 1)
        slot_of = lax.shift_right_logical(refs[0:1], 7) - upper
        even, odd = grads_pad[0 : 2 * HALF, cols], grads_pad[2 * HALF :, cols]
        spread = jnp.where(node_rows == node[0:1], weights[0:1], 0.0)
        for k in range(1, refs.shape[0]):
            spread = spread + jnp.where(node_rows == node[k : k + 1], weights[k : k + 1], 0.0)
        spread_out[:, cols] = spread

        def mask(pair):
            here = slot_of == 2 * pair
            rows = pl.multiple_of(2 * HALF * pair, 2 * HALF)
            masked[pl.ds(rows, 2 * HALF), cols] = jnp.where(here, even, 0.0).astype(bf16)
            rows = pl.multiple_of(side + 2 * HALF * pair, 2 * HALF)
            masked[pl.ds(rows, 2 * HALF), cols] = jnp.where(here, odd, 0.0).astype(bf16)

        loop(side // (2 * HALF), mask)


def table_kernel(sizes, gathered, table_out, frames_out, sums_out):
    owners, cams, slot_count, held, params, part, half_pieces, extra, back_rows, step = sizes
    devices = owners * cams
    piece = held * part
    half = half_pieces * part
    block_rows = half * held + extra
    receiver = lax.axis_index("nodes")
    cam = lax.axis_index("cams")
    curvature = jnp.zeros((1, LANES), f32)
    inside = cam * part < params
    offset = jnp.minimum(cam // 2, half_pieces - 1) * piece
    for c in range(cams):
        device = receiver * cams + c
        value = gathered[pl.ds(device * block_rows + offset, piece), :]
        before = gathered[pl.ds(jnp.maximum(device - step, 0) * block_rows + offset, piece), :]
        after = gathered[
            pl.ds(jnp.minimum(device + step, devices - 1) * block_rows + offset, piece), :
        ]
        earlier = jnp.where(jnp.logical_and(inside, device >= step), before, 0.0)
        following = jnp.where(jnp.logical_and(inside, device + step < devices), after, 0.0)
        frames = -temporal_weight * (earlier + following)
        frames_out[c * piece : (c + 1) * piece, :] = frames
        curvature = curvature + rows_sum(value * frames)
    sums_out[0:1, :] = curvature

    owner_rows = cams * block_rows
    table_row = lax.broadcasted_iota(jnp.int32, (slot_count * HALF, 1), 0)
    within = table_row % HALF
    lane_of = lax.broadcasted_iota(jnp.int32, (slot_count * HALF, LANES), 1)
    entry = table_row // HALF * owners + receiver
    column = lax.broadcasted_iota(jnp.int32, (slot_count * HALF, owner_rows), 1)
    list_row = [lane_of + line * LANES == entry for line in range(extra)]

    def fetch(owner):
        at = owner * owner_rows
        listed = jnp.zeros((slot_count * HALF, LANES), f32)
        for line in range(extra):
            row = gathered[pl.ds(at + half * held + line, 1), :]
            listed = listed + jnp.where(list_row[line], row, 0.0)
        listed = jnp.maximum(jnp.sum(listed, axis=1, keepdims=True), 0.0).astype(jnp.int32)
        source = listed // held * block_rows + listed % held + within * held
        source = jnp.where(within < half, source, -1)
        choose = jnp.where(column == source, 1.0, 0.0).astype(bf16)
        high, low = halves(gathered[pl.ds(at, owner_rows), :])
        picked = lax.dot_general(choose, high, NN, preferred_element_type=f32)
        picked = picked + lax.dot_general(choose, low, NN, preferred_element_type=f32)
        rows = pl.multiple_of(owner * slot_count * HALF, HALF)
        table_out[pl.ds(rows, slot_count * HALF), :] = picked

    filled = owners * slot_count * HALF
    if table_out.shape[0] > filled:
        table_out[filled:, :] = jnp.zeros((table_out.shape[0] - filled, LANES), f32)
    loop(owners, fetch)


def pull(table, masked, parity, cols):
    side = masked.shape[0] // 2
    live = masked[pl.ds(pl.multiple_of(parity * side, 2 * HALF), side), cols]
    pulled = lax.dot_general(table, live, NN, preferred_element_type=f32)
    return pulled[:LANES] + pulled[LANES:]


def turned_halves(table):
    return jnp.concatenate(halves(table[...].T), axis=0)


def own_kernel(table, masked, pulled_out):
    parity = lax.rem(lax.axis_index("cams"), 2)
    turned_table = turned_halves(table)
    chunk = min(2048, masked.shape[1])
    for at in range(0, masked.shape[1], chunk):
        cols = slice(at, at + chunk)
        pulled_out[:, cols] = pull(turned_table, masked, parity, cols)


def data_kernel(sizes, pulled_own, table, spread, masked, out, squares_out, products):
    owners, cams, slot_count, held, params, part, half_pieces, extra, back_rows, step = sizes
    side = masked.shape[0] // 2
    parity = 1 - lax.rem(lax.axis_index("cams"), 2)
    turned_table = turned_halves(table)
    squares = jnp.zeros((1, LANES), f32)
    chunk = min(2048, masked.shape[1])
    for at in range(0, spread.shape[1], chunk):
        cols = slice(at, at + chunk)
        weights = spread[:, cols]
        pulled = pulled_own[:, cols] + pull(turned_table, masked, parity, cols)
        projected = rows_sum(weights * pulled)
        squared = projected * projected
        for lane in range(0, chunk, LANES):
            squares = squares + squared[:, lane : lane + LANES]
        both = jnp.concatenate(halves(weights * projected), axis=0)
        back = lax.dot_general(masked[:, cols], both, NT, preferred_element_type=f32)
        back = back[:, :LANES] + back[:, LANES:]
        if at == 0:
            products[...] = back
        else:
            products[...] += back

    squares_out[0:1, :] = squares

    def give(owner):
        for c in range(cams):
            base = (owner * cams + c) * back_rows
            for s in range(slot_count):
                if c * part < params:
                    at = (c % 2) * side + (owner * slot_count + s) * HALF + (c // 2) * part
                    value = products[pl.ds(at, part), :]
                else:
                    value = jnp.zeros((part, LANES), f32)
                out[pl.ds(base + s * part, part), :] = value

    loop(owners, give)


def image_kernel(sizes, choose, received, frames, near_sums, frame_sums, squares, *refs):
    owners, cams, slot_count, held, params, part, half_pieces, extra, back_rows, step = sizes
    mine, (blocks, image) = refs[:cams], refs[cams:]
    cam = lax.axis_index("cams")
    piece = held * part
    value = received[...]
    high, rest = halves(value)
    low = (value - high.astype(f32) - rest.astype(f32)).astype(bf16)
    total = sum(
        lax.dot_general(choose[...], term, NN, preferred_element_type=f32)
        for term in (high, rest, low)
    )
    image[...] = total[0 : cams * piece] + frames[...]
    cross = jnp.zeros((1, LANES), f32)
    square = jnp.zeros((1, LANES), f32)
    for distance, block in enumerate(mine):
        rows = pl.ds(lax.rem(cam + cams - distance, cams) * piece, piece)
        residual, precond, near = (block[k * piece : (k + 1) * piece, :] for k in range(3))
        value = image[rows, :] + near
        image[rows, :] = value
        cross = cross + rows_sum(value * (precond * residual))
        square = square + rows_sum(value * (precond * value))
    curvature = near_sums[1:2, :] + frame_sums[0:1, :] + squares[0:1, :]
    lane_of = lax.broadcasted_iota(jnp.int32, (1, LANES), 1)
    scalars = jnp.zeros((1, LANES), f32)
    for k, row in enumerate((near_sums[0:1, :], curvature, cross, square)):
        scalars = jnp.where(lane_of == k, jnp.sum(row, axis=1, keepdims=True), scalars)

    def tell(owner):
        for c in range(cams):
            base = (owner * cams + c) * (piece + 1)
            blocks[pl.ds(base, 1), :] = scalars
            blocks[pl.ds(base + 1, piece), :] = image[c * piece : (c + 1) * piece, :]

    loop(owners, tell)


def update_kernel(
    sizes, arrived, iterate, residual, direction, precond,
    new_iterate, new_residual, new_direction,
):
    owners, cams, slot_count, held, params, part, half_pieces, extra, back_rows, step = sizes
    piece = held * part
    rows = iterate.shape[0]
    own = lax.axis_index("nodes")
    scalars = arrived[0:1, :]
    for device in range(1, owners * cams):
        scalars = scalars + arrived[device * (piece + 1) : device * (piece + 1) + 1, :]
    lane_of = lax.broadcasted_iota(jnp.int32, (1, LANES), 1)
    start, curvature, cross, square = (
        jnp.sum(jnp.where(lane_of == k, scalars, 0.0), axis=1, keepdims=True) for k in range(4)
    )
    length = start / curvature
    norm = start - 2.0 * length * cross + length * length * square
    ratio = norm / start
    for c in range(rows // piece):
        here = slice(c * piece, (c + 1) * piece)
        image = arrived[pl.ds((own * cams + c) * (piece + 1) + 1, piece), :]
        value = direction[here, :]
        left = residual[here, :] - length * image
        new_iterate[here, :] = iterate[here, :] + length * value
        new_residual[here, :] = left
        new_direction[here, :] = precond[here, :] * left + ratio * value


def flat(value):
    return jnp.transpose(value, (1, 0, 2)).reshape(-1, value.shape[2])


def joined_rows(parts):
    count = -(-sum(part.shape[0] for part in parts) // 8) * 8
    width = max(part.shape[-1] for part in parts)
    total, at = None, 0
    for part in parts:
        sides = [(at, count - at - part.shape[0], 0)] + [(0, 0, 0)] * (part.ndim - 1)
        sides[-1] = (0, width - part.shape[-1], 0)
        value = lax.pad(part, jnp.zeros((), part.dtype), sides).astype(f32)
        total = value if total is None else total + value
        at += part.shape[0]
    return total


def exchange(blocks, axes):
    rows, lanes = blocks.shape
    peers = lax.axis_size(axes)
    blocks = blocks.reshape(peers, rows // peers, 1, lanes)
    blocks = lax.all_to_all(blocks, axes, split_axis=0, concat_axis=0, tiled=True)
    return blocks.reshape(rows, lanes)


def on_device(iterate, residual, direction, precond, send_list, grads, node_refs, skin, rigid_nbr):
    held, params, lanes = direction.shape
    pixels = grads.shape[1]
    owners = lax.axis_size("nodes")
    cams = lax.axis_size("cams")
    devices = owners * cams
    slot_count = send_list.shape[2]
    slots = owners * slot_count
    asked = limit(slots, pixels)
    rows = held * params
    extra = -(-slots // lanes)
    part = next(n for n in range(1, params + 1) if params % n == 0 and n * cams >= params)
    piece = held * part
    back_rows = slot_count * part
    half_pieces = -(-(params // part) // 2)
    side = (slots + slots % 2) * HALF
    sizes = (
        owners, cams, slot_count, held, params, part, half_pieces, extra, back_rows, devices // FRAMES
    )

    def array(count):
        return jax.ShapeDtypeStruct((count, lanes), f32)

    iterate, residual, direction, precond = (flat(v) for v in (iterate, residual, direction, precond))
    by_slot = jnp.transpose(send_list, (2, 0, 1))
    source = joined_rows((direction.reshape(rows, 1, lanes), by_slot))
    size = half_pieces * piece + extra
    packed = pl.pallas_call(
        functools.partial(
            pack_kernel, (rows, slot_count, piece, params // part, half_pieces), owners, cams, extra
        ),
        out_shape=array(devices * size),
        in_specs=[VMEM],
        out_specs=VMEM,
        scratch_shapes=[
            pltpu.VMEM((-(-2 * size // 8) * 8, lanes), f32),
            pltpu.VMEM((-(-extra // 8) * 8, lanes), f32),
        ],
        compiler_params=asked,
        name="pack",
    )(source.reshape(-1, lanes))
    packed, rigid_nbr, node_refs = lax.optimization_barrier((packed, rigid_nbr, node_refs))
    gathered = exchange(packed, AXES)

    joined = joined_rows(
        [v.reshape(params, held, lanes) for v in (direction, residual, precond)]
        + [jnp.transpose(rigid_nbr, (1, 0, 2))]
    ).reshape(-1, lanes)
    image_rows = -(-cams * piece // 16) * 16
    sums, choose, *pieces = pl.pallas_call(
        functools.partial(near_kernel, sizes, rows, rigid_nbr.shape[1]),
        out_shape=(array(8), jax.ShapeDtypeStruct((image_rows, devices * back_rows), bf16))
        + (array(3 * piece),) * cams,
        in_specs=[SMEM, VMEM],
        out_specs=(VMEM,) * (2 + cams),
        scratch_shapes=[pltpu.VMEM((rows, lanes), f32)],
        compiler_params=asked,
        name="near",
    )(by_slot, joined)
    spread, masked = pl.pallas_call(
        functools.partial(masks_kernel, params, node_refs.shape[0], part, half_pieces),
        out_shape=(
            jax.ShapeDtypeStruct((lanes, pixels), f32),
            jax.ShapeDtypeStruct((2 * side, pixels), bf16),
        ),
        in_specs=[VMEM],
        out_specs=(VMEM,) * 2,
        scratch_shapes=[pltpu.VMEM((4 * HALF, pixels), f32)],
        compiler_params=asked,
        name="masks",
    )(joined_rows((grads, skin, node_refs)))
    gathered, spread, sums = lax.optimization_barrier((gathered, spread, sums))
    table, frames, frame_sums = pl.pallas_call(
        functools.partial(table_kernel, sizes),
        out_shape=(array(side), array(cams * piece), array(8)),
        in_specs=[VMEM],
        out_specs=(VMEM,) * 3,
        compiler_params=asked,
        name="table",
    )(gathered)
    other = lax.ppermute(table, "cams", [(c, c ^ 1) for c in range(cams)])
    pulled = pl.pallas_call(
        own_kernel,
        out_shape=jax.ShapeDtypeStruct((lanes, pixels), f32),
        in_specs=[VMEM] * 2,
        out_specs=VMEM,
        compiler_params=asked,
        name="own_half",
    )(table, masked)
    products, squares = pl.pallas_call(
        functools.partial(data_kernel, sizes),
        out_shape=(array(devices * back_rows), array(8)),
        in_specs=[VMEM] * 4,
        out_specs=(VMEM,) * 2,
        scratch_shapes=[pltpu.VMEM((2 * side, lanes), f32)],
        compiler_params=asked,
        name="data_products",
    )(pulled, other, spread, masked)
    products, *pieces = lax.optimization_barrier((products, *pieces))
    received = exchange(products, AXES)
    mine = [pieces[0]]
    for distance in range(1, cams):
        turn = [(c, (c + distance) % cams) for c in range(cams)]
        mine.append(lax.ppermute(pieces[distance], "cams", turn))

    blocks = pl.pallas_call(
        functools.partial(image_kernel, sizes),
        out_shape=array(devices * (piece + 1)),
        in_specs=[VMEM] * (6 + cams),
        out_specs=VMEM,
        scratch_shapes=[pltpu.VMEM((cams * piece, lanes), f32)],
        compiler_params=asked,
        name="image",
    )(choose, received, frames, sums, frame_sums, squares, *mine)
    arrived = exchange(blocks, AXES)
    outs = pl.pallas_call(
        functools.partial(update_kernel, sizes),
        out_shape=(array(rows),) * 3,
        in_specs=[VMEM] * 5,
        out_specs=(VMEM,) * 3,
        compiler_params=asked,
        name="update",
    )(arrived, iterate, residual, direction, precond)
    return tuple(jnp.transpose(v.reshape(params, held, lanes), (1, 0, 2)) for v in outs)


def solution(mesh):
    split = P(AXES, None, None)
    pixel_split = P(None, AXES)
    in_specs = (split,) * 4 + (P("nodes", None, None),) + (pixel_split,) * 3 + (split,)
    return jax.shard_map(
        on_device, mesh=mesh, in_specs=in_specs, out_specs=(split,) * 3, check_vma=False
    )
```
